32 devices in a mesh: dp: 4 (over x, core), seq: 8 (over z, y).
Axes of the slice: x: 2, y: 2, z: 4, core: 2. Of those that a mesh axis runs over, the one named last changes fastest.
Arguments:
- tokens: bfloat16 [8, 2048, 2048], P('dp', 'seq'), may hold values from -6 to 6
- cotangent: bfloat16 [8, 2048, 2048], P('dp', 'seq'), may hold values from -6 to 6
- segments: int32 [8, 2048], P('dp'), may hold values from 0 to 3, as said below
- joint_projection_matrix: bfloat16 [2048, 2560], P(('dp', 'seq')), may hold values from -0.125 to 0.125
- output_weight_rows: bfloat16 [2048, 2048], P(('dp', 'seq')), may hold values from -1 to 1
- gate_up_weight: bfloat16 [2048, 11264], P(('dp', 'seq')), may hold values from -0.125 to 0.125
- down_weight_rows: bfloat16 [2048, 5632], P(('dp', 'seq')), may hold values from -0.078125 to 0.078125
- attn_gain: bfloat16 [2048], replicated, may hold values from 0.099609375 to 1.8984375
- ffn_gain: bfloat16 [2048], replicated, may hold values from 0.099609375 to 1.8984375
Outputs:
- output: bfloat16 [8, 2048, 2048], P('dp', 'seq')
- d_tokens: float32 [8, 2048, 2048], P('dp', 'seq')
- d_w_qkv: float32 [2048, 2560], P(('dp', 'seq'))
- d_w_out_t: float32 [2048, 2048], P(('dp', 'seq'))
- d_w_gate_up: float32 [2048, 11264], P(('dp', 'seq'))
- d_w_down_t: float32 [2048, 5632], P(('dp', 'seq'))
- d_attn_gain: float32 [2048], replicated
- d_ffn_gain: float32 [2048], replicated
The draws below stay inside these ranges and needn't reach their ends.
Inputs may be any that keep to these rules, and one draw needn't show every extreme that they name: `segments`: segment numbers start at 0 and never fall along a sequence. A sequence holds one document or 4; of the 2 sequences of each index of dp, one chosen at random is a single document.
All inputs are finite; a program needn't handle non-finite values.
Results may differ from the reference program's by a relative error of at most 0.015.
Values may be sent and summed in bfloat16 or wider, within the bound.
No kernel may reach another device: no remote copies, remote signals or barrier semaphores. Data moves between devices by JAX's collectives and lax.ppermute only.
A program may use at most 640 MiB of HBM per device.

```python
import math
import jax
import jax.numpy as jnp
from jax import lax

D = 2048
H = 32
HD = 64
KV = 4
FF = 5632
L = 2048
DOCS = 4
SEQS = 2
BATCH = 8
N_SEQ = 8


def draw_segments(key, part):
    key = jax.random.fold_in(key, 7)
    cut_key, pick_key = jax.random.split(key)
    row_keys = jax.random.split(cut_key, BATCH)
    orders = jax.vmap(lambda row_key: jax.random.permutation(row_key, L - 1))(row_keys) + 1
    cuts = orders[:, :DOCS - 1]
    column = jnp.arange(L, dtype=jnp.int32)
    starts = jnp.sum((column[None, :, None] == cuts[:, None, :]).astype(jnp.int32), axis=-1)
    segment_ids = jnp.cumsum(starts, axis=1)
    picked = jax.random.randint(pick_key, (BATCH // SEQS,), 0, SEQS)
    single = jnp.arange(BATCH, dtype=jnp.int32) % SEQS == jnp.repeat(picked, SEQS)
    return jnp.where(single[:, None], 0, segment_ids).astype(jnp.int32)


def block_scale(own_key, extent, cuts, least, high):
    def one(dim, blocks):
        draws = jax.random.uniform(jax.random.fold_in(jax.random.fold_in(own_key, 6), dim), (blocks,), jnp.float32, least / len(cuts), high / len(cuts))
        return jnp.repeat(jnp.exp(draws), extent[dim] // blocks).reshape((-1,) + (1,) * (len(extent) - dim - 1))

    level = one(*cuts[0])
    for cut in cuts[1:]:
        level = level * one(*cut)
    return level


def noise(own_key, shape, deviation, most, cuts=(), kind=jnp.bfloat16):
    factor_of = block_scale(own_key, shape, cuts, -0.22, 0.18) if cuts else 1.0
    array = jax.random.normal(own_key, shape, jnp.float32) * deviation * factor_of
    return jnp.minimum(jnp.maximum(array, -most), most).astype(kind)


def setup_inputs(seed: int = 0) -> dict:
    key_of = jax.random.split(jax.random.key(seed), 10)
    tokens = noise(key_of[0], (BATCH, L, D), 1.0, 6.0, ((0, 4), (1, 8)))
    cotangent = noise(key_of[1], (BATCH, L, D), 1.0, 6.0, ((0, 4), (1, 8)))
    segments = draw_segments(jax.random.fold_in(key_of[9], 71), 0)
    joint_projection_matrix = noise(key_of[3], (D, H * HD + 2 * KV * HD), D ** -0.5, 0.125, ((0, 32),))
    output_weight_rows = noise(key_of[4], (D, H * HD), (H * HD // 64) ** -0.5, 1.0, ((0, 32),))
    gate_up_weight = noise(key_of[5], (D, 2 * FF), D ** -0.5, 0.125, ((0, 32),))
    down_weight_rows = noise(key_of[6], (D, FF), FF ** -0.5, 0.078125, ((0, 32),))
    attn_gain = jnp.clip(1.0 + 0.18 * jax.random.normal(key_of[7], (D,), jnp.float32), 0.099609375, 1.8984375).astype(jnp.bfloat16)
    ffn_gain = jnp.clip(1.0 + 0.18 * jax.random.normal(key_of[8], (D,), jnp.float32), 0.099609375, 1.8984375).astype(jnp.bfloat16)
    return {"tokens": tokens, "cotangent": cotangent, "segments": segments, "joint_projection_matrix": joint_projection_matrix, "output_weight_rows": output_weight_rows, "gate_up_weight": gate_up_weight, "down_weight_rows": down_weight_rows, "attn_gain": attn_gain, "ffn_gain": ffn_gain}


EPSILON = 1e-05
MASKED = -1e+30
ROTARY_BASE = 10000.0

@jax.custom_vjp
def low(v):
    return lax.optimization_barrier(v.astype(jnp.bfloat16)).astype(jnp.float32)

@jax.custom_vjp
def lower_backward(v):
    return v

def low_keep(v):
    return (low(v), None)

def low_pass(kept, grad):
    return (grad,)

def back_keep(v):
    return (v, None)

def back_low(kept, grad):
    return (low(grad),)
low.defvjp(low_keep, low_pass)
lower_backward.defvjp(back_keep, back_low)

def doc_positions(segments):
    length = segments.shape[-1]
    column = jnp.arange(length, dtype=jnp.int32)
    starts_here = jnp.concatenate([jnp.ones(segments.shape[:-1] + (1,), dtype=bool), segments[..., 1:] != segments[..., :-1]], axis=-1)
    doc_start = lax.cummax(jnp.where(starts_here, column, 0).astype(jnp.int32), axis=segments.ndim - 1)
    return column - doc_start

def rotary_tables(position, head_size):
    half_size = head_size // 2
    frequency = ROTARY_BASE ** (-(jnp.arange(half_size, dtype=jnp.float32) * 2.0) / head_size)
    angles = position.astype(jnp.float32)[..., None] * frequency
    return (jnp.cos(angles), jnp.sin(angles))

def rotate(values, cosine, sine_part):
    half_size = values.shape[-1] // 2
    first_half = values[..., :half_size]
    second_half = values[..., half_size:]
    return jnp.concatenate([first_half * cosine - second_half * sine_part, second_half * cosine + first_half * sine_part], axis=-1)

def layer(hidden, joint_projection_matrix, output_weight_rows, gate_up_weight, down_weight_rows, attn_gain, ffn_gain, cosine, sine_part, segments):
    exact_matmul_mode = lax.Precision.HIGHEST
    group_size = hidden.shape[0]
    q_width = H * HD
    kv_width = KV * HD
    inverse_one = lax.rsqrt(lax.optimization_barrier(jnp.mean(hidden * hidden, axis=-1, keepdims=True)) + EPSILON)
    prenorm_activations = low(hidden * inverse_one * attn_gain)
    mapped_token_vectors = jnp.einsum('une,es->uns', prenorm_activations, joint_projection_matrix, precision=exact_matmul_mode)
    cos_heads = cosine[:, :, None, :]
    sin_heads = sine_part[:, :, None, :]
    query = mapped_token_vectors[..., :q_width].reshape(group_size, L, H, HD)
    key_part = mapped_token_vectors[..., q_width:q_width + kv_width].reshape(group_size, L, KV, HD)
    value_part = mapped_token_vectors[..., q_width + kv_width:].reshape(group_size, L, KV, HD)
    query = lower_backward(low(rotate(lower_backward(query), cos_heads, sin_heads)))
    key_part = low(rotate(lower_backward(key_part), cos_heads, sin_heads))
    value_part = low(lower_backward(value_part))
    copies = N_SEQ // KV
    per_device = H // N_SEQ
    key_part = jnp.repeat(lower_backward(jnp.repeat(key_part, copies, axis=2)), per_device, axis=2)
    value_part = jnp.repeat(lower_backward(jnp.repeat(value_part, copies, axis=2)), per_device, axis=2)
    score_scale = HD ** (-0.5)
    column = jnp.arange(L, dtype=jnp.int32)
    allowed = (segments[:, :, None] == segments[:, None, :]) & (column[None, None, :] <= column[None, :, None])

    def one_head(operands):
        q_head, k_head, v_head = operands
        scores = lower_backward(score_scale * jnp.einsum('sqd,skd->sqk', q_head, k_head, precision=exact_matmul_mode))
        scores = jnp.where(allowed, scores, MASKED)
        probabilities = jnp.exp(scores - jax.nn.logsumexp(scores, axis=-1, keepdims=True))
        return jnp.einsum('sqk,skd->sqd', low(probabilities), v_head, precision=exact_matmul_mode)
    head_results = lax.map(jax.checkpoint(one_head), (jnp.moveaxis(query, 2, 0), jnp.moveaxis(key_part, 2, 0), jnp.moveaxis(value_part, 2, 0)))
    attended_rows = lower_backward(low(jnp.moveaxis(head_results, 0, 2).reshape(group_size, L, q_width)))
    attention_output = lower_backward(jnp.einsum('xtm,pm->xtp', attended_rows, output_weight_rows, precision=exact_matmul_mode))
    middle_hidden = hidden + attention_output
    inverse_two = lax.rsqrt(lax.optimization_barrier(jnp.mean(middle_hidden * middle_hidden, axis=-1, keepdims=True)) + EPSILON)
    second_normed = low(middle_hidden * inverse_two * ffn_gain)
    gate_and_up = lower_backward(jnp.einsum('cut,tk->cuk', second_normed, gate_up_weight, precision=exact_matmul_mode))
    active_branch = low(jax.nn.silu(gate_and_up[..., :FF]) * gate_and_up[..., FF:])
    return middle_hidden + jnp.einsum('xtm,pm->xtp', active_branch, down_weight_rows, precision=exact_matmul_mode)

def reference(tokens, cotangent, segments, joint_projection_matrix, output_weight_rows, gate_up_weight, down_weight_rows, attn_gain, ffn_gain):
    weights = (joint_projection_matrix.astype(jnp.float32), output_weight_rows.astype(jnp.float32), gate_up_weight.astype(jnp.float32), down_weight_rows.astype(jnp.float32), attn_gain.astype(jnp.float32), ffn_gain.astype(jnp.float32))
    batch_size = tokens.shape[0]
    group_size = math.gcd(batch_size, max(1, 4096 // L))
    num_groups = batch_size // group_size
    position = doc_positions(segments)
    cosine, sine_part = rotary_tables(position, HD)

    def by_group(values):
        return values.reshape((num_groups, group_size) + values.shape[1:])

    def group_step(totals, inputs):
        hidden, grad_out, cos_group, sin_group, seg_group = inputs

        def forward(hidden_in, weight_qkv, weight_out, weight_gate_up, weight_down, gain_one, gain_two):
            return layer(hidden_in, weight_qkv, weight_out, weight_gate_up, weight_down, gain_one, gain_two, cos_group, sin_group, seg_group)
        result, pullback = jax.vjp(forward, hidden.astype(jnp.float32), weights[0], weights[1], weights[2], weights[3], weights[4], weights[5])
        gradients = pullback(grad_out.astype(jnp.float32))
        totals = tuple((running + update for running, update in zip(totals, gradients[1:])))
        return (totals, (result.astype(jnp.bfloat16), gradients[0]))
    initial = tuple((jnp.zeros_like(weight) for weight in weights))
    totals, (results, grad_inputs) = lax.scan(group_step, initial, (by_group(tokens), by_group(cotangent), by_group(cosine), by_group(sine_part), by_group(segments)))
    return (results.reshape(tokens.shape), grad_inputs.reshape(tokens.shape), totals[0], totals[1], totals[2], totals[3], totals[4], totals[5])
```

```python
import functools
import math

import jax
import jax.numpy as jnp
from jax import lax
from jax.experimental import pallas as pl
from jax.experimental.pallas import tpu as pltpu
from jax.sharding import Mesh
from jax.sharding import PartitionSpec as P

H = 32
HD = 64
KV = 4
FF = 5632

EPSILON = 1e-05
NEG = -1e30
ROTARY_BASE = 10000.0
LOG2E = math.log2(math.e)
LANES = 128

bf16 = jnp.bfloat16
f32 = jnp.float32


def dot(a, b, dims=((1,), (0,))):
    return lax.dot_general(a, b, (dims, ((), ())), preferred_element_type=f32)


def bits_of(size):
    return max(size - 1, 0).bit_length()


def axis_bits(axis):
    return [(axis, b) for b in reversed(range(bits_of(lax.axis_size(axis))))]


def canonical():
    return axis_bits("x") + axis_bits("core") + axis_bits("z") + axis_bits("y")


def my_bit(key):
    axis, b = key
    return (lax.axis_index(axis) >> b) & 1


def swap(values, key):
    axis, b = key
    return lax.ppermute(values, axis, [(i, i ^ (1 << b)) for i in range(lax.axis_size(axis))])


def place_of(key, have):
    order = canonical()
    return sum(order.index(k) < order.index(key) for k in have)


def gather_bits(piece, have, keys):
    have = list(have)
    for key in keys:
        other = swap(piece, key)
        low = my_bit(key) == 0
        piece = jnp.stack(
            [jnp.where(low, piece, other), jnp.where(low, other, piece)], axis=place_of(key, have)
        )
        have.append(key)
    return piece


def scatter_bits(terms, have, keys):
    have = list(have)
    for key in keys:
        at = place_of(key, [k for k in have if k != key])
        bit = my_bit(key)
        arrived = swap(lax.dynamic_index_in_dim(terms, 1 - bit, at, keepdims=False), key)
        kept = lax.dynamic_index_in_dim(terms, bit, at, keepdims=False)
        have.remove(key)
        terms = kept.astype(f32) + arrived.astype(f32)
        if have:
            terms = terms.astype(bf16)
    return terms


def sum_all(values):
    for key in canonical():
        values = values + swap(values, key)
    return values


def stack_heads(x, heads):
    return jnp.concatenate([x[:, h * HD : (h + 1) * HD] for h in range(heads)], axis=0)


def unstack_heads(x, heads):
    rows = x.shape[0] // heads
    return jnp.concatenate([x[h * rows : (h + 1) * rows] for h in range(heads)], axis=1)


def block_allowed(i, j, rows, start):
    key_pos = j * rows + lax.broadcasted_iota(jnp.int32, (rows, rows), 0)
    query_pos = i * rows + lax.broadcasted_iota(jnp.int32, (rows, rows), 1)
    return (key_pos <= query_pos) & (key_pos >= start)


def attend_kernel(
    heads, me_ref, lo_ref, hi_ref, start_ref, qkv_ref, out_ref, raw_ref, lse_ref, m_s, l_s, acc_s
):
    rows = qkv_ref.shape[1]
    qw = heads * HD
    scale = LOG2E * HD**-0.5
    me = me_ref[0]
    i = pl.program_id(0)
    q = stack_heads(qkv_ref[i ^ me, :, :qw], heads)
    m_s[...] = jnp.full_like(m_s, NEG)
    l_s[...] = jnp.zeros_like(l_s)
    acc_s[...] = jnp.zeros_like(acc_s)

    def block(j, masked):
        k = qkv_ref[j ^ me, :, qw : qw + HD]
        v = qkv_ref[j ^ me, :, qw + HD : qw + 2 * HD]
        s = dot(k, q, ((1,), (1,)))
        if masked:
            ok = block_allowed(i, j, rows, start_ref[0])
            s = jnp.where(jnp.concatenate([ok] * heads, axis=1), s, NEG)
        m_old = m_s[...]
        m_new = jnp.maximum(m_old, jnp.max(s, axis=0, keepdims=True) * scale)
        p = jnp.exp2(s * scale - m_new)
        keep = jnp.exp2(m_old - m_new)
        l_s[...] = l_s[...] * keep + jnp.sum(p, axis=0, keepdims=True)
        acc_s[...] = acc_s[...] * keep + dot(v, p.astype(bf16), ((0,), (0,)))
        m_s[...] = m_new

    def masked_step(j, carry):
        block(j, True)
        return carry

    def plain_step(j, carry):
        block(j, False)
        return carry

    block(i, True)
    lax.fori_loop(lo_ref[i], hi_ref[i], masked_step, 0)
    lax.fori_loop(hi_ref[i], i, plain_step, 0)
    total = l_s[...]
    result = unstack_heads(jnp.transpose(acc_s[...] / total), heads)
    raw_ref[0] = result
    out_ref[0] = result.astype(bf16)
    lse_ref[0] = jnp.broadcast_to(m_s[...] + jnp.log2(total), (8, heads * rows))


def attend(me, lo, hi, start, qkv, heads):
    n, rows, w = qkv.shape
    qw = heads * HD
    smem = pl.BlockSpec(memory_space=pltpu.SMEM)
    pairs = heads * (n * rows) ** 2 // 2
    per_block = lambda shape: pl.BlockSpec((1,) + shape, lambda i: (i, 0, 0))
    return pl.pallas_call(
        functools.partial(attend_kernel, heads),
        grid=(n,),
        out_shape=(
            jax.ShapeDtypeStruct((n, rows, qw), bf16),
            jax.ShapeDtypeStruct((n, rows, qw), f32),
            jax.ShapeDtypeStruct((n, 8, heads * rows), f32),
        ),
        in_specs=[
            smem,
            smem,
            smem,
            per_block((1, rows)),
            pl.BlockSpec((n, rows, w), lambda i: (0, 0, 0)),
        ],
        out_specs=(per_block((rows, qw)), per_block((rows, qw)), per_block((8, heads * rows))),
        scratch_shapes=[
            pltpu.VMEM((1, heads * rows), f32),
            pltpu.VMEM((1, heads * rows), f32),
            pltpu.VMEM((HD, heads * rows), f32),
        ],
        compiler_params=pltpu.CompilerParams(vmem_limit_bytes=48 << 20),
        cost_estimate=pl.CostEstimate(
            flops=16 * HD * pairs, bytes_accessed=8 << 20, transcendentals=pairs
        ),
        name="attend",
    )(me, lo, hi, start, qkv)


def attend_back_kernel(
    heads,
    me_ref,
    lo_ref,
    hi_ref,
    start_ref,
    qkv_ref,
    g_ref,
    raw_ref,
    lse_ref,
    dq_ref,
    dkv_ref,
    dkv_s,
    dq_s,
):
    n, rows, _ = qkv_ref.shape
    qw = heads * HD
    scale = LOG2E * HD**-0.5
    me = me_ref[0]
    i = pl.program_id(0)

    @pl.when(i == 0)
    def _():
        dkv_s[...] = jnp.zeros_like(dkv_s)

    dq_s[...] = jnp.zeros_like(dq_s)
    q = stack_heads(qkv_ref[i ^ me, :, :qw], heads)
    g_flat = g_ref[i ^ me]
    g = stack_heads(g_flat, heads)
    product = g_flat.astype(f32) * raw_ref[0]
    inner = jnp.concatenate(
        [
            jnp.sum(product[:, h * HD : (h + 1) * HD], axis=1, keepdims=True)
            for h in range(heads)
        ],
        axis=0,
    )
    inner = jnp.transpose(jnp.broadcast_to(inner, (heads * rows, LANES)))[:1]
    lse = lse_ref[0, :1]

    def block(j, masked):
        k = qkv_ref[j ^ me, :, qw : qw + HD]
        v = qkv_ref[j ^ me, :, qw + HD : qw + 2 * HD]
        s = dot(k, q, ((1,), (1,)))
        grad_probs = dot(v, g, ((1,), (1,)))
        p = jnp.exp2(s * scale - lse)
        if masked:
            ok = block_allowed(i, j, rows, start_ref[0])
            p = jnp.where(jnp.concatenate([ok] * heads, axis=1), p, 0.0)
        grad_scores = (p * (grad_probs - inner)).astype(bf16)
        dkv_s[j, :, :HD] += dot(grad_scores, q)
        dkv_s[j, :, HD:] += dot(p.astype(bf16), g)
        dq_s[...] += dot(k, grad_scores, ((0,), (0,)))

    def masked_step(j, carry):
        block(j, True)
        return carry

    def plain_step(j, carry):
        block(j, False)
        return carry

    lax.fori_loop(lo_ref[i], hi_ref[i], masked_step, 0)
    lax.fori_loop(hi_ref[i], i, plain_step, 0)
    block(i, True)
    dq = unstack_heads(jnp.transpose(dq_s[...] * HD**-0.5), heads)
    dq_ref[0] = dq.astype(bf16)

    @pl.when(i == n - 1)
    def _():
        for r in range(n):
            done = dkv_s[r]
            dkv_ref[r] = jnp.concatenate([done[:, :HD] * HD**-0.5, done[:, HD:]], axis=1).astype(
                bf16
            )


def attend_back(me, lo, hi, start, qkv, grad, raw, lse, heads):
    n, rows, w = qkv.shape
    qw = heads * HD
    smem = pl.BlockSpec(memory_space=pltpu.SMEM)
    pairs = heads * (n * rows) ** 2 // 2
    per_block = lambda shape: pl.BlockSpec((1,) + shape, lambda i: (i, 0, 0))
    whole = lambda shape: pl.BlockSpec(shape, lambda i: (0, 0, 0))
    return pl.pallas_call(
        functools.partial(attend_back_kernel, heads),
        grid=(n,),
        out_shape=(
            jax.ShapeDtypeStruct((n, rows, qw), bf16),
            jax.ShapeDtypeStruct((n, rows, 2 * HD), bf16),
        ),
        in_specs=[
            smem,
            smem,
            smem,
            per_block((1, rows)),
            whole((n, rows, w)),
            whole((n, rows, qw)),
            per_block((rows, qw)),
            per_block((8, heads * rows)),
        ],
        out_specs=(per_block((rows, qw)), whole((n, rows, 2 * HD))),
        scratch_shapes=[
            pltpu.VMEM((n, rows, 2 * HD), f32),
            pltpu.VMEM((HD, heads * rows), f32),
        ],
        compiler_params=pltpu.CompilerParams(vmem_limit_bytes=48 << 20),
        cost_estimate=pl.CostEstimate(
            flops=28 * HD * pairs, bytes_accessed=8 << 20, transcendentals=pairs
        ),
        name="attend_back",
    )(me, lo, hi, start, qkv, grad, raw, lse)


def rotate_lanes(v, cosine, signed_sine):
    parts = []
    for c in range(v.shape[1] // LANES):
        part = v[:, c * LANES : (c + 1) * LANES]
        lane = lax.broadcasted_iota(jnp.int32, part.shape, 1)
        other = jnp.where(
            lane % HD < HD // 2,
            pltpu.roll(part, LANES - HD // 2, 1),
            pltpu.roll(part, HD // 2, 1),
        )
        parts.append(part * cosine + other * signed_sine)
    return jnp.concatenate(parts, axis=1) if len(parts) > 1 else parts[0]


def pack_kernel(copies, q_ref, k_ref, v_ref, cos_ref, sin_ref, out_ref):
    qw = q_ref.shape[1]
    head = pl.program_id(1) // copies
    cosine = cos_ref[...]
    sine = sin_ref[...]
    out_ref[0, 0, :, :qw] = rotate_lanes(q_ref[...], cosine, sine).astype(bf16)
    k = rotate_lanes(k_ref[...], cosine, sine)
    v = v_ref[...]
    first = head % 2 == 0
    lane = lax.broadcasted_iota(jnp.int32, k.shape, 1)
    k = jnp.where(first, k, pltpu.roll(k, HD, 1))
    v = jnp.where(first, pltpu.roll(v, HD, 1), v)
    out_ref[0, 0, :, qw:] = jnp.where(lane < HD, k, v).astype(bf16)


def pack_heads(projected, cosine, sine, seqs, n):
    rows = projected.shape[0] // seqs
    qw = H * HD // n
    copies = n // KV
    k_at = H * HD // LANES
    v_at = k_at + KV * HD // LANES
    return pl.pallas_call(
        functools.partial(pack_kernel, copies),
        grid=(seqs, n),
        out_shape=jax.ShapeDtypeStruct((seqs, n, rows, qw + 2 * HD), bf16),
        in_specs=[
            pl.BlockSpec((rows, qw), lambda b, d: (b, d)),
            pl.BlockSpec((rows, LANES), lambda b, d: (b, k_at + d // copies // 2)),
            pl.BlockSpec((rows, LANES), lambda b, d: (b, v_at + d // copies // 2)),
            pl.BlockSpec((rows, LANES), lambda b, d: (b, 0)),
            pl.BlockSpec((rows, LANES), lambda b, d: (b, 0)),
        ],
        out_specs=pl.BlockSpec((1, 1, rows, qw + 2 * HD), lambda b, d: (b, d, 0, 0)),
        cost_estimate=pl.CostEstimate(flops=0, bytes_accessed=10 << 20, transcendentals=0),
        name="pack_heads",
    )(projected, projected, projected, cosine, sine)


def unpack_kernel(n, me_ref, in_ref, cos_ref, sin_ref, out_ref):
    qw = in_ref.shape[3] - 2 * HD
    copies = n // KV
    me = me_ref[0]
    cosine = cos_ref[...]
    sine = -sin_ref[...]
    for d in range(n):
        part = in_ref[0, d ^ me, :, :qw].astype(f32)
        out_ref[:, d * qw : (d + 1) * qw] = rotate_lanes(part, cosine, sine).astype(bf16)
    lane = lax.broadcasted_iota(jnp.int32, cosine.shape, 1)
    for pair in range(KV // 2):
        sums = []
        for head in (2 * pair, 2 * pair + 1):
            total = in_ref[0, (head * copies) ^ me, :, qw:].astype(f32)
            for c in range(1, copies):
                total = total + in_ref[0, (head * copies + c) ^ me, :, qw:].astype(f32)
            sums.append(total)
        k = jnp.where(lane < HD, sums[0], pltpu.roll(sums[1], HD, 1))
        v = jnp.where(lane < HD, pltpu.roll(sums[0], HD, 1), sums[1])
        k_at = H * HD + pair * LANES
        v_at = k_at + KV * HD
        out_ref[:, k_at : k_at + LANES] = rotate_lanes(k, cosine, sine).astype(bf16)
        out_ref[:, v_at : v_at + LANES] = v.astype(bf16)


def unpack_heads(me, pieces, cosine, sine):
    seqs, n, rows, w = pieces.shape
    cols = H * HD + 2 * KV * HD
    return pl.pallas_call(
        functools.partial(unpack_kernel, n),
        grid=(seqs,),
        out_shape=jax.ShapeDtypeStruct((seqs * rows, cols), bf16),
        in_specs=[
            pl.BlockSpec(memory_space=pltpu.SMEM),
            pl.BlockSpec((1, n, rows, w), lambda b: (b, 0, 0, 0)),
            pl.BlockSpec((rows, LANES), lambda b: (b, 0)),
            pl.BlockSpec((rows, LANES), lambda b: (b, 0)),
        ],
        out_specs=pl.BlockSpec((rows, cols), lambda b: (b, 0)),
        cost_estimate=pl.CostEstimate(flops=0, bytes_accessed=6 << 20, transcendentals=0),
        name="unpack_heads",
    )(me, pieces, cosine, sine)


def rms_scale(hidden):
    return lax.rsqrt(jnp.mean(hidden * hidden, axis=-1, keepdims=True) + EPSILON)


def rms_back(grad_scaled, scaled, inverse):
    return inverse * (grad_scaled - scaled * jnp.mean(grad_scaled * scaled, axis=-1, keepdims=True))


def to_owners(pieces, me, n):
    parts = [lax.dynamic_index_in_dim(pieces, me, 0, keepdims=False)]
    for r in range(1, n):
        piece = lax.dynamic_index_in_dim(pieces, me ^ r, 0, keepdims=False)
        parts.append(lax.ppermute(piece, ("z", "y"), [(i, i ^ r) for i in range(n)]))
    return jnp.stack(parts)


def local(
    tokens,
    cotangent,
    segments,
    joint_projection_matrix,
    output_weight_rows,
    gate_up_weight,
    down_weight_rows,
    attn_gain,
    ffn_gain,
):
    n = lax.axis_size("z") * lax.axis_size("y")
    me = lax.axis_index("z") * lax.axis_size("y") + lax.axis_index("y")
    me_arg = me.astype(jnp.int32).reshape(1)
    core = lax.axis_index("core")
    core_key = ("core", 0)
    seqs, rows, width = tokens.shape
    full_len = segments.shape[1]
    tok_rows = seqs * rows
    heads = H // n
    qw = heads * HD
    q_width = H * HD
    half = FF // 2
    xs, zs, ys = axis_bits("x"), axis_bits("z"), axis_bits("y")
    gain_one = attn_gain.astype(f32)
    gain_two = ffn_gain.astype(f32)

    column = jnp.arange(full_len, dtype=jnp.int32)
    starts_here = jnp.concatenate(
        [jnp.ones((seqs, 1), dtype=bool), segments[:, 1:] != segments[:, :-1]], axis=1
    )
    doc_start = lax.cummax(jnp.where(starts_here, column, 0), axis=1)
    position = lax.dynamic_slice_in_dim(column - doc_start, me * rows, rows, 1).reshape(tok_rows, 1)
    doc_start = doc_start.reshape(seqs, n, rows)
    first_block = doc_start[:, :, 0] // rows
    plain_from = jnp.minimum((doc_start[:, :, -1] + rows - 1) // rows, jnp.arange(n))
    plain_from = jnp.maximum(plain_from, first_block)
    doc_start = doc_start[:, :, None, :]
    frequency = ROTARY_BASE ** (-(jnp.arange(HD // 2, dtype=f32) * 2.0) / HD)
    angles = position.astype(f32) * frequency
    cosine = jnp.concatenate([jnp.cos(angles)] * 4, axis=1)
    sine = jnp.concatenate([-jnp.sin(angles), jnp.sin(angles)] * 2, axis=1)

    w_qkv = gather_bits(joint_projection_matrix, [], zs + ys + xs + [core_key])
    w_qkv = w_qkv.reshape(width, -1)
    w_out = gather_bits(output_weight_rows, [], zs + xs + ys + [core_key]).reshape(width, -1)

    def half_columns(weight, owner):
        blocks = weight.reshape(weight.shape[0], -1, 2, half)
        picked = lax.dynamic_index_in_dim(blocks, owner, 2, keepdims=False)
        return picked.reshape(weight.shape[0], -1)

    def gather_half(weight, keys):
        mine = half_columns(weight, core)
        other = swap(half_columns(weight, 1 - core), core_key)
        low = core == 0
        pair = jnp.stack([jnp.where(low, mine, other), jnp.where(low, other, mine)])
        return gather_bits(pair, [core_key], keys).reshape(width, -1)

    w_gate_up = gather_half(gate_up_weight, zs + ys + xs)
    w_down = gather_half(down_weight_rows, zs + xs + ys)

    def with_sibling(values):
        return jnp.concatenate([values, swap(values, core_key)], axis=0)

    def summed_with_sibling(partial):
        arrived = swap(partial[tok_rows:].astype(bf16), core_key)
        return partial[:tok_rows] + arrived.astype(f32)

    hidden = tokens.reshape(tok_rows, width).astype(f32)
    inverse_one = rms_scale(hidden)
    scaled_one = hidden * inverse_one
    normed_one = (scaled_one * gain_one).astype(bf16)
    packed = pack_heads(dot(normed_one, w_qkv), cosine, sine, seqs, n)
    qkv, raw, lse, returned = [], [], [], []
    for b in range(seqs):
        qkv.append(to_owners(packed[b], me, n))
        out_b, raw_b, lse_b = attend(
            me_arg, first_block[b], plain_from[b], doc_start[b], qkv[b], heads
        )
        raw.append(raw_b)
        lse.append(lse_b)
        back = to_owners(out_b, me, n)
        returned.append(
            jnp.concatenate(
                [lax.dynamic_index_in_dim(back, s ^ me, 0, keepdims=False) for s in range(n)],
                axis=1,
            )
        )
    attended = jnp.concatenate(returned, axis=0)
    middle = hidden + dot(attended, w_out, ((1,), (1,)))

    inverse_two = rms_scale(middle)
    scaled_two = middle * inverse_two
    normed_two = (scaled_two * gain_two).astype(bf16)
    normed_pair = with_sibling(normed_two)
    both = dot(normed_pair, w_gate_up)
    gate = both[:, :half]
    up = both[:, half:]
    sigmoid_gate = jax.nn.sigmoid(gate)
    silu_gate = gate * sigmoid_gate
    active = (silu_gate * up).astype(bf16)
    result = middle + summed_with_sibling(dot(active, w_down, ((1,), (1,))))
    result = result.astype(bf16).reshape(tokens.shape)

    grad_out = cotangent.reshape(tok_rows, width)
    grad_pair = with_sibling(grad_out)
    grad_active = dot(grad_pair, w_down)
    grad_gate = grad_active * up * sigmoid_gate * (1.0 + gate * (1.0 - sigmoid_gate))
    grad_up = grad_active * silu_gate
    grad_both = jnp.concatenate([grad_gate, grad_up], axis=1).astype(bf16)
    grad_normed_two = summed_with_sibling(dot(grad_both, w_gate_up, ((1,), (1,))))
    ffn_gain_grad = jnp.sum(grad_normed_two * scaled_two, axis=0)
    grad_middle = grad_out.astype(f32) + rms_back(
        grad_normed_two * gain_two, scaled_two, inverse_two
    )
    grad_branch = grad_middle.astype(bf16)

    def bit_shape(terms, keys):
        return terms.astype(bf16).reshape((2,) * len(keys) + (-1, terms.shape[1]))

    outer = lambda a, b: dot(a, b, ((0,), (0,)))

    def scatter_columns(terms, keys):
        have = canonical()
        pair = scatter_bits_open(bit_shape(terms, have), have, keys)
        mine = lax.dynamic_index_in_dim(pair, core, 0, keepdims=False)
        other = swap(lax.dynamic_index_in_dim(pair, 1 - core, 0, keepdims=False), core_key)
        low = core == 0
        blocks = pair.shape[-1] // half
        mine = mine.reshape(-1, blocks, 1, half)
        other = other.reshape(-1, blocks, 1, half)
        joined = jnp.concatenate(
            [jnp.where(low, mine, other), jnp.where(low, other, mine)], axis=2
        )
        return joined.reshape(mine.shape[0], -1)

    def scatter_bits_open(terms, have, keys):
        have = list(have)
        for step, key in enumerate(keys):
            at = place_of(key, [k for k in have if k != key])
            bit = my_bit(key)
            arrived = swap(lax.dynamic_index_in_dim(terms, 1 - bit, at, keepdims=False), key)
            kept = lax.dynamic_index_in_dim(terms, bit, at, keepdims=False)
            have.remove(key)
            terms = kept.astype(f32) + arrived.astype(f32)
            if step < len(keys) - 1:
                terms = terms.astype(bf16)
        return terms

    d_gate_up = scatter_columns(outer(normed_pair, grad_both), xs + ys + zs[::-1])
    d_down = scatter_columns(outer(grad_pair, active), ys + xs + zs[::-1])

    grad_attended = dot(grad_branch, w_out).astype(bf16)
    grad_heads = jnp.moveaxis(grad_attended.reshape(seqs, rows, n, qw), 2, 1)
    back = []
    for b in range(seqs):
        grad_b = to_owners(grad_heads[b], me, n)
        dq, dkv = attend_back(
            me_arg, first_block[b], plain_from[b], doc_start[b], qkv[b], grad_b, raw[b], lse[b], heads
        )
        back.append(to_owners(jnp.concatenate([dq, dkv], axis=2), me, n))
    grad_proj = unpack_heads(me_arg, jnp.stack(back), cosine, sine)
    grad_normed_one = dot(grad_proj, w_qkv, ((1,), (1,)))
    attn_gain_grad = jnp.sum(grad_normed_one * scaled_one, axis=0)
    grad_input = grad_middle + rms_back(grad_normed_one * gain_one, scaled_one, inverse_one)

    def scatter_rows(terms, keys):
        return scatter_bits(bit_shape(terms, canonical()), canonical(), keys)

    d_out = scatter_rows(outer(grad_branch, attended), [core_key] + xs + ys + zs[::-1])
    d_qkv = scatter_rows(outer(normed_one, grad_proj), [core_key] + ys + xs + zs[::-1])
    return (
        result,
        grad_input.reshape(tokens.shape),
        d_qkv,
        d_out,
        d_gate_up,
        d_down,
        sum_all(attn_gain_grad),
        sum_all(ffn_gain_grad),
    )


def solution(mesh):
    dp, seq = mesh.devices.shape
    fine = Mesh(mesh.devices.reshape(dp // 2, 2, seq // 2, 2), ("x", "core", "z", "y"))
    by_token = P(("x", "core"), ("z", "y"), None)
    by_row = P(("x", "core", "z", "y"), None)
    return jax.shard_map(
        local,
        mesh=fine,
        in_specs=(
            by_token,
            by_token,
            P(("x", "core"), None),
            by_row,
            by_row,
            by_row,
            by_row,
            P(),
            P(),
        ),
        out_specs=(by_token, by_token, by_row, by_row, by_row, by_row, P(), P()),
        check_vma=False,
    )
```

```python
import functools
import math

import jax
import jax.numpy as jnp
from jax import lax
from jax.experimental import pallas as pl
from jax.experimental.pallas import tpu as pltpu
from jax.sharding import Mesh
from jax.sharding import PartitionSpec as P

H = 32
HD = 64
KV = 4
FF = 5632

EPSILON = 1e-05
NEG = -1e30
ROTARY_BASE = 10000.0
LOG2E = math.log2(math.e)
LANES = 128

bf16 = jnp.bfloat16
f32 = jnp.float32


def dot(a, b, dims=((1,), (0,))):
    return lax.dot_general(a, b, (dims, ((), ())), preferred_element_type=f32)


CORE = ("core", 0)
NEAR = ("z", 0)


def axis_bits(axis):
    return [(axis, b) for b in reversed(range((lax.axis_size(axis) - 1).bit_length()))]


def my_bit(key):
    axis, b = key
    return (lax.axis_index(axis) >> b) & 1


def swap(values, key):
    axis, b = key
    return lax.ppermute(values, axis, [(i, i ^ (1 << b)) for i in range(lax.axis_size(axis))])


class Flow:
    def __init__(self):
        self.token = jnp.zeros((), f32)

    def open(self, *values):
        opened = lax.optimization_barrier(values + (self.token,))[:-1]
        return opened if len(values) > 1 else opened[0]

    def close(self, *values):
        *values, self.token = lax.optimization_barrier(values + (self.token,))
        return values if len(values) > 1 else values[0]


def pair_rows(values, key):
    other = swap(values, key)
    low = my_bit(key) == 0
    return jnp.concatenate([jnp.where(low, values, other), jnp.where(low, other, values)], axis=0)


def choose(values, key, axis):
    bit = my_bit(key)
    return (
        lax.dynamic_index_in_dim(values, bit, axis, keepdims=False),
        lax.dynamic_index_in_dim(values, 1 - bit, axis, keepdims=False),
    )


def by_bit(mine, other, key, axis):
    low = my_bit(key) == 0
    return jnp.stack([jnp.where(low, mine, other), jnp.where(low, other, mine)], axis=axis)


def chunk_keys():
    return axis_bits("x") + axis_bits("y") + axis_bits("z")[:-1]


def mask_of(key):
    keys = chunk_keys()
    return 1 << (len(keys) - 1 - keys.index(key))


def gather_step(chunks, have, key):
    at = sum(mask_of(k) > mask_of(key) for k in have)
    return jnp.stack([chunks, swap(chunks, key)], axis=at), have + [key]


def gather_steps(chunks, have, keys):
    for key in keys:
        chunks, have = gather_step(chunks, have, key)
    return chunks, have


def scatter_step(terms, have, key):
    at = sum(mask_of(k) > mask_of(key) for k in have)
    mine = lax.index_in_dim(terms, 0, at, keepdims=False)
    arrived = swap(lax.index_in_dim(terms, 1, at, keepdims=False), key)
    have = [k for k in have if k != key]
    total = mine.astype(f32) + arrived.astype(f32)
    return (total.astype(bf16) if have else total), have


def scatter_steps(terms, have, keys):
    for key in keys:
        terms, have = scatter_step(terms, have, key)
    return terms, have


def sum_all(values):
    for axis in ("core", "x", "y", "z"):
        for key in axis_bits(axis):
            values = values + swap(values, key)
    return values


def stack_heads(x, heads):
    return jnp.concatenate([x[:, h * HD : (h + 1) * HD] for h in range(heads)], axis=0)


def unstack_heads(x, heads):
    rows = x.shape[0] // heads
    return jnp.concatenate([x[h * rows : (h + 1) * rows] for h in range(heads)], axis=1)


def block_allowed(i, j, rows, start):
    key_pos = j * rows + lax.broadcasted_iota(jnp.int32, (rows, rows), 0)
    query_pos = i * rows + lax.broadcasted_iota(jnp.int32, (rows, rows), 1)
    return (key_pos <= query_pos) & (key_pos >= start)


def attend_kernel(
    heads, lo_ref, hi_ref, start_ref, qkv_ref, out_ref, raw_ref, lse_ref, m_s, l_s, acc_s
):
    rows = qkv_ref.shape[1]
    qw = heads * HD
    scale = LOG2E * HD**-0.5
    i = pl.program_id(0)
    q = stack_heads(qkv_ref[i, :, :qw], heads)
    m_s[...] = jnp.full_like(m_s, NEG)
    l_s[...] = jnp.zeros_like(l_s)
    acc_s[...] = jnp.zeros_like(acc_s)

    def block(j, masked):
        k = qkv_ref[j, :, qw : qw + HD]
        v = qkv_ref[j, :, qw + HD : qw + 2 * HD]
        s = dot(k, q, ((1,), (1,)))
        if masked:
            ok = block_allowed(i, j, rows, start_ref[0])
            s = jnp.where(jnp.concatenate([ok] * heads, axis=1), s, NEG)
        m_old = m_s[...]
        m_new = jnp.maximum(m_old, jnp.max(s, axis=0, keepdims=True) * scale)
        p = jnp.exp2(s * scale - m_new)
        keep = jnp.exp2(m_old - m_new)
        l_s[...] = l_s[...] * keep + jnp.sum(p, axis=0, keepdims=True)
        acc_s[...] = acc_s[...] * keep + dot(v, p.astype(bf16), ((0,), (0,)))
        m_s[...] = m_new

    def masked_step(j, carry):
        block(j, True)
        return carry

    def plain_step(j, carry):
        block(j, False)
        return carry

    block(i, True)
    lax.fori_loop(lo_ref[i], hi_ref[i], masked_step, 0)
    lax.fori_loop(hi_ref[i], i, plain_step, 0)
    total = l_s[...]
    result = unstack_heads(jnp.transpose(acc_s[...] / total), heads)
    raw_ref[0] = result
    out_ref[0] = result.astype(bf16)
    lse_ref[0] = jnp.broadcast_to(m_s[...] + jnp.log2(total), (8, heads * rows))


def attend(lo, hi, start, qkv, heads):
    n, rows, w = qkv.shape
    qw = heads * HD
    smem = pl.BlockSpec(memory_space=pltpu.SMEM)
    pairs = heads * (n * rows) ** 2 // 2
    per_block = lambda shape: pl.BlockSpec((1,) + shape, lambda i: (i, 0, 0))
    return pl.pallas_call(
        functools.partial(attend_kernel, heads),
        grid=(n,),
        out_shape=(
            jax.ShapeDtypeStruct((n, rows, qw), bf16),
            jax.ShapeDtypeStruct((n, rows, qw), f32),
            jax.ShapeDtypeStruct((n, 8, heads * rows), f32),
        ),
        in_specs=[
            smem,
            smem,
            per_block((1, rows)),
            pl.BlockSpec((n, rows, w), lambda i: (0, 0, 0)),
        ],
        out_specs=(per_block((rows, qw)), per_block((rows, qw)), per_block((8, heads * rows))),
        scratch_shapes=[
            pltpu.VMEM((1, heads * rows), f32),
            pltpu.VMEM((1, heads * rows), f32),
            pltpu.VMEM((HD, heads * rows), f32),
        ],
        compiler_params=pltpu.CompilerParams(vmem_limit_bytes=48 << 20),
        cost_estimate=pl.CostEstimate(
            flops=16 * HD * pairs, bytes_accessed=8 << 20, transcendentals=pairs
        ),
        name="attend",
    )(lo, hi, start, qkv)


def attend_back_kernel(
    heads,
    lo_ref,
    hi_ref,
    start_ref,
    qkv_ref,
    g_ref,
    raw_ref,
    lse_ref,
    dq_ref,
    dkv_ref,
    dkv_s,
    dq_s,
):
    n, rows, _ = qkv_ref.shape
    qw = heads * HD
    scale = LOG2E * HD**-0.5
    i = pl.program_id(0)

    @pl.when(i == 0)
    def _():
        dkv_s[...] = jnp.zeros_like(dkv_s)

    dq_s[...] = jnp.zeros_like(dq_s)
    q = stack_heads(qkv_ref[i, :, :qw], heads)
    g_flat = g_ref[i]
    g = stack_heads(g_flat, heads)
    product = g_flat.astype(f32) * raw_ref[0]
    inner = jnp.concatenate(
        [
            jnp.sum(product[:, h * HD : (h + 1) * HD], axis=1, keepdims=True)
            for h in range(heads)
        ],
        axis=0,
    )
    inner = jnp.transpose(jnp.broadcast_to(inner, (heads * rows, LANES)))[:1]
    lse = lse_ref[0, :1]

    def block(j, masked):
        k = qkv_ref[j, :, qw : qw + HD]
        v = qkv_ref[j, :, qw + HD : qw + 2 * HD]
        s = dot(k, q, ((1,), (1,)))
        grad_probs = dot(v, g, ((1,), (1,)))
        p = jnp.exp2(s * scale - lse)
        if masked:
            ok = block_allowed(i, j, rows, start_ref[0])
            p = jnp.where(jnp.concatenate([ok] * heads, axis=1), p, 0.0)
        grad_scores = (p * (grad_probs - inner)).astype(bf16)
        dkv_s[j, :, :HD] += dot(grad_scores, q)
        dkv_s[j, :, HD:] += dot(p.astype(bf16), g)
        dq_s[...] += dot(k, grad_scores, ((0,), (0,)))

    def masked_step(j, carry):
        block(j, True)
        return carry

    def plain_step(j, carry):
        block(j, False)
        return carry

    lax.fori_loop(lo_ref[i], hi_ref[i], masked_step, 0)
    lax.fori_loop(hi_ref[i], i, plain_step, 0)
    block(i, True)
    dq = unstack_heads(jnp.transpose(dq_s[...] * HD**-0.5), heads)
    dq_ref[0] = dq.astype(bf16)

    @pl.when(i == n - 1)
    def _():
        for r in range(n):
            done = dkv_s[r]
            dkv_ref[r] = jnp.concatenate([done[:, :HD] * HD**-0.5, done[:, HD:]], axis=1).astype(
                bf16
            )


def attend_back(lo, hi, start, qkv, grad, raw, lse, heads):
    n, rows, w = qkv.shape
    qw = heads * HD
    smem = pl.BlockSpec(memory_space=pltpu.SMEM)
    pairs = heads * (n * rows) ** 2 // 2
    per_block = lambda shape: pl.BlockSpec((1,) + shape, lambda i: (i, 0, 0))
    whole = lambda shape: pl.BlockSpec(shape, lambda i: (0, 0, 0))
    return pl.pallas_call(
        functools.partial(attend_back_kernel, heads),
        grid=(n,),
        out_shape=(
            jax.ShapeDtypeStruct((n, rows, qw), bf16),
            jax.ShapeDtypeStruct((n, rows, 2 * HD), bf16),
        ),
        in_specs=[
            smem,
            smem,
            per_block((1, rows)),
            whole((n, rows, w)),
            whole((n, rows, qw)),
            per_block((rows, qw)),
            per_block((8, heads * rows)),
        ],
        out_specs=(per_block((rows, qw)), whole((n, rows, 2 * HD))),
        scratch_shapes=[
            pltpu.VMEM((n, rows, 2 * HD), f32),
            pltpu.VMEM((HD, heads * rows), f32),
        ],
        compiler_params=pltpu.CompilerParams(vmem_limit_bytes=48 << 20),
        cost_estimate=pl.CostEstimate(
            flops=28 * HD * pairs, bytes_accessed=8 << 20, transcendentals=pairs
        ),
        name="attend_back",
    )(lo, hi, start, qkv, grad, raw, lse)


def rotate_lanes(v, cosine, signed_sine):
    parts = []
    for c in range(v.shape[1] // LANES):
        part = v[:, c * LANES : (c + 1) * LANES]
        lane = lax.broadcasted_iota(jnp.int32, part.shape, 1)
        other = jnp.where(
            lane % HD < HD // 2,
            pltpu.roll(part, LANES - HD // 2, 1),
            pltpu.roll(part, HD // 2, 1),
        )
        parts.append(part * cosine + other * signed_sine)
    return jnp.concatenate(parts, axis=1) if len(parts) > 1 else parts[0]


def pack_kernel(copies, core_ref, q_own, q_other, k_own, k_other, v_own, v_other, cos_ref, sin_ref, out_ref):
    qw = q_own.shape[1]
    n = pl.num_programs(1)
    d = pl.program_id(1)
    here = d // (n // 2) == core_ref[0]
    cosine = cos_ref[...]
    sine = sin_ref[...]
    q = jnp.where(here, q_own[...], q_other[...])
    out_ref[0, 0, :, :qw] = rotate_lanes(q, cosine, sine).astype(bf16)
    k = rotate_lanes(jnp.where(here, k_own[...], k_other[...]), cosine, sine)
    v = jnp.where(here, v_own[...], v_other[...])
    first = (d // copies) % 2 == 0
    lane = lax.broadcasted_iota(jnp.int32, k.shape, 1)
    k = jnp.where(first, k, pltpu.roll(k, HD, 1))
    v = jnp.where(first, pltpu.roll(v, HD, 1), v)
    out_ref[0, 0, :, qw:] = jnp.where(lane < HD, k, v).astype(bf16)


def pack_heads(core, projected, cosine, sine, seqs, n):
    own, other = projected
    rows = own.shape[0] // seqs
    qw = H * HD // n
    kv_at = H * HD // 2 // LANES
    q_spec = pl.BlockSpec((rows, qw), lambda b, d: (b, d % (n // 2)))
    k_spec = pl.BlockSpec((rows, LANES), lambda b, d: (b, kv_at))
    v_spec = pl.BlockSpec((rows, LANES), lambda b, d: (b, kv_at + 1))
    table = pl.BlockSpec((rows, LANES), lambda b, d: (b, 0))
    return [
        pl.pallas_call(
            functools.partial(pack_kernel, n // KV),
            grid=(1, n),
            in_specs=[pl.BlockSpec(memory_space=pltpu.SMEM)]
            + [
                pl.BlockSpec(spec.block_shape, lambda _, d, spec=spec, seq=seq: spec.index_map(seq, d))
                for spec in (q_spec, q_spec, k_spec, k_spec, v_spec, v_spec, table, table)
            ],
            out_specs=pl.BlockSpec((1, 1, rows, qw + 2 * HD), lambda b, d: (b, d, 0, 0)),
            out_shape=jax.ShapeDtypeStruct((1, n, rows, qw + 2 * HD), bf16),
            cost_estimate=pl.CostEstimate(flops=0, bytes_accessed=6 << 20, transcendentals=0),
            name="pack_heads",
        )(core, own, other, own, other, own, other, cosine, sine)[0]
        for seq in range(seqs)
    ]


def unpack_kernel(n, core_ref, in_ref, cos_ref, sin_ref, out_ref):
    qw = in_ref.shape[2] - 2 * HD
    copies = n // KV
    own = core_ref[0] * (n // 2)
    cosine = cos_ref[...]
    sine = -sin_ref[...]
    lane = lax.broadcasted_iota(jnp.int32, cosine.shape, 1)
    half_cols = out_ref.shape[1] // 2
    for half in range(2):
        at = half * half_cols
        first = half * (n // 2)
        for d in range(n // 2):
            part = in_ref[(first + d) ^ own, :, :qw].astype(f32)
            rotated = rotate_lanes(part, cosine, sine).astype(bf16)
            out_ref[:, at + d * qw : at + (d + 1) * qw] = rotated
        sums = []
        for head in range(2):
            total = None
            for c in range(copies):
                slot = in_ref[(first + head * copies + c) ^ own, :, qw:].astype(f32)
                total = slot if total is None else total + slot
            sums.append(total)
        k = jnp.where(lane < HD, sums[0], pltpu.roll(sums[1], HD, 1))
        v = jnp.where(lane < HD, pltpu.roll(sums[0], HD, 1), sums[1])
        k_at = at + H * HD // 2
        out_ref[:, k_at : k_at + LANES] = rotate_lanes(k, cosine, sine).astype(bf16)
        out_ref[:, k_at + LANES : k_at + 2 * LANES] = v.astype(bf16)


def unpack_heads(core, pieces, cosine, sine):
    n, rows, w = pieces.shape
    cols = H * HD + 2 * KV * HD
    return pl.pallas_call(
        functools.partial(unpack_kernel, n),
        out_shape=jax.ShapeDtypeStruct((rows, cols), bf16),
        in_specs=[pl.BlockSpec(memory_space=pltpu.SMEM)]
        + [pl.BlockSpec(memory_space=pltpu.VMEM)] * 3,
        out_specs=pl.BlockSpec(memory_space=pltpu.VMEM),
        compiler_params=pltpu.CompilerParams(vmem_limit_bytes=32 << 20),
        cost_estimate=pl.CostEstimate(flops=0, bytes_accessed=4 << 20, transcendentals=0),
        name="unpack_heads",
    )(core, pieces, cosine, sine)


def rms_scale(hidden):
    return lax.rsqrt(jnp.mean(hidden * hidden, axis=-1, keepdims=True) + EPSILON)


def rms_back(grad_scaled, scaled, inverse):
    return inverse * (grad_scaled - scaled * jnp.mean(grad_scaled * scaled, axis=-1, keepdims=True))


def exchange(pieces):
    return lax.all_to_all(pieces, ("z", "y"), split_axis=0, concat_axis=0, tiled=True)


def pick(values, index):
    return lax.dynamic_index_in_dim(values, index, 0, keepdims=False)


def feature_order(width, sub):
    place = jnp.arange(width, dtype=jnp.int32)
    group = place // sub
    chunk = group // 4
    at = {"core": group % 2, "x": 0, "y": 0, "z": (group // 2) % 2}
    for key in chunk_keys():
        bit = ((chunk // mask_of(key)) % 2) ^ my_bit(key)
        at[key[0]] = at[key[0]] + (bit << key[1])
    source = ((at["x"] * 2 + at["core"]) * lax.axis_size("z") + at["z"]) * lax.axis_size("y")
    source = (source + at["y"]) * sub + place % sub
    return (place[:, None] == source[None, :]).astype(bf16)


def local(
    tokens,
    cotangent,
    segments,
    joint_projection_matrix,
    output_weight_rows,
    gate_up_weight,
    down_weight_rows,
    attn_gain,
    ffn_gain,
):
    n = lax.axis_size("z") * lax.axis_size("y")
    me = lax.axis_index("z") * lax.axis_size("y") + lax.axis_index("y")
    me = me.astype(jnp.int32)
    core = lax.axis_index("core").astype(jnp.int32)
    core_arg = core.reshape(1)
    seqs, rows, width = tokens.shape
    full_len = segments.shape[1]
    heads = H // n
    qw = heads * HD
    sub = joint_projection_matrix.shape[0]
    part = FF // 4
    xs, ys, zs = axis_bits("x"), axis_bits("y"), axis_bits("z")[:-1]
    chunk_bits = (2,) * len(xs + ys + zs)
    flow = Flow()

    column = jnp.arange(full_len, dtype=jnp.int32)
    starts_here = jnp.concatenate(
        [jnp.ones((seqs, 1), dtype=bool), segments[:, 1:] != segments[:, :-1]], axis=1
    )
    doc_start = lax.cummax(jnp.where(starts_here, column, 0), axis=1)
    position = lax.dynamic_slice_in_dim(column - doc_start, me * rows, rows, 1)
    doc_start = doc_start.reshape(seqs, n, rows)
    first_block = doc_start[:, :, 0] // rows
    plain_from = jnp.minimum((doc_start[:, :, -1] + rows - 1) // rows, jnp.arange(n))
    plain_from = jnp.maximum(plain_from, first_block)
    doc_start = doc_start[:, :, None, :]
    frequency = ROTARY_BASE ** (-(jnp.arange(HD // 2, dtype=f32) * 2.0) / HD)
    angles = position.astype(f32).reshape(seqs * rows, 1) * frequency
    cosine = jnp.concatenate([jnp.cos(angles)] * 4, axis=1)
    sine = jnp.concatenate([-jnp.sin(angles), jnp.sin(angles)] * 2, axis=1)

    def core_columns(weight, widths):
        mine, other, at = [], [], 0
        for w in widths:
            block = weight[:, at : at + 2 * w].reshape(sub, 2, w)
            a, b = choose(block, CORE, 1)
            mine.append(a)
            other.append(b)
            at += 2 * w
        mine = jnp.concatenate(mine, axis=1)
        arrived = swap(jnp.concatenate(other, axis=1), CORE)
        low = core == 0
        pair = [jnp.where(low, mine, arrived), jnp.where(low, arrived, mine)]
        return jnp.concatenate(pair, axis=0)

    def flat(chunks):
        return chunks.reshape(-1, chunks.shape[-1])

    def halves(chunks):
        return jnp.split(chunks, 2, axis=-1)

    qkv_widths = (H * HD // 2, KV * HD // 2, KV * HD // 2)
    qkv = flow.close(pair_rows(core_columns(joint_projection_matrix, qkv_widths), NEAR))

    qkv = flow.open(qkv)
    ffn = jnp.concatenate([gate_up_weight, down_weight_rows], axis=1).reshape(sub, 3, 2, 2, part)
    mine, other = choose(ffn, NEAR, 2)
    other = flow.open(other)
    out = pair_rows(core_columns(output_weight_rows, (H * HD // 2,)), NEAR)
    ffn = by_bit(mine, swap(other, NEAR), NEAR, 0)
    qkv, have = gather_steps(qkv, [], zs)
    order = feature_order(width, sub)
    hidden_all = dot(tokens.reshape(seqs * rows, width), order)
    gain_one = dot(attn_gain.reshape(1, width), order)
    gain_two = dot(ffn_gain.reshape(1, width), order)
    inverse_one = rms_scale(hidden_all)
    scaled_one = hidden_all * inverse_one
    normed_one = (scaled_one * gain_one).astype(bf16)
    qkv, ffn, normed_one = flow.close(qkv, ffn, normed_one)

    qkv, ffn = flow.open(qkv, ffn)
    left, right = halves(qkv)
    left, have_left = gather_steps(left, have, ys)
    right, have_right = gather_steps(right, have, xs)
    mine, other = choose(ffn, CORE, 3)
    ffn = by_bit(mine, swap(other, CORE), CORE, 1).reshape(4 * sub, 3, part)
    gate, up, down = ffn[:, 0], ffn[:, 1], ffn[:, 2]
    grad_out_all = dot(cotangent.reshape(seqs * rows, width), order)
    grad_out_low = grad_out_all.astype(bf16)
    left, right, gate, up, down, out, grad_out_low = flow.close(
        left, right, gate, up, down, out, grad_out_low
    )
    left, right, gate = flow.open(left, right, gate)
    left, _ = gather_steps(left, have_left, xs)
    right, _ = gather_steps(right, have_right, ys)
    gate, _ = gather_steps(gate, [], zs)
    w_qkv_own = jnp.concatenate([flat(left), flat(right)], axis=1)
    w_qkv_own, gate = flow.close(w_qkv_own, gate)

    w_qkv_own, gate, up, out = flow.open(w_qkv_own, gate, up, out)
    w_qkv_other = swap(w_qkv_own, CORE)
    up, _ = gather_steps(up, [], zs)
    out, _ = gather_steps(out, [], zs)
    gate, have_gate = gather_steps(gate, have, ys)
    projected = [dot(normed_one, w_qkv_own), dot(normed_one, w_qkv_other)]
    packed = pack_heads(core_arg, projected, cosine, sine, seqs, n)
    packed_0, packed_1, up, out, gate = flow.close(*packed, up, out, gate)

    def attend_one(b, qkv_b):
        return attend(first_block[b], plain_from[b], doc_start[b], qkv_b, heads)

    packed_0, up, out = flow.open(packed_0, up, out)
    out_left, out_right = halves(out)
    out_left, have_out_left = gather_steps(out_left, have, ys)
    out_right, have_out_right = gather_steps(out_right, have, xs)
    up, have_up = gather_steps(up, have, xs)
    qkv_0 = exchange(packed_0)
    qkv_0, out_left, out_right, up = flow.close(qkv_0, out_left, out_right, up)

    qkv_0, packed_1, out_left, out_right, gate, down = flow.open(
        qkv_0, packed_1, out_left, out_right, gate, down
    )
    qkv_1 = exchange(packed_1)
    out_left, _ = gather_steps(out_left, have_out_left, xs)
    out_right, _ = gather_steps(out_right, have_out_right, ys)
    gate, _ = gather_steps(gate, have_gate, xs)
    attended_0, raw_0, lse_0 = attend_one(0, qkv_0)
    w_out_own = jnp.concatenate([flat(out_left), flat(out_right)], axis=1)
    attended_0, qkv_1, w_out_own = flow.close(attended_0, qkv_1, w_out_own)

    attended_0, qkv_1, w_out_own, up = flow.open(attended_0, qkv_1, w_out_own, up)
    back_0 = exchange(attended_0)
    w_out = jnp.concatenate([w_out_own, swap(w_out_own, CORE)], axis=1)
    up, _ = gather_steps(up, have_up, ys)
    down, _ = gather_steps(down, [], zs)
    attended_1, raw_1, lse_1 = attend_one(1, qkv_1)
    attended_1, back_0, w_out, down = flow.close(attended_1, back_0, w_out, down)

    own_half = core * (n // 2)

    def after_attention(b, back):
        attended = jnp.concatenate([pick(back, s ^ own_half) for s in range(n)], axis=1)
        middle = hidden_all[b * rows : (b + 1) * rows] + dot(attended, w_out, ((1,), (1,)))
        inverse = rms_scale(middle)
        scaled = middle * inverse
        return attended, middle, inverse, scaled, (scaled * gain_two).astype(bf16)

    def tensor_group(values):
        near = swap(values, NEAR)
        return jnp.concatenate([values, swap(values, CORE), near, swap(near, CORE)], axis=0)

    def tensor_sum(partial):
        p = [partial[k * rows : (k + 1) * rows] for k in range(4)]
        near = p[2] + swap(p[3].astype(bf16), CORE).astype(f32)
        near = swap(near.astype(bf16), NEAR)
        return p[0] + swap(p[1].astype(bf16), CORE).astype(f32) + near.astype(f32)

    attended_1, back_0, down = flow.open(attended_1, back_0, down)
    back_1 = exchange(attended_1)
    attended_0, middle_0, inverse_0, scaled_0, normed_0 = after_attention(0, back_0)
    back_1, normed_0 = flow.close(back_1, normed_0)

    back_1, normed_0, down = flow.open(back_1, normed_0, down)
    group_0 = tensor_group(normed_0)
    attended_1, middle_1, inverse_1, scaled_1, normed_1 = after_attention(1, back_1)
    w_gate = flat(gate)
    group_0, normed_1, w_gate, w_up = flow.close(group_0, normed_1, w_gate, flat(up))

    def forward(group):
        gate = dot(group, w_gate)
        up = dot(group, w_up)
        sigmoid_gate = jax.nn.sigmoid(gate)
        return gate, up, (gate * sigmoid_gate * up).astype(bf16)

    def backward(grad_group, gate, up):
        sigmoid_gate = jax.nn.sigmoid(gate)
        grad_active = dot(grad_group, w_down)
        grad_gate = grad_active * up * sigmoid_gate * (1.0 + gate * (1.0 - sigmoid_gate))
        return grad_gate.astype(bf16), (grad_active * gate * sigmoid_gate).astype(bf16)

    def normed_terms(grad_gate, grad_up):
        return dot(grad_gate, w_gate, ((1,), (1,))) + dot(grad_up, w_up, ((1,), (1,)))

    group_0, normed_1, down = flow.open(group_0, normed_1, down)
    group_1 = tensor_group(normed_1)
    down, have_down = gather_steps(down, have, ys)
    gate_0, up_0, active_0 = forward(group_0)
    group_1, active_0, down = flow.close(group_1, active_0, down)

    group_1, down = flow.open(group_1, down)
    grad_low_0, grad_low_1 = flow.open(grad_out_low[:rows], grad_out_low[rows:])
    down, _ = gather_steps(down, have_down, xs)
    grad_group_0 = tensor_group(grad_low_0)
    gate_1, up_1, active_1 = forward(group_1)
    w_down = flat(down)
    w_down, active_1, grad_group_0 = flow.close(w_down, active_1, grad_group_0)

    grad_group_0 = flow.open(grad_group_0)
    grad_group_1 = tensor_group(flow.open(grad_low_1))
    grad_gate_0, grad_up_0 = backward(grad_group_0, gate_0, up_0)
    terms_0 = normed_terms(grad_gate_0, grad_up_0)
    terms_0, grad_group_1 = flow.close(terms_0, grad_group_1)

    terms_0, grad_group_1 = flow.open(terms_0, grad_group_1)
    grad_normed_0 = tensor_sum(terms_0)
    grad_gate_1, grad_up_1 = backward(grad_group_1, gate_1, up_1)
    terms_1 = normed_terms(grad_gate_1, grad_up_1)
    terms_1, grad_normed_0 = flow.close(terms_1, grad_normed_0)

    outer = lambda a, b: dot(a, b, ((0,), (0,)))

    def weight_terms(left, right):
        return outer(left, right).astype(bf16).reshape(chunk_bits + (4 * sub, part))

    def before_attention(b, g, scaled, inverse):
        grad_middle = grad_out_all[b * rows : (b + 1) * rows] + rms_back(
            g * gain_two, scaled, inverse
        )
        grad_branch = grad_middle.astype(bf16)
        grad_attended = dot(grad_branch, w_out).astype(bf16)
        grad_heads = [pick(jnp.moveaxis(grad_attended.reshape(rows, n, qw), 1, 0), s ^ own_half)
                      for s in range(n)]
        return grad_middle, grad_branch, jnp.stack(grad_heads)

    terms_1, grad_normed_0 = flow.open(terms_1, grad_normed_0)
    grad_normed_1 = tensor_sum(terms_1)
    grad_middle_0, grad_branch_0, grad_heads_0 = before_attention(
        0, grad_normed_0, scaled_0, inverse_0
    )
    grad_heads_0, grad_normed_1 = flow.close(grad_heads_0, grad_normed_1)

    grad_heads_0, grad_normed_1 = flow.open(grad_heads_0, grad_normed_1)
    grad_heads_0 = exchange(grad_heads_0)
    grad_middle_1, grad_branch_1, grad_heads_1 = before_attention(
        1, grad_normed_1, scaled_1, inverse_1
    )
    active = flow.open(jnp.concatenate([active_0, active_1], axis=0))
    grad_group = jnp.concatenate([grad_group_0, grad_group_1], axis=0)
    d_down = weight_terms(grad_group, active)
    normed_group = jnp.concatenate([group_0, group_1], axis=0)
    grad_heads_0, grad_heads_1, d_down = flow.close(grad_heads_0, grad_heads_1, d_down)

    def attend_back_one(b, qkv_b, grad_b, raw_b, lse_b):
        dq, dkv = attend_back(
            first_block[b], plain_from[b], doc_start[b], qkv_b, grad_b, raw_b, lse_b, heads
        )
        return jnp.concatenate([dq, dkv], axis=2)

    grad_heads_1, d_down = flow.open(grad_heads_1, d_down)
    grad_heads_1 = exchange(grad_heads_1)
    normed_group, grad_gate = flow.open(
        normed_group, jnp.concatenate([grad_gate_0, grad_gate_1], axis=0)
    )
    d_gate = weight_terms(normed_group, grad_gate)
    d_up = weight_terms(normed_group, jnp.concatenate([grad_up_0, grad_up_1], axis=0))
    d_down, have_d_down = scatter_steps(d_down, xs + ys + zs, ys)
    d_gate, d_up, grad_heads_1, d_down = flow.close(d_gate, d_up, grad_heads_1, d_down)

    grad_heads_0, d_gate, d_down = flow.open(grad_heads_0, d_gate, d_down)
    d_gate, have_d_gate = scatter_steps(d_gate, xs + ys + zs, xs)
    back_0 = attend_back_one(0, qkv_0, grad_heads_0, raw_0, lse_0)
    back_0, d_gate = flow.close(back_0, d_gate)

    grad_heads_1, back_0, d_up, d_down, d_gate = flow.open(grad_heads_1, back_0, d_up, d_down, d_gate)
    back_0 = exchange(back_0)
    d_up, have_d_up = scatter_steps(d_up, xs + ys + zs, ys)
    d_down, have_d_down = scatter_steps(d_down, have_d_down, xs)
    back_1 = attend_back_one(1, qkv_1, grad_heads_1, raw_1, lse_1)
    back_0, back_1, d_up, d_down = flow.close(back_0, back_1, d_up, d_down)

    back_0, back_1, d_up, d_down, d_gate, active = flow.open(
        back_0, back_1, d_up, d_down, d_gate, active
    )
    back_1 = exchange(back_1)
    d_gate, have_d_gate = scatter_steps(d_gate, have_d_gate, ys)
    d_up, have_d_up = scatter_steps(d_up, have_d_up, xs)
    d_down, _ = scatter_steps(d_down, have_d_down, zs)
    grad_proj_0 = unpack_heads(core_arg, back_0, cosine[:rows], sine[:rows])
    partial_0 = dot(active[: 4 * rows], w_down, ((1,), (1,)))
    partial_1 = dot(active[4 * rows :], w_down, ((1,), (1,)))
    back_1, grad_proj_0, d_gate, d_up, d_down, partial_0, partial_1 = flow.close(
        back_1, grad_proj_0, d_gate, d_up, d_down, partial_0, partial_1
    )

    def attention_terms(left, right):
        half = right.shape[1] // 2
        own, other = right[:, :half], right[:, half:]
        arrived = swap(outer(left, other).astype(bf16), CORE)
        total = (outer(left, own) + arrived.astype(f32)).astype(bf16)
        return total.reshape(chunk_bits + (4 * sub, half))

    def rows_back(chunk, widths):
        chunk = chunk.reshape(2, 2, sub, -1)
        mine, send = choose(chunk, NEAR, 0)
        mine = mine + swap(send.astype(bf16), NEAR).astype(f32)
        mine, send = choose(mine, CORE, 0)
        both = by_bit(mine, swap(send, CORE), CORE, 1)
        columns, at = [], 0
        for w in widths:
            columns.append(both[:, :, at : at + w].reshape(sub, 2 * w))
            at += w
        return jnp.concatenate(columns, axis=1)

    back_1, d_gate, d_up = flow.open(back_1, d_gate, d_up)
    grad_proj_1 = unpack_heads(core_arg, back_1, cosine[rows:], sine[rows:])
    grad_proj = jnp.concatenate([grad_proj_0, grad_proj_1], axis=0)
    d_qkv = attention_terms(normed_one, grad_proj)
    d_gate, _ = scatter_steps(d_gate, have_d_gate, zs)
    d_qkv, d_gate = flow.close(d_qkv, d_gate)

    d_qkv, d_up = flow.open(d_qkv, d_up)
    left, right = halves(d_qkv)
    left, have_left = scatter_steps(left, xs + ys + zs, xs)
    right, have_right = scatter_steps(right, xs + ys + zs, ys)
    d_up, _ = scatter_steps(d_up, have_d_up, zs)
    w_qkv = jnp.concatenate([w_qkv_own, w_qkv_other], axis=1)
    grad_normed_one = dot(grad_proj, w_qkv, ((1,), (1,)))
    attn_gain_grad = jnp.sum(grad_normed_one * scaled_one, axis=0)
    grad_input = jnp.concatenate([grad_middle_0, grad_middle_1], axis=0) + rms_back(
        grad_normed_one * gain_one, scaled_one, inverse_one
    )
    high = grad_input.astype(bf16)
    low = (grad_input - high.astype(f32)).astype(bf16)
    grad_input = dot(high, order, ((1,), (1,))) + dot(low, order, ((1,), (1,)))
    grad_branch = jnp.concatenate([grad_branch_0, grad_branch_1], axis=0)
    attended = jnp.concatenate([attended_0, attended_1], axis=0)
    d_out = attention_terms(grad_branch, attended)
    left, right, d_up, d_out = flow.close(left, right, d_up, d_out)

    left, right, d_out = flow.open(left, right, d_out)
    left, have_left = scatter_steps(left, have_left, ys)
    right, have_right = scatter_steps(right, have_right, xs)
    out_left, out_right = halves(d_out)
    out_left, have_out_left = scatter_steps(out_left, xs + ys + zs, xs)
    out_right, have_out_right = scatter_steps(out_right, xs + ys + zs, ys)
    middle = jnp.concatenate([tensor_sum(partial_0), tensor_sum(partial_1)], axis=0)
    result = (middle + jnp.concatenate([middle_0, middle_1], axis=0)).astype(bf16)
    result = dot(result, order, ((1,), (1,))).astype(bf16)
    left, right, out_left, out_right, result = flow.close(left, right, out_left, out_right, result)

    left, right, out_left, out_right = flow.open(left, right, out_left, out_right)
    d_qkv, _ = scatter_steps(jnp.concatenate([left, right], axis=-1), have_left, zs)
    out_left, have_out_left = scatter_steps(out_left, have_out_left, ys)
    out_right, have_out_right = scatter_steps(out_right, have_out_right, xs)
    d_qkv = rows_back(d_qkv, qkv_widths)
    d_out, _ = scatter_steps(jnp.concatenate([out_left, out_right], axis=-1), have_out_left, zs)
    d_out = rows_back(d_out, (H * HD // 2,))

    ffn = jnp.stack([d_gate, d_up, d_down], axis=1).reshape(2, 2, sub, 3, part)
    mine, send = choose(ffn, NEAR, 0)
    ffn = by_bit(mine, swap(send.astype(bf16), NEAR).astype(f32), NEAR, 3)
    mine, send = choose(ffn, CORE, 0)
    ffn = by_bit(mine, swap(send.astype(bf16), CORE).astype(f32), CORE, 3)
    ffn = ffn.reshape(sub, 3 * FF)
    ffn_gain_grad = jnp.sum(grad_normed_0 * scaled_0, axis=0) + jnp.sum(
        grad_normed_1 * scaled_1, axis=0
    )
    gains = lax.dot_general(
        jnp.stack([attn_gain_grad, ffn_gain_grad]),
        order.astype(f32),
        (((1,), (1,)), ((), ())),
        precision=lax.Precision.HIGHEST,
        preferred_element_type=f32,
    )
    gains = sum_all(gains)
    return (
        result.reshape(tokens.shape),
        grad_input.reshape(tokens.shape),
        d_qkv,
        d_out,
        ffn[:, : 2 * FF],
        ffn[:, 2 * FF :],
        gains[0],
        gains[1],
    )


def solution(mesh):
    dp, seq = mesh.devices.shape
    fine = Mesh(mesh.devices.reshape(dp // 2, 2, seq // 2, 2), ("x", "core", "z", "y"))
    by_token = P(("x", "core"), ("z", "y"), None)
    by_row = P(("x", "core", "z", "y"), None)
    return jax.shard_map(
        local,
        mesh=fine,
        in_specs=(
            by_token,
            by_token,
            P(("x", "core"), None),
            by_row,
            by_row,
            by_row,
            by_row,
            P(),
            P(),
        ),
        out_specs=(by_token, by_token, by_row, by_row, by_row, by_row, P(), P()),
        check_vma=False,
    )
```

```python
import functools
import math

import jax
import jax.numpy as jnp
from jax import lax
from jax.experimental import pallas as pl
from jax.experimental.pallas import tpu as pltpu
from jax.sharding import Mesh
from jax.sharding import PartitionSpec as P

H = 32
HD = 64
KV = 4
FF = 5632

EPSILON = 1e-05
NEG = -1e30
ROTARY_BASE = 10000.0
LOG2E = math.log2(math.e)
LANES = 128

bf16 = jnp.bfloat16
f32 = jnp.float32


def dot(a, b, dims=((1,), (0,))):
    return lax.dot_general(a, b, (dims, ((), ())), preferred_element_type=f32)


CORE = ("core", 0)
NEAR = ("near", 0)
SEQ = ("far", "near", "y")


def axis_bits(axis):
    return [(axis, b) for b in reversed(range((lax.axis_size(axis) - 1).bit_length()))]


def my_bit(key):
    axis, b = key
    return (lax.axis_index(axis) >> b) & 1


def swap(values, key):
    axis, b = key
    return lax.ppermute(values, axis, [(i, i ^ (1 << b)) for i in range(lax.axis_size(axis))])


class Flow:
    def __init__(self):
        self.token = jnp.zeros((), f32)

    def open(self, *values):
        opened = lax.optimization_barrier(values + (self.token,))[:-1]
        return opened if len(values) > 1 else opened[0]

    def close(self, *values, wait=()):
        arrived = tuple(transfer.arrived for transfer in wait)
        closed = lax.optimization_barrier(values + arrived + (self.token,))
        for transfer, value in zip(wait, closed[len(values) :]):
            transfer.arrived = value
        self.token = closed[-1]
        return closed[: len(values)] if len(values) > 1 else closed[0]


def choose(values, key, axis):
    bit = my_bit(key)
    return (
        lax.dynamic_index_in_dim(values, bit, axis, keepdims=False),
        lax.dynamic_index_in_dim(values, 1 - bit, axis, keepdims=False),
    )


def by_bit(mine, other, key, axis):
    low = my_bit(key) == 0
    return jnp.stack([jnp.where(low, mine, other), jnp.where(low, other, mine)], axis=axis)


class Swap:
    def __init__(self, values, key):
        self.arrived = swap(values, key)


class Gather:
    def __init__(self, values, axis, at):
        self.values, self.axis, self.at = values, axis, at
        self.arrived = swap(values, axis_bits(axis)[0])

    def done(self):
        values, other, shape = self.values, self.arrived, self.values.shape
        for step, key in enumerate(axis_bits(self.axis)):
            if step:
                other = swap(values, key)
            values = by_bit(values, other, key, self.at + step)
        return values.reshape(shape[: self.at] + (lax.axis_size(self.axis),) + shape[self.at :])


class Scatter:
    def __init__(self, values, axis, at):
        self.keys, self.at = axis_bits(axis), at
        shape = values.shape
        values = values.reshape(shape[:at] + (2,) * len(self.keys) + shape[at + 1 :])
        self.start(values)

    def start(self, values):
        self.mine, send = choose(values, self.keys[0], self.at)
        self.arrived = swap(send.astype(bf16), self.keys[0])

    def done(self, last=False):
        while True:
            values = self.mine.astype(f32) + self.arrived.astype(f32)
            if not last:
                values = values.astype(bf16)
            self.keys = self.keys[1:]
            if not self.keys:
                return values
            self.start(values)


def sum_axes(values, *axes):
    for axis in axes:
        for key in axis_bits(axis):
            values = values + swap(values, key)
    return values


def stack_heads(x, heads):
    return jnp.concatenate([x[:, h * HD : (h + 1) * HD] for h in range(heads)], axis=0)


def unstack_heads(x, heads):
    rows = x.shape[0] // heads
    return jnp.concatenate([x[h * rows : (h + 1) * rows] for h in range(heads)], axis=1)


def block_allowed(i, j, rows, start):
    key_pos = j * rows + lax.broadcasted_iota(jnp.int32, (rows, rows), 0)
    query_pos = i * rows + lax.broadcasted_iota(jnp.int32, (rows, rows), 1)
    return (key_pos <= query_pos) & (key_pos >= start)


def attend_kernel(
    heads, lo_ref, hi_ref, start_ref, qkv_ref, out_ref, raw_ref, lse_ref, m_s, l_s, acc_s
):
    rows = qkv_ref.shape[1]
    qw = heads * HD
    scale = LOG2E * HD**-0.5
    i = pl.program_id(0)
    q = stack_heads(qkv_ref[i, :, :qw], heads)
    m_s[...] = jnp.full_like(m_s, NEG)
    l_s[...] = jnp.zeros_like(l_s)
    acc_s[...] = jnp.zeros_like(acc_s)

    def block(j, masked):
        k = qkv_ref[j, :, qw : qw + HD]
        v = qkv_ref[j, :, qw + HD : qw + 2 * HD]
        s = dot(k, q, ((1,), (1,)))
        if masked:
            ok = block_allowed(i, j, rows, start_ref[0])
            s = jnp.where(jnp.concatenate([ok] * heads, axis=1), s, NEG)
        m_old = m_s[...]
        m_new = jnp.maximum(m_old, jnp.max(s, axis=0, keepdims=True) * scale)
        p = jnp.exp2(s * scale - m_new)
        keep = jnp.exp2(m_old - m_new)
        l_s[...] = l_s[...] * keep + jnp.sum(p, axis=0, keepdims=True)
        acc_s[...] = acc_s[...] * keep + dot(v, p.astype(bf16), ((0,), (0,)))
        m_s[...] = m_new

    def masked_step(j, carry):
        block(j, True)
        return carry

    def plain_step(j, carry):
        block(j, False)
        return carry

    block(i, True)
    lax.fori_loop(lo_ref[i], hi_ref[i], masked_step, 0)
    lax.fori_loop(hi_ref[i], i, plain_step, 0)
    total = l_s[...]
    result = unstack_heads(jnp.transpose(acc_s[...] / total), heads)
    raw_ref[0] = result
    out_ref[0] = result.astype(bf16)
    lse_ref[0] = jnp.broadcast_to(m_s[...] + jnp.log2(total), (8, heads * rows))


def attend(lo, hi, start, qkv, heads):
    n, rows, w = qkv.shape
    qw = heads * HD
    smem = pl.BlockSpec(memory_space=pltpu.SMEM)
    pairs = heads * (n * rows) ** 2 // 2
    per_block = lambda shape: pl.BlockSpec((1,) + shape, lambda i: (i, 0, 0))
    return pl.pallas_call(
        functools.partial(attend_kernel, heads),
        grid=(n,),
        out_shape=(
            jax.ShapeDtypeStruct((n, rows, qw), bf16),
            jax.ShapeDtypeStruct((n, rows, qw), f32),
            jax.ShapeDtypeStruct((n, 8, heads * rows), f32),
        ),
        in_specs=[
            smem,
            smem,
            per_block((1, rows)),
            pl.BlockSpec((n, rows, w), lambda i: (0, 0, 0)),
        ],
        out_specs=(per_block((rows, qw)), per_block((rows, qw)), per_block((8, heads * rows))),
        scratch_shapes=[
            pltpu.VMEM((1, heads * rows), f32),
            pltpu.VMEM((1, heads * rows), f32),
            pltpu.VMEM((HD, heads * rows), f32),
        ],
        compiler_params=pltpu.CompilerParams(vmem_limit_bytes=48 << 20),
        cost_estimate=pl.CostEstimate(flops=0, bytes_accessed=1 << 20, transcendentals=0),
        name="attend",
    )(lo, hi, start, qkv)


def attend_back_kernel(
    heads,
    lo_ref,
    hi_ref,
    start_ref,
    qkv_ref,
    g_ref,
    raw_ref,
    lse_ref,
    dq_ref,
    dkv_ref,
    dkv_s,
    dq_s,
):
    n, rows, _ = qkv_ref.shape
    qw = heads * HD
    scale = LOG2E * HD**-0.5
    i = pl.program_id(0)

    @pl.when(i == 0)
    def _():
        dkv_s[...] = jnp.zeros_like(dkv_s)

    dq_s[...] = jnp.zeros_like(dq_s)
    q = stack_heads(qkv_ref[i, :, :qw], heads)
    g_flat = g_ref[i]
    g = stack_heads(g_flat, heads)
    product = g_flat.astype(f32) * raw_ref[0]
    inner = jnp.concatenate(
        [
            jnp.sum(product[:, h * HD : (h + 1) * HD], axis=1, keepdims=True)
            for h in range(heads)
        ],
        axis=0,
    )
    inner = jnp.transpose(jnp.broadcast_to(inner, (heads * rows, LANES)))[:1]
    lse = lse_ref[0, :1]

    def block(j, masked):
        k = qkv_ref[j, :, qw : qw + HD]
        v = qkv_ref[j, :, qw + HD : qw + 2 * HD]
        s = dot(k, q, ((1,), (1,)))
        grad_probs = dot(v, g, ((1,), (1,)))
        p = jnp.exp2(s * scale - lse)
        if masked:
            ok = block_allowed(i, j, rows, start_ref[0])
            p = jnp.where(jnp.concatenate([ok] * heads, axis=1), p, 0.0)
        grad_scores = (p * (grad_probs - inner)).astype(bf16)
        dkv_s[j, :, :HD] += dot(grad_scores, q)
        dkv_s[j, :, HD:] += dot(p.astype(bf16), g)
        dq_s[...] += dot(k, grad_scores, ((0,), (0,)))

    def masked_step(j, carry):
        block(j, True)
        return carry

    def plain_step(j, carry):
        block(j, False)
        return carry

    lax.fori_loop(lo_ref[i], hi_ref[i], masked_step, 0)
    lax.fori_loop(hi_ref[i], i, plain_step, 0)
    block(i, True)
    dq = unstack_heads(jnp.transpose(dq_s[...] * HD**-0.5), heads)
    dq_ref[0] = dq.astype(bf16)

    @pl.when(i == n - 1)
    def _():
        for r in range(n):
            done = dkv_s[r]
            dkv_ref[r] = jnp.concatenate([done[:, :HD] * HD**-0.5, done[:, HD:]], axis=1).astype(
                bf16
            )


def attend_back(lo, hi, start, qkv, grad, raw, lse, heads):
    n, rows, w = qkv.shape
    qw = heads * HD
    smem = pl.BlockSpec(memory_space=pltpu.SMEM)
    pairs = heads * (n * rows) ** 2 // 2
    per_block = lambda shape: pl.BlockSpec((1,) + shape, lambda i: (i, 0, 0))
    whole = lambda shape: pl.BlockSpec(shape, lambda i: (0, 0, 0))
    return pl.pallas_call(
        functools.partial(attend_back_kernel, heads),
        grid=(n,),
        out_shape=(
            jax.ShapeDtypeStruct((n, rows, qw), bf16),
            jax.ShapeDtypeStruct((n, rows, 2 * HD), bf16),
        ),
        in_specs=[
            smem,
            smem,
            per_block((1, rows)),
            whole((n, rows, w)),
            whole((n, rows, qw)),
            per_block((rows, qw)),
            per_block((8, heads * rows)),
        ],
        out_specs=(per_block((rows, qw)), whole((n, rows, 2 * HD))),
        scratch_shapes=[
            pltpu.VMEM((n, rows, 2 * HD), f32),
            pltpu.VMEM((HD, heads * rows), f32),
        ],
        compiler_params=pltpu.CompilerParams(vmem_limit_bytes=48 << 20),
        cost_estimate=pl.CostEstimate(flops=0, bytes_accessed=1 << 20, transcendentals=0),
        name="attend_back",
    )(lo, hi, start, qkv, grad, raw, lse)


def rotate_lanes(v, cosine, signed_sine):
    parts = []
    for c in range(v.shape[1] // LANES):
        part = v[:, c * LANES : (c + 1) * LANES]
        lane = lax.broadcasted_iota(jnp.int32, part.shape, 1)
        other = jnp.where(
            lane % HD < HD // 2,
            pltpu.roll(part, LANES - HD // 2, 1),
            pltpu.roll(part, HD // 2, 1),
        )
        parts.append(part * cosine + other * signed_sine)
    return jnp.concatenate(parts, axis=1) if len(parts) > 1 else parts[0]


def pack_kernel(copies, q_ref, k_ref, v_ref, cos_ref, sin_ref, out_ref):
    qw = q_ref.shape[1]
    cosine = cos_ref[...]
    sine = sin_ref[...]
    out_ref[0, :, :qw] = rotate_lanes(q_ref[...], cosine, sine).astype(bf16)
    k = rotate_lanes(k_ref[...], cosine, sine)
    v = v_ref[...]
    first = (pl.program_id(0) // copies) % 2 == 0
    lane = lax.broadcasted_iota(jnp.int32, k.shape, 1)
    k = jnp.where(first, k, pltpu.roll(k, HD, 1))
    v = jnp.where(first, pltpu.roll(v, HD, 1), v)
    out_ref[0, :, qw:] = jnp.where(lane < HD, k, v).astype(bf16)


def pack_heads(projected, cosine, sine, seq, rows, n):
    qw = H * HD // n
    copies = n // KV
    k_at = H * HD // LANES
    v_at = k_at + KV * HD // LANES
    table = pl.BlockSpec((rows, LANES), lambda d: (seq, 0))
    return pl.pallas_call(
        functools.partial(pack_kernel, copies),
        grid=(n,),
        in_specs=[
            pl.BlockSpec((rows, qw), lambda d: (seq, d)),
            pl.BlockSpec((rows, LANES), lambda d: (seq, k_at + d // copies // 2)),
            pl.BlockSpec((rows, LANES), lambda d: (seq, v_at + d // copies // 2)),
            table,
            table,
        ],
        out_specs=pl.BlockSpec((1, rows, qw + 2 * HD), lambda d: (d, 0, 0)),
        out_shape=jax.ShapeDtypeStruct((n, rows, qw + 2 * HD), bf16),
        cost_estimate=pl.CostEstimate(flops=0, bytes_accessed=6 << 20, transcendentals=0),
        name="pack_heads",
    )(projected, projected, projected, cosine, sine)


def unpack_kernel(n, in_ref, cos_ref, sin_ref, out_ref):
    qw = in_ref.shape[2] - 2 * HD
    copies = n // KV
    cosine = cos_ref[...]
    sine = -sin_ref[...]
    lane = lax.broadcasted_iota(jnp.int32, cosine.shape, 1)
    for d in range(n):
        part = in_ref[d, :, :qw].astype(f32)
        out_ref[:, d * qw : (d + 1) * qw] = rotate_lanes(part, cosine, sine).astype(bf16)
    for pair in range(KV // 2):
        sums = []
        for head in (2 * pair, 2 * pair + 1):
            slots = [in_ref[head * copies + c, :, qw:].astype(f32) for c in range(copies)]
            sums.append(sum(slots[1:], slots[0]))
        k = jnp.where(lane < HD, sums[0], pltpu.roll(sums[1], HD, 1))
        v = jnp.where(lane < HD, pltpu.roll(sums[0], HD, 1), sums[1])
        k_at = H * HD + pair * LANES
        v_at = k_at + KV * HD
        out_ref[:, k_at : k_at + LANES] = rotate_lanes(k, cosine, sine).astype(bf16)
        out_ref[:, v_at : v_at + LANES] = v.astype(bf16)


def unpack_heads(pieces, cosine, sine):
    n, rows, w = pieces.shape
    cols = H * HD + 2 * KV * HD
    return pl.pallas_call(
        functools.partial(unpack_kernel, n),
        out_shape=jax.ShapeDtypeStruct((rows, cols), bf16),
        in_specs=[pl.BlockSpec(memory_space=pltpu.VMEM)] * 3,
        out_specs=pl.BlockSpec(memory_space=pltpu.VMEM),
        compiler_params=pltpu.CompilerParams(vmem_limit_bytes=32 << 20),
        cost_estimate=pl.CostEstimate(flops=0, bytes_accessed=4 << 20, transcendentals=0),
        name="unpack_heads",
    )(pieces, cosine, sine)


def interleave_kernel(core_ref, own_ref, other_ref, out_ref):
    del core_ref
    for i, ref in enumerate((own_ref, other_ref)):

        @pl.when(pl.program_id(2) == i)
        def _():
            out_ref[0, 0, 0] = ref[0, :, 0]


def interleave(core, own, other):
    nx, ny, inner, sub, cols = own.shape
    spec = pl.BlockSpec((1, ny, 1, sub, cols), lambda x, k, i, core_ref: (x, 0, k, 0, 0))
    return pl.pallas_call(
        interleave_kernel,
        grid_spec=pltpu.PrefetchScalarGridSpec(
            num_scalar_prefetch=1,
            grid=(nx, inner, 2),
            in_specs=[spec, spec],
            out_specs=pl.BlockSpec(
                (1, 1, 1, ny, sub, cols), lambda x, k, i, core_ref: (x, core_ref[0] ^ i, k, 0, 0, 0)
            ),
        ),
        out_shape=jax.ShapeDtypeStruct((nx, 2, inner, ny, sub, cols), own.dtype),
        compiler_params=pltpu.CompilerParams(vmem_limit_bytes=48 << 20),
        cost_estimate=pl.CostEstimate(flops=0, bytes_accessed=1 << 16, transcendentals=0),
        name="interleave",
    )(core, own, other)


ROW_TILE = 256


def small_cost(size):
    return pl.CostEstimate(flops=0, bytes_accessed=size, transcendentals=0)


def resident(shape, index):
    return pl.BlockSpec(shape, lambda i: index, pipeline_mode=pl.Buffered(1))


def by_rows(tile, cols, at=0):
    return pl.BlockSpec((tile, cols), lambda i: (i, at))


def load_rows(w_ref, w_s, sems):
    xy, _, nfar, _, sub, _ = w_ref.shape
    ny = 2
    copies = []
    for g in range(xy):
        for core in range(2):
            for far in range(nfar):
                for near in range(2):
                    block = (((g // ny * 2 + core) * nfar + far) * 2 + near) * ny + g % ny
                    copies.append(
                        pltpu.make_async_copy(
                            w_ref.at[g, core, far, near],
                            w_s.at[pl.ds(block * sub, sub)],
                            sems.at[block],
                        )
                    )
    for copy in copies:
        copy.start()
    for copy in copies:
        copy.wait()


def with_weights(kernel):
    def run(x_ref, w_ref, *refs):
        *refs, w_s, sems = refs

        @pl.when(pl.program_id(0) == 0)
        def _():
            load_rows(w_ref, w_s, sems)

        kernel(x_ref, w_s, *refs)

    return run


def over_rows(kernel, x, w, others, outs, name):
    m = x.shape[0]
    blocks = w.shape[0] * w.shape[1] * w.shape[2] * w.shape[3]
    tile = min(ROW_TILE, m)
    return pl.pallas_call(
        with_weights(kernel),
        grid=(m // tile,),
        in_specs=[by_rows(tile, x.shape[1]), pl.BlockSpec(memory_space=pl.ANY)]
        + [by_rows(tile, other.shape[1]) for other in others],
        out_specs=[by_rows(tile, cols) for cols, _ in outs],
        out_shape=[jax.ShapeDtypeStruct((m, cols), t) for cols, t in outs],
        scratch_shapes=[
            pltpu.VMEM((blocks * w.shape[4], w.shape[5]), bf16),
            pltpu.SemaphoreType.DMA((blocks,)),
        ],
        compiler_params=pltpu.CompilerParams(vmem_limit_bytes=48 << 20),
        cost_estimate=small_cost(1 << 16),
        name=name,
    )(x, w, *others)


def ffn_forward_kernel(x_ref, w_ref, gate_ref, up_ref, active_ref):
    units = gate_ref.shape[1]
    x = x_ref[...]
    gate = dot(x, w_ref[:, :units])
    gate_ref[...] = gate
    up = dot(x, w_ref[:, units:])
    up_ref[...] = up
    active_ref[...] = (gate * jax.nn.sigmoid(gate) * up).astype(bf16)


def ffn_forward(x, w_gate_up):
    units = w_gate_up.shape[-1] // 2
    outs = [(units, f32), (units, f32), (units, bf16)]
    return over_rows(ffn_forward_kernel, x, w_gate_up, [], outs, "ffn_forward")


def ffn_backward_kernel(g_ref, w_ref, gate_ref, up_ref, both_ref):
    units = gate_ref.shape[1]
    grad_active = dot(g_ref[...], w_ref[...])
    gate = gate_ref[...]
    s = jax.nn.sigmoid(gate)
    grad_gate = grad_active * up_ref[...] * s * (1.0 + gate * (1.0 - s))
    both_ref[:, :units] = grad_gate.astype(bf16)
    both_ref[:, units:] = (grad_active * gate * s).astype(bf16)


def ffn_backward(grad, w_down, gate, up):
    outs = [(2 * gate.shape[1], bf16)]
    return over_rows(ffn_backward_kernel, grad, w_down, [gate, up], outs, "ffn_backward")[0]


def project_rows_kernel(x_ref, w_ref, out_ref):
    out_ref[...] = dot(x_ref[...], w_ref[...], ((1,), (1,))).astype(bf16)


def project_rows(x, w):
    rows = w.shape[0] * w.shape[1] * w.shape[2] * w.shape[3] * w.shape[4]
    return over_rows(project_rows_kernel, x, w, [], [(rows, bf16)], "project_rows")[0]


def outer_sum_kernel(pairs, *refs):
    out_ref = refs[-1]
    _, ny, _, nfar, _, sub, _ = out_ref.shape
    total = None
    for p in range(pairs):
        term = dot(refs[2 * p][...], refs[2 * p + 1][...], ((0,), (0,)))
        total = term if total is None else total + term
    for far in range(nfar):
        for near in range(2):
            for y in range(ny):
                at = ((far * 2 + near) * ny + y) * sub
                out_ref[0, y, 0, far, near] = total[at : at + sub].astype(bf16)


def outer_sum(pairs, cols, at, owners):
    nx, nfar, ny = owners
    width = pairs[0][0].shape[1]
    tile = width // (2 * nx)
    sub = tile // (2 * nfar * ny)
    in_specs, operands = [], []
    for a, b in pairs:
        in_specs.append(pl.BlockSpec((a.shape[0], tile), lambda i: (0, i)))
        in_specs.append(resident((b.shape[0], cols), (0, at)))
        operands += [a, b]
    return pl.pallas_call(
        functools.partial(outer_sum_kernel, len(pairs)),
        grid=(2 * nx,),
        in_specs=in_specs,
        out_specs=pl.BlockSpec(
            (1, ny, 1, nfar, 2, sub, cols), lambda i: (i // 2, 0, i % 2, 0, 0, 0, 0)
        ),
        out_shape=jax.ShapeDtypeStruct((nx, ny, 2, nfar, 2, sub, cols), bf16),
        compiler_params=pltpu.CompilerParams(vmem_limit_bytes=48 << 20),
        cost_estimate=small_cost(1 << 16),
        name="outer_sum",
    )(*operands)


def rms_scale(hidden):
    return lax.rsqrt(jnp.mean(hidden * hidden, axis=-1, keepdims=True) + EPSILON)


def rms_back(grad_scaled, scaled, inverse):
    return inverse * (grad_scaled - scaled * jnp.mean(grad_scaled * scaled, axis=-1, keepdims=True))


def exchange(pieces):
    return lax.all_to_all(pieces, SEQ, split_axis=0, concat_axis=0, tiled=True)


def local(
    tokens,
    cotangent,
    segments,
    joint_projection_matrix,
    output_weight_rows,
    gate_up_weight,
    down_weight_rows,
    attn_gain,
    ffn_gain,
):
    n = lax.axis_size(SEQ)
    me = lax.axis_index(SEQ)
    seqs, rows, width = tokens.shape
    full_len = segments.shape[1]
    heads = H // n
    qw = heads * HD
    sub = joint_projection_matrix.shape[0]
    part = FF // 4
    nx, nfar, ny = (lax.axis_size(axis) for axis in ("x", "far", "y"))
    flow = Flow()

    column = jnp.arange(full_len, dtype=jnp.int32)
    starts_here = jnp.concatenate(
        [jnp.ones((seqs, 1), dtype=bool), segments[:, 1:] != segments[:, :-1]], axis=1
    )
    doc_start = lax.cummax(jnp.where(starts_here, column, 0), axis=1)
    position = lax.dynamic_slice_in_dim(column - doc_start, me * rows, rows, 1)
    doc_start = doc_start.reshape(seqs, n, rows)
    first_block = doc_start[:, :, 0] // rows
    plain_from = jnp.minimum((doc_start[:, :, -1] + rows - 1) // rows, jnp.arange(n))
    plain_from = jnp.maximum(plain_from, first_block)
    doc_start = doc_start[:, :, None, :]
    frequency = ROTARY_BASE ** (-(jnp.arange(HD // 2, dtype=f32) * 2.0) / HD)
    angles = position.astype(f32).reshape(seqs * rows, 1) * frequency
    cosine = jnp.concatenate([jnp.cos(angles)] * 4, axis=1)
    sine = jnp.concatenate([-jnp.sin(angles), jnp.sin(angles)] * 2, axis=1)

    hidden_all = tokens.reshape(seqs * rows, width).astype(f32)
    grad_out_all = cotangent.reshape(seqs * rows, width)
    gain_one = attn_gain.astype(f32)
    gain_two = ffn_gain.astype(f32)

    def own_rows(weight):
        gathered = lax.all_gather(weight, ("x",) + SEQ, axis=0, tiled=True)
        return gathered.reshape(nx, -1, weight.shape[1])

    def core_features(values):
        w = width // (2 * nx)
        bit = my_bit(CORE)
        return tuple(
            jnp.concatenate(
                [lax.dynamic_slice_in_dim(values, (2 * i + c) * w, w, 1) for i in range(nx)], axis=1
            )
            for c in (bit, 1 - bit)
        )

    def flat(values):
        return values.reshape(-1, values.shape[-1])

    def lane_halves(values, key):
        w = values.shape[-1] // 2
        bit = my_bit(key)
        return (
            lax.dynamic_slice_in_dim(values, bit * w, w, values.ndim - 1),
            lax.dynamic_slice_in_dim(values, (1 - bit) * w, w, values.ndim - 1),
        )

    def lanes_by_bit(mine, other, key):
        low = my_bit(key) == 0
        return [jnp.where(low, mine, other), jnp.where(low, other, mine)]

    class Group:
        def __init__(self, values):
            self.values, self.core = values, swap(values, CORE)
            self.arrived = swap(values, NEAR)

        def done(self):
            near = self.arrived
            return jnp.concatenate([self.values, self.core, near, swap(near, CORE)], axis=0)

    class GroupSum:
        def __init__(self, partial):
            self.mine = partial.reshape(2, 2, rows, -1)
            self.arrived = swap(self.mine[:, 1], CORE)

        def next(self):
            both = self.mine[:, 0].astype(f32) + self.arrived.astype(f32)
            self.mine = both[0]
            self.arrived = swap(both[1].astype(bf16), NEAR)

        def done(self):
            return self.mine + self.arrived.astype(f32)

    qkv = Gather(joint_projection_matrix, "near", 0)
    out = Gather(output_weight_rows, "far", 0)
    flow.close(flow.token, wait=[qkv])

    qkv = Gather(qkv.done(), "far", 0)
    near_parts, near_swaps = [], []
    for weight in (gate_up_weight[:, :FF], gate_up_weight[:, FF:], down_weight_rows):
        mine, other = lane_halves(weight, NEAR)
        near_parts.append(mine)
        near_swaps.append(other)
    near_swap = Swap(flow.open(jnp.stack(near_swaps)), NEAR)
    inverse_one = rms_scale(hidden_all)
    scaled_one = hidden_all * inverse_one
    normed_one = (scaled_one * gain_one).astype(bf16)
    normed_one_own, normed_one_other = core_features(normed_one)
    normed_one_own, normed_one_other, cosine, sine = flow.close(
        normed_one_own, normed_one_other, cosine, sine, wait=[qkv, near_swap, out]
    )

    left, right = jnp.split(qkv.done(), 2, axis=-1)
    left = Gather(left, "y", 2)
    right = Gather(right, "x", 0)
    core_parts, core_swaps = [], []
    for mine, arrived in zip(near_parts, near_swap.arrived):
        mine, other = lane_halves(by_bit(mine, arrived, NEAR, 0), CORE)
        core_parts.append(mine)
        core_swaps.append(other)
    core_swap = Swap(jnp.stack(core_swaps), CORE)
    out = Gather(out.done(), "near", 1)
    flow.close(flow.token, wait=[left, right, core_swap, out])

    def over_xy(values):
        gathered = lax.all_gather(flat(values), ("x", "y"), axis=0, tiled=True)
        return gathered.reshape((nx * ny,) + values.shape)

    left = Gather(left.done(), "x", 0)
    right = Gather(right.done(), "y", 3)
    gate, up, down = (
        by_bit(mine, arrived, CORE, 0) for mine, arrived in zip(core_parts, core_swap.arrived)
    )
    gate = Gather(gate, "far", 1)
    w_out_own = over_xy(out.done())
    up, down = flow.close(up, down, wait=[left, right, gate])

    w_own = jnp.concatenate([flat(left.done()), flat(right.done())], axis=1)
    w_swap = Swap(w_own, CORE)
    up = Gather(up, "far", 1)
    projected = dot(normed_one_own, w_own)
    w_other = w_swap.arrived
    projected = projected + dot(normed_one_other, w_other)
    packed_0 = pack_heads(projected, cosine, sine, 0, rows, n)
    packed_0 = flow.close(packed_0, wait=[up])

    def attend_one(b, qkv_b):
        return attend(first_block[b], plain_from[b], doc_start[b], qkv_b, heads)

    packed_0, projected, w_other = flow.open(packed_0, projected, w_other)
    qkv_0 = exchange(packed_0)
    w_gate_up = over_xy(jnp.concatenate([gate.done(), up.done()], axis=-1))
    packed_1 = pack_heads(projected, cosine, sine, 1, rows, n)
    core_arg = lax.axis_index("core").astype(jnp.int32).reshape(1)
    w_shape = (nx, 1, nfar * 2, -1, w_own.shape[1])
    w_qkv = flat(interleave(core_arg, w_own.reshape(w_shape), w_other.reshape(w_shape)))
    qkv_0, packed_1, w_qkv = flow.close(qkv_0, packed_1, w_qkv)

    qkv_0, packed_1 = flow.open(qkv_0, packed_1)
    qkv_1 = exchange(packed_1)
    attended_0, raw_0, lse_0 = attend_one(0, qkv_0)
    attended_0, qkv_1, w_out_own = flow.close(attended_0, qkv_1, w_out_own)

    attended_0, qkv_1 = flow.open(attended_0, qkv_1)
    back_0 = exchange(attended_0)
    out_swap = Swap(w_out_own, CORE)
    attended_1, raw_1, lse_1 = attend_one(1, qkv_1)
    attended_1, back_0 = flow.close(attended_1, back_0, wait=[out_swap])

    def after_attention(b, back):
        attended = jnp.concatenate([back[s] for s in range(n)], axis=1)
        middle = hidden_all[b * rows : (b + 1) * rows] + dot(attended, w_out, ((1,), (1,)))
        inverse = rms_scale(middle)
        scaled = middle * inverse
        return attended, middle, inverse, scaled, (scaled * gain_two).astype(bf16)

    attended_1, back_0 = flow.open(attended_1, back_0)
    back_1 = exchange(attended_1)
    w_shape = (nx, ny, nfar * 2, sub, width)
    w_out = interleave(core_arg, w_out_own.reshape(w_shape), out_swap.arrived.reshape(w_shape))
    w_out = flat(w_out)
    down = Gather(flow.open(down), "far", 1)
    attended_0, middle_0, inverse_0, scaled_0, normed_0 = after_attention(0, back_0)
    back_1, normed_0 = flow.close(back_1, normed_0)

    back_1, normed_0 = flow.open(back_1, normed_0)
    group_0 = Group(normed_0)
    attended_1, middle_1, inverse_1, scaled_1, normed_1 = after_attention(1, back_1)
    normed_1, w_gate_up = flow.close(normed_1, w_gate_up, wait=[group_0, down])
    w_down = over_xy(down.done())
    group_1 = Group(normed_1)
    group_0 = group_0.done()

    gate_0, up_0, active_0 = ffn_forward(group_0, w_gate_up)
    grad_group_0 = Group(flow.open(grad_out_all[:rows]))
    grad_group_1 = Group(flow.open(grad_out_all[rows:]))
    active_0 = flow.close(active_0, wait=[group_1])

    group_1 = group_1.done()
    gate_1, up_1, active_1 = ffn_forward(flow.open(group_1), w_gate_up)
    active_1 = flow.close(active_1, wait=[grad_group_0, grad_group_1])
    grad_group_0 = grad_group_0.done()
    grad_group_1 = grad_group_1.done()

    outer = lambda a, b: dot(a, b, ((0,), (0,)))
    owners = (nx, nfar, ny)

    def sum_to_owners(terms):
        rest = terms.shape[2:]
        terms = terms.reshape(-1, terms.shape[-1])
        total = lax.psum_scatter(terms, ("x", "y"), scatter_dimension=0, tiled=True)
        return total.reshape(rest)

    d_down = outer_sum(
        [(grad_group_0, active_0), (grad_group_1, flow.open(active_1))], part, 0, owners
    )
    d_down = flow.close(d_down)

    d_down = sum_to_owners(flow.open(d_down))
    both_0 = ffn_backward(flow.open(grad_group_0), w_down, gate_0, up_0)
    terms_0 = flow.close(project_rows(both_0, w_gate_up))

    grad_normed_0 = GroupSum(terms_0)
    partial_0 = project_rows(flow.open(active_0), w_down)
    partial_0 = flow.close(partial_0, wait=[grad_normed_0])
    grad_normed_0.next()
    result_0 = GroupSum(partial_0)
    both_1 = ffn_backward(flow.open(grad_group_1), w_down, gate_1, up_1)
    terms_1 = project_rows(both_1, w_gate_up)
    terms_1 = flow.close(terms_1, wait=[grad_normed_0, result_0])

    def before_attention(b, g, scaled, inverse):
        grad_middle = grad_out_all[b * rows : (b + 1) * rows].astype(f32) + rms_back(
            g * gain_two, scaled, inverse
        )
        grad_branch = grad_middle.astype(bf16)
        grad_attended = dot(grad_branch, w_out).astype(bf16)
        grad_heads = [grad_attended[:, d * qw : (d + 1) * qw] for d in range(n)]
        return grad_middle, grad_branch, jnp.stack(grad_heads)

    grad_normed_1 = GroupSum(terms_1)
    result_0.next()
    grad_normed_0 = grad_normed_0.done()
    grad_middle_0, grad_branch_0, grad_heads_0 = before_attention(
        0, grad_normed_0, scaled_0, inverse_0
    )
    grad_heads_0 = flow.close(grad_heads_0, wait=[grad_normed_1])

    grad_normed_1.next()
    grad_heads_0 = exchange(grad_heads_0)
    d_down = Scatter(flow.open(d_down), "far", 1)
    d_up = outer_sum([(flow.open(group_0), both_0), (group_1, both_1)], part, 1, owners)
    d_up = flow.close(d_up, wait=[grad_normed_1])

    d_up = sum_to_owners(flow.open(d_up))
    d_gate = outer_sum([(flow.open(group_0), both_0), (group_1, both_1)], part, 0, owners)
    d_gate, grad_heads_0 = flow.close(d_gate, grad_heads_0, wait=[d_down])

    d_gate = sum_to_owners(flow.open(d_gate))
    grad_normed_1 = grad_normed_1.done()
    grad_middle_1, grad_branch_1, grad_heads_1 = before_attention(
        1, grad_normed_1, scaled_1, inverse_1
    )
    grad_heads_1 = flow.close(grad_heads_1)

    grad_heads_1 = exchange(grad_heads_1)
    grad_branch = jnp.concatenate([grad_branch_0, grad_branch_1], axis=0)
    attended = jnp.concatenate([attended_0, attended_1], axis=0)
    d_out = outer(flow.open(grad_branch), attended).astype(bf16)
    d_out = flow.close(d_out.reshape((nx, 2, -1, attended.shape[1])))

    def core_sum(mine, send):
        total = mine.astype(f32) + swap(send.astype(bf16), CORE).astype(f32)
        total = total.astype(bf16).reshape((nx, nfar, 2, ny, sub, total.shape[-1]))
        return total.transpose((0, 3, 1, 2, 4, 5))

    def attend_back_one(b, qkv_b, grad_b, raw_b, lse_b):
        dq, dkv = attend_back(
            first_block[b], plain_from[b], doc_start[b], qkv_b, grad_b, raw_b, lse_b, heads
        )
        return jnp.concatenate([dq, dkv], axis=2)

    d_out = sum_to_owners(core_sum(*choose(d_out, CORE, 1)))
    back_0 = attend_back_one(0, qkv_0, flow.open(grad_heads_0), raw_0, lse_0)
    d_up = Scatter(flow.open(d_up), "far", 1)
    back_0, grad_heads_1 = flow.close(back_0, grad_heads_1)

    back_0 = exchange(back_0)
    back_1 = attend_back_one(1, qkv_1, flow.open(grad_heads_1), raw_1, lse_1)
    back_1, back_0, d_gate = flow.close(back_1, back_0, d_gate, wait=[d_up])

    back_1 = exchange(back_1)
    partial_1 = project_rows(flow.open(active_1), w_down)
    grad_proj_0 = unpack_heads(flow.open(back_0), cosine[:rows], sine[:rows])
    back_1, grad_proj_0, partial_1 = flow.close(
        back_1, grad_proj_0, partial_1, wait=[result_0]
    )

    d_gate = Scatter(d_gate, "far", 1)
    result_1 = GroupSum(partial_1)
    grad_proj_1 = unpack_heads(back_1, cosine[rows:], sine[rows:])
    grad_proj = jnp.concatenate([grad_proj_0, grad_proj_1], axis=0)
    core_back = Swap(outer(normed_one_other, grad_proj).astype(bf16), CORE)
    grad_normed_one = dot(grad_proj, w_qkv, ((1,), (1,)))
    grad_proj, grad_normed_one = flow.close(
        grad_proj, grad_normed_one, wait=[core_back, result_1, d_gate]
    )
    d_qkv = outer(normed_one_own, grad_proj) + core_back.arrived.astype(f32)
    d_qkv = d_qkv.astype(bf16).reshape((nx, nfar, 2, ny, sub, -1))
    left, right = flow.close(*jnp.split(d_qkv, 2, axis=-1))

    left = Scatter(left, "x", 0)
    right = Scatter(right, "y", 3)
    result_1.next()
    d_out = Scatter(flow.open(d_out), "far", 0)
    ffn = jnp.stack([t.done(last=True) for t in (d_gate, d_up, d_down)])
    mine, send = choose(ffn, NEAR, 2)
    near_back = Swap(send.astype(bf16), NEAR)
    flow.close(flow.token, wait=[left, right])

    left = Scatter(left.done(), "y", 2)
    right = Scatter(right.done(), "x", 0)
    attn_gain_grad = jnp.sum(grad_normed_one * scaled_one, axis=0)
    ffn_gain_grad = jnp.sum(grad_normed_0 * scaled_0, axis=0) + jnp.sum(
        grad_normed_1 * scaled_1, axis=0
    )
    gains = jnp.stack([attn_gain_grad, ffn_gain_grad])
    gains, grad_normed_one = flow.close(gains, grad_normed_one, wait=[left, right, near_back])

    d_qkv = Scatter(jnp.concatenate([left.done(), right.done()], axis=-1), "far", 0)
    gains = sum_axes(gains, "x", "y", "core")
    quarters = []
    for part_of in lanes_by_bit(mine, near_back.arrived.astype(f32), NEAR):
        part_mine, part_send = choose(part_of, CORE, 1)
        quarters += lanes_by_bit(part_mine, swap(part_send.astype(bf16), CORE).astype(f32), CORE)
    d_gate_up = jnp.concatenate([q[k] for k in (0, 1) for q in quarters], axis=1)
    d_down = jnp.concatenate([q[2] for q in quarters], axis=1)
    grad_input = jnp.concatenate([grad_middle_0, grad_middle_1], axis=0) + rms_back(
        grad_normed_one * gain_one, scaled_one, inverse_one
    )
    grad_input, gains, d_gate_up, d_down = flow.close(
        grad_input, gains, d_gate_up, d_down, wait=[d_qkv, d_out]
    )

    d_qkv = Scatter(d_qkv.done(), "near", 0)
    d_out = Scatter(d_out.done(), "near", 0)
    gains = sum_axes(gains, "near", "far")
    result = jnp.concatenate([middle_0 + result_0.done(), middle_1 + result_1.done()], axis=0)
    return (
        result.astype(bf16).reshape(tokens.shape),
        grad_input.reshape(tokens.shape),
        d_qkv.done(last=True),
        d_out.done(last=True),
        d_gate_up,
        d_down,
        gains[0],
        gains[1],
    )


def solution(mesh):
    dp, seq = mesh.devices.shape
    shape = (dp // 2, 2, seq // 4, 2, 2)
    fine = Mesh(mesh.devices.reshape(shape), ("x", "core") + SEQ)
    by_token = P(("x", "core"), SEQ, None)
    by_row = P(("x", "core") + SEQ, None)
    return jax.shard_map(
        local,
        mesh=fine,
        in_specs=(
            by_token,
            by_token,
            P(("x", "core"), None),
            by_row,
            by_row,
            by_row,
            by_row,
            P(),
            P(),
        ),
        out_specs=(by_token, by_token, by_row, by_row, by_row, by_row, P(), P()),
        check_vma=False,
    )
```

```python
import functools
import math

import jax
import jax.numpy as jnp
from jax import lax
from jax.experimental import pallas as pl
from jax.experimental.pallas import tpu as pltpu
from jax.sharding import Mesh
from jax.sharding import PartitionSpec as P

H = 32
HD = 64
KV = 4
FF = 5632

EPSILON = 1e-05
NEG = -1e30
ROTARY_BASE = 10000.0
LOG2E = math.log2(math.e)
LANES = 128

bf16 = jnp.bfloat16
f32 = jnp.float32


def dot(a, b, dims=((1,), (0,))):
    return lax.dot_general(a, b, (dims, ((), ())), preferred_element_type=f32)


CORE = ("core", 0)
NEAR = ("near", 0)
SEQ = ("far", "near", "y")


def axis_bits(axis):
    return [(axis, b) for b in reversed(range((lax.axis_size(axis) - 1).bit_length()))]


def my_bit(key):
    axis, b = key
    return (lax.axis_index(axis) >> b) & 1


def swap(values, key):
    axis, b = key
    return lax.ppermute(values, axis, [(i, i ^ (1 << b)) for i in range(lax.axis_size(axis))])


class Flow:
    def __init__(self):
        self.token = jnp.zeros((), f32)

    def open(self, *values):
        opened = lax.optimization_barrier(values + (self.token,))[:-1]
        return opened if len(values) > 1 else opened[0]

    def close(self, *values, wait=()):
        arrived = tuple(transfer.arrived for transfer in wait)
        closed = lax.optimization_barrier(values + arrived + (self.token,))
        for transfer, value in zip(wait, closed[len(values) :]):
            transfer.arrived = value
        self.token = closed[-1]
        return closed[: len(values)] if len(values) > 1 else closed[0]


def choose(values, key, axis):
    bit = my_bit(key)
    return (
        lax.dynamic_index_in_dim(values, bit, axis, keepdims=False),
        lax.dynamic_index_in_dim(values, 1 - bit, axis, keepdims=False),
    )


def by_bit(mine, other, key, axis):
    low = my_bit(key) == 0
    return jnp.stack([jnp.where(low, mine, other), jnp.where(low, other, mine)], axis=axis)


class Swap:
    def __init__(self, values, key):
        self.arrived = swap(values, key)


class Gather:
    def __init__(self, values, axis, at):
        self.values, self.axis, self.at = values, axis, at
        self.arrived = swap(values, axis_bits(axis)[0])

    def done(self):
        values, other, shape = self.values, self.arrived, self.values.shape
        for step, key in enumerate(axis_bits(self.axis)):
            if step:
                other = swap(values, key)
            values = by_bit(values, other, key, self.at + step)
        return values.reshape(shape[: self.at] + (lax.axis_size(self.axis),) + shape[self.at :])


class Scatter:
    def __init__(self, values, axis, at):
        self.keys, self.at = axis_bits(axis), at
        shape = values.shape
        values = values.reshape(shape[:at] + (2,) * len(self.keys) + shape[at + 1 :])
        self.start(values)

    def start(self, values):
        self.mine, send = choose(values, self.keys[0], self.at)
        self.arrived = swap(send.astype(bf16), self.keys[0])

    def done(self, last=False):
        while True:
            values = self.mine.astype(f32) + self.arrived.astype(f32)
            if not last:
                values = values.astype(bf16)
            self.keys = self.keys[1:]
            if not self.keys:
                return values
            self.start(values)


def sum_axes(values, *axes):
    for axis in axes:
        for key in axis_bits(axis):
            values = values + swap(values, key)
    return values


def stack_heads(x, heads):
    return jnp.concatenate([x[:, h * HD : (h + 1) * HD] for h in range(heads)], axis=0)


def unstack_heads(x, heads):
    rows = x.shape[0] // heads
    return jnp.concatenate([x[h * rows : (h + 1) * rows] for h in range(heads)], axis=1)


def block_allowed(i, j, rows, start):
    key_pos = j * rows + lax.broadcasted_iota(jnp.int32, (rows, rows), 0)
    query_pos = i * rows + lax.broadcasted_iota(jnp.int32, (rows, rows), 1)
    return (key_pos <= query_pos) & (key_pos >= start)


def attend_kernel(
    heads, lo_ref, hi_ref, start_ref, qkv_ref, out_ref, raw_ref, lse_ref, m_s, l_s, acc_s
):
    rows = qkv_ref.shape[1]
    qw = heads * HD
    scale = LOG2E * HD**-0.5
    i = pl.program_id(0)
    q = stack_heads(qkv_ref[i, :, :qw], heads)
    m_s[...] = jnp.full_like(m_s, NEG)
    l_s[...] = jnp.zeros_like(l_s)
    acc_s[...] = jnp.zeros_like(acc_s)

    def block(j, masked):
        k = qkv_ref[j, :, qw : qw + HD]
        v = qkv_ref[j, :, qw + HD : qw + 2 * HD]
        s = dot(k, q, ((1,), (1,)))
        if masked:
            ok = block_allowed(i, j, rows, start_ref[0])
            s = jnp.where(jnp.concatenate([ok] * heads, axis=1), s, NEG)
        m_old = m_s[...]
        m_new = jnp.maximum(m_old, jnp.max(s, axis=0, keepdims=True) * scale)
        p = jnp.exp2(s * scale - m_new)
        keep = jnp.exp2(m_old - m_new)
        l_s[...] = l_s[...] * keep + jnp.sum(p, axis=0, keepdims=True)
        acc_s[...] = acc_s[...] * keep + dot(v, p.astype(bf16), ((0,), (0,)))
        m_s[...] = m_new

    def masked_step(j, carry):
        block(j, True)
        return carry

    def plain_step(j, carry):
        block(j, False)
        return carry

    block(i, True)
    lax.fori_loop(lo_ref[i], hi_ref[i], masked_step, 0)
    lax.fori_loop(hi_ref[i], i, plain_step, 0)
    total = l_s[...]
    result = unstack_heads(jnp.transpose(acc_s[...] / total), heads)
    raw_ref[0] = result
    out_ref[0] = result.astype(bf16)
    lse_ref[0] = jnp.broadcast_to(m_s[...] + jnp.log2(total), (8, heads * rows))


def attend(lo, hi, start, qkv, heads):
    n, rows, w = qkv.shape
    qw = heads * HD
    smem = pl.BlockSpec(memory_space=pltpu.SMEM)
    pairs = heads * (n * rows) ** 2 // 2
    per_block = lambda shape: pl.BlockSpec((1,) + shape, lambda i: (i, 0, 0))
    return pl.pallas_call(
        functools.partial(attend_kernel, heads),
        grid=(n,),
        out_shape=(
            jax.ShapeDtypeStruct((n, rows, qw), bf16),
            jax.ShapeDtypeStruct((n, rows, qw), f32),
            jax.ShapeDtypeStruct((n, 8, heads * rows), f32),
        ),
        in_specs=[
            smem,
            smem,
            per_block((1, rows)),
            pl.BlockSpec((n, rows, w), lambda i: (0, 0, 0)),
        ],
        out_specs=(per_block((rows, qw)), per_block((rows, qw)), per_block((8, heads * rows))),
        scratch_shapes=[
            pltpu.VMEM((1, heads * rows), f32),
            pltpu.VMEM((1, heads * rows), f32),
            pltpu.VMEM((HD, heads * rows), f32),
        ],
        compiler_params=pltpu.CompilerParams(vmem_limit_bytes=48 << 20),
        cost_estimate=pl.CostEstimate(flops=0, bytes_accessed=1 << 20, transcendentals=0),
        name="attend",
    )(lo, hi, start, qkv)


def attend_back_kernel(
    heads,
    lo_ref,
    hi_ref,
    start_ref,
    qkv_ref,
    g_ref,
    raw_ref,
    lse_ref,
    dq_ref,
    dkv_ref,
    dkv_s,
    dq_s,
):
    n, rows, _ = qkv_ref.shape
    qw = heads * HD
    scale = LOG2E * HD**-0.5
    i = pl.program_id(0)

    @pl.when(i == 0)
    def _():
        dkv_s[...] = jnp.zeros_like(dkv_s)

    dq_s[...] = jnp.zeros_like(dq_s)
    q = stack_heads(qkv_ref[i, :, :qw], heads)
    g_flat = g_ref[i]
    g = stack_heads(g_flat, heads)
    product = g_flat.astype(f32) * raw_ref[0]
    inner = jnp.concatenate(
        [
            jnp.sum(product[:, h * HD : (h + 1) * HD], axis=1, keepdims=True)
            for h in range(heads)
        ],
        axis=0,
    )
    inner = jnp.transpose(jnp.broadcast_to(inner, (heads * rows, LANES)))[:1]
    lse = lse_ref[0, :1]

    def block(j, masked):
        k = qkv_ref[j, :, qw : qw + HD]
        v = qkv_ref[j, :, qw + HD : qw + 2 * HD]
        s = dot(k, q, ((1,), (1,)))
        grad_probs = dot(v, g, ((1,), (1,)))
        p = jnp.exp2(s * scale - lse)
        if masked:
            ok = block_allowed(i, j, rows, start_ref[0])
            p = jnp.where(jnp.concatenate([ok] * heads, axis=1), p, 0.0)
        grad_scores = (p * (grad_probs - inner)).astype(bf16)
        dkv_s[j, :, :HD] += dot(grad_scores, q)
        dkv_s[j, :, HD:] += dot(p.astype(bf16), g)
        dq_s[...] += dot(k, grad_scores, ((0,), (0,)))

    def masked_step(j, carry):
        block(j, True)
        return carry

    def plain_step(j, carry):
        block(j, False)
        return carry

    lax.fori_loop(lo_ref[i], hi_ref[i], masked_step, 0)
    lax.fori_loop(hi_ref[i], i, plain_step, 0)
    block(i, True)
    dq = unstack_heads(jnp.transpose(dq_s[...] * HD**-0.5), heads)
    dq_ref[0] = dq.astype(bf16)

    @pl.when(i == n - 1)
    def _():
        for r in range(n):
            done = dkv_s[r]
            dkv_ref[r] = jnp.concatenate([done[:, :HD] * HD**-0.5, done[:, HD:]], axis=1).astype(
                bf16
            )


def attend_back(lo, hi, start, qkv, grad, raw, lse, heads):
    n, rows, w = qkv.shape
    qw = heads * HD
    smem = pl.BlockSpec(memory_space=pltpu.SMEM)
    pairs = heads * (n * rows) ** 2 // 2
    per_block = lambda shape: pl.BlockSpec((1,) + shape, lambda i: (i, 0, 0))
    whole = lambda shape: pl.BlockSpec(shape, lambda i: (0, 0, 0))
    return pl.pallas_call(
        functools.partial(attend_back_kernel, heads),
        grid=(n,),
        out_shape=(
            jax.ShapeDtypeStruct((n, rows, qw), bf16),
            jax.ShapeDtypeStruct((n, rows, 2 * HD), bf16),
        ),
        in_specs=[
            smem,
            smem,
            per_block((1, rows)),
            whole((n, rows, w)),
            whole((n, rows, qw)),
            per_block((rows, qw)),
            per_block((8, heads * rows)),
        ],
        out_specs=(per_block((rows, qw)), whole((n, rows, 2 * HD))),
        scratch_shapes=[
            pltpu.VMEM((n, rows, 2 * HD), f32),
            pltpu.VMEM((HD, heads * rows), f32),
        ],
        compiler_params=pltpu.CompilerParams(vmem_limit_bytes=48 << 20),
        cost_estimate=pl.CostEstimate(flops=0, bytes_accessed=1 << 20, transcendentals=0),
        name="attend_back",
    )(lo, hi, start, qkv, grad, raw, lse)


def rotate_lanes(v, cosine, signed_sine):
    parts = []
    for c in range(v.shape[1] // LANES):
        part = v[:, c * LANES : (c + 1) * LANES]
        lane = lax.broadcasted_iota(jnp.int32, part.shape, 1)
        other = jnp.where(
            lane % HD < HD // 2,
            pltpu.roll(part, LANES - HD // 2, 1),
            pltpu.roll(part, HD // 2, 1),
        )
        parts.append(part * cosine + other * signed_sine)
    return jnp.concatenate(parts, axis=1) if len(parts) > 1 else parts[0]


def pack_kernel(copies, q_ref, k_ref, v_ref, cos_ref, sin_ref, out_ref):
    qw = q_ref.shape[1]
    cosine = cos_ref[...]
    sine = sin_ref[...]
    out_ref[0, :, :qw] = rotate_lanes(q_ref[...], cosine, sine).astype(bf16)
    k = rotate_lanes(k_ref[...], cosine, sine)
    v = v_ref[...]
    first = (pl.program_id(0) // copies) % 2 == 0
    lane = lax.broadcasted_iota(jnp.int32, k.shape, 1)
    k = jnp.where(first, k, pltpu.roll(k, HD, 1))
    v = jnp.where(first, pltpu.roll(v, HD, 1), v)
    out_ref[0, :, qw:] = jnp.where(lane < HD, k, v).astype(bf16)


def pack_heads(projected, cosine, sine, seq, rows, n):
    qw = H * HD // n
    copies = n // KV
    k_at = H * HD // LANES
    v_at = k_at + KV * HD // LANES
    table = pl.BlockSpec((rows, LANES), lambda d: (seq, 0))
    return pl.pallas_call(
        functools.partial(pack_kernel, copies),
        grid=(n,),
        in_specs=[
            pl.BlockSpec((rows, qw), lambda d: (seq, d)),
            pl.BlockSpec((rows, LANES), lambda d: (seq, k_at + d // copies // 2)),
            pl.BlockSpec((rows, LANES), lambda d: (seq, v_at + d // copies // 2)),
            table,
            table,
        ],
        out_specs=pl.BlockSpec((1, rows, qw + 2 * HD), lambda d: (d, 0, 0)),
        out_shape=jax.ShapeDtypeStruct((n, rows, qw + 2 * HD), bf16),
        cost_estimate=pl.CostEstimate(flops=0, bytes_accessed=6 << 20, transcendentals=0),
        name="pack_heads",
    )(projected, projected, projected, cosine, sine)


def unpack_kernel(n, in_ref, cos_ref, sin_ref, out_ref):
    qw = in_ref.shape[2] - 2 * HD
    copies = n // KV
    cosine = cos_ref[...]
    sine = -sin_ref[...]
    lane = lax.broadcasted_iota(jnp.int32, cosine.shape, 1)
    for d in range(n):
        part = in_ref[d, :, :qw].astype(f32)
        out_ref[:, d * qw : (d + 1) * qw] = rotate_lanes(part, cosine, sine).astype(bf16)
    for pair in range(KV // 2):
        sums = []
        for head in (2 * pair, 2 * pair + 1):
            slots = [in_ref[head * copies + c, :, qw:].astype(f32) for c in range(copies)]
            sums.append(sum(slots[1:], slots[0]))
        k = jnp.where(lane < HD, sums[0], pltpu.roll(sums[1], HD, 1))
        v = jnp.where(lane < HD, pltpu.roll(sums[0], HD, 1), sums[1])
        k_at = H * HD + pair * LANES
        v_at = k_at + KV * HD
        out_ref[:, k_at : k_at + LANES] = rotate_lanes(k, cosine, sine).astype(bf16)
        out_ref[:, v_at : v_at + LANES] = v.astype(bf16)


def unpack_heads(pieces, cosine, sine):
    n, rows, w = pieces.shape
    cols = H * HD + 2 * KV * HD
    return pl.pallas_call(
        functools.partial(unpack_kernel, n),
        out_shape=jax.ShapeDtypeStruct((rows, cols), bf16),
        in_specs=[pl.BlockSpec(memory_space=pltpu.VMEM)] * 3,
        out_specs=pl.BlockSpec(memory_space=pltpu.VMEM),
        compiler_params=pltpu.CompilerParams(vmem_limit_bytes=32 << 20),
        cost_estimate=pl.CostEstimate(flops=0, bytes_accessed=4 << 20, transcendentals=0),
        name="unpack_heads",
    )(pieces, cosine, sine)


def interleave_kernel(core_ref, own_ref, other_ref, out_ref):
    del core_ref
    for i, ref in enumerate((own_ref, other_ref)):

        @pl.when(pl.program_id(2) == i)
        def _():
            out_ref[0, 0, 0] = ref[0, :, 0]


def interleave(core, own, other):
    nx, ny, inner, sub, cols = own.shape
    spec = pl.BlockSpec((1, ny, 1, sub, cols), lambda x, k, i, core_ref: (x, 0, k, 0, 0))
    return pl.pallas_call(
        interleave_kernel,
        grid_spec=pltpu.PrefetchScalarGridSpec(
            num_scalar_prefetch=1,
            grid=(nx, inner, 2),
            in_specs=[spec, spec],
            out_specs=pl.BlockSpec(
                (1, 1, 1, ny, sub, cols), lambda x, k, i, core_ref: (x, core_ref[0] ^ i, k, 0, 0, 0)
            ),
        ),
        out_shape=jax.ShapeDtypeStruct((nx, 2, inner, ny, sub, cols), own.dtype),
        compiler_params=pltpu.CompilerParams(vmem_limit_bytes=48 << 20),
        cost_estimate=pl.CostEstimate(flops=0, bytes_accessed=1 << 16, transcendentals=0),
        name="interleave",
    )(core, own, other)


ROW_TILE = 256


def small_cost(size):
    return pl.CostEstimate(flops=0, bytes_accessed=size, transcendentals=0)


def resident(shape, index):
    return pl.BlockSpec(shape, lambda i: index, pipeline_mode=pl.Buffered(1))


def by_rows(tile, cols, at=0):
    return pl.BlockSpec((tile, cols), lambda i: (i, at))


def load_rows(w_ref, w_s, sems):
    xy, _, nfar, _, sub, _ = w_ref.shape
    ny = 2
    copies = []
    for g in range(xy):
        for core in range(2):
            for far in range(nfar):
                for near in range(2):
                    block = (((g // ny * 2 + core) * nfar + far) * 2 + near) * ny + g % ny
                    copies.append(
                        pltpu.make_async_copy(
                            w_ref.at[g, core, far, near],
                            w_s.at[pl.ds(block * sub, sub)],
                            sems.at[block],
                        )
                    )
    for copy in copies:
        copy.start()
    for copy in copies:
        copy.wait()


def with_weights(kernel):
    def run(x_ref, w_ref, *refs):
        *refs, w_s, sems = refs

        @pl.when(pl.program_id(0) == 0)
        def _():
            load_rows(w_ref, w_s, sems)

        kernel(x_ref, w_s, *refs)

    return run


def over_rows(kernel, x, w, others, outs, name):
    m = x.shape[0]
    blocks = w.shape[0] * w.shape[1] * w.shape[2] * w.shape[3]
    tile = min(ROW_TILE, m)
    return pl.pallas_call(
        with_weights(kernel),
        grid=(m // tile,),
        in_specs=[by_rows(tile, x.shape[1]), pl.BlockSpec(memory_space=pl.ANY)]
        + [by_rows(tile, other.shape[1]) for other in others],
        out_specs=[by_rows(tile, cols) for cols, _ in outs],
        out_shape=[jax.ShapeDtypeStruct((m, cols), t) for cols, t in outs],
        scratch_shapes=[
            pltpu.VMEM((blocks * w.shape[4], w.shape[5]), bf16),
            pltpu.SemaphoreType.DMA((blocks,)),
        ],
        compiler_params=pltpu.CompilerParams(vmem_limit_bytes=48 << 20),
        cost_estimate=small_cost(1 << 16),
        name=name,
    )(x, w, *others)


def ffn_forward_kernel(x_ref, w_ref, gate_ref, up_ref, active_ref):
    units = gate_ref.shape[1]
    x = x_ref[...]
    gate = dot(x, w_ref[:, :units])
    gate_ref[...] = gate
    up = dot(x, w_ref[:, units:])
    up_ref[...] = up
    active_ref[...] = (gate * jax.nn.sigmoid(gate) * up).astype(bf16)


def ffn_forward(x, w_gate_up):
    units = w_gate_up.shape[-1] // 2
    outs = [(units, f32), (units, f32), (units, bf16)]
    return over_rows(ffn_forward_kernel, x, w_gate_up, [], outs, "ffn_forward")


def ffn_backward_kernel(g_ref, w_ref, gate_ref, up_ref, both_ref):
    units = gate_ref.shape[1]
    grad_active = dot(g_ref[...], w_ref[...])
    gate = gate_ref[...]
    s = jax.nn.sigmoid(gate)
    grad_gate = grad_active * up_ref[...] * s * (1.0 + gate * (1.0 - s))
    both_ref[:, :units] = grad_gate.astype(bf16)
    both_ref[:, units:] = (grad_active * gate * s).astype(bf16)


def ffn_backward(grad, w_down, gate, up):
    outs = [(2 * gate.shape[1], bf16)]
    return over_rows(ffn_backward_kernel, grad, w_down, [gate, up], outs, "ffn_backward")[0]


def project_rows_kernel(x_ref, w_ref, out_ref):
    out_ref[...] = dot(x_ref[...], w_ref[...], ((1,), (1,))).astype(bf16)


def project_rows(x, w):
    rows = w.shape[0] * w.shape[1] * w.shape[2] * w.shape[3] * w.shape[4]
    return over_rows(project_rows_kernel, x, w, [], [(rows, bf16)], "project_rows")[0]


def rows_by_kernel(x_ref, w_ref, out_ref):
    out_ref[...] = dot(x_ref[...], w_ref[...], ((1,), (1,)))


def rows_by(x, w):
    m = x.shape[0]
    tile = min(ROW_TILE, m)
    return pl.pallas_call(
        rows_by_kernel,
        grid=(m // tile,),
        in_specs=[by_rows(tile, x.shape[1]), resident(w.shape, (0, 0))],
        out_specs=by_rows(tile, w.shape[0]),
        out_shape=jax.ShapeDtypeStruct((m, w.shape[0]), f32),
        compiler_params=pltpu.CompilerParams(vmem_limit_bytes=48 << 20),
        cost_estimate=small_cost(1 << 16),
        name="rows_by",
    )(x, w)


def outer_rows_kernel(*refs):
    total = None
    for p in range(len(refs) // 2):
        term = dot(refs[2 * p][...], refs[2 * p + 1][...], ((0,), (0,)))
        total = term if total is None else total + term
    refs[-1][...] = total.astype(bf16)


def outer_rows(pairs):
    width = pairs[0][0].shape[1]
    cols = pairs[0][1].shape[1]
    tile = min(ROW_TILE, width)
    in_specs, operands = [], []
    for a, b in pairs:
        in_specs.append(pl.BlockSpec((a.shape[0], tile), lambda i: (0, i)))
        in_specs.append(resident(b.shape, (0, 0)))
        operands += [a, b]
    return pl.pallas_call(
        outer_rows_kernel,
        grid=(width // tile,),
        in_specs=in_specs,
        out_specs=by_rows(tile, cols),
        out_shape=jax.ShapeDtypeStruct((width, cols), bf16),
        compiler_params=pltpu.CompilerParams(vmem_limit_bytes=48 << 20),
        cost_estimate=small_cost(1 << 16),
        name="outer_rows",
    )(*operands)


def outer_sum_kernel(pairs, *refs):
    out_ref = refs[-1]
    _, ny, _, nfar, _, sub, _ = out_ref.shape
    total = None
    for p in range(pairs):
        term = dot(refs[2 * p][...], refs[2 * p + 1][...], ((0,), (0,)))
        total = term if total is None else total + term
    for far in range(nfar):
        for near in range(2):
            for y in range(ny):
                at = ((far * 2 + near) * ny + y) * sub
                out_ref[0, y, 0, far, near] = total[at : at + sub].astype(bf16)


def outer_sum(pairs, cols, at, owners):
    nx, nfar, ny = owners
    width = pairs[0][0].shape[1]
    tile = width // (2 * nx)
    sub = tile // (2 * nfar * ny)
    in_specs, operands = [], []
    for a, b in pairs:
        in_specs.append(pl.BlockSpec((a.shape[0], tile), lambda i: (0, i)))
        in_specs.append(resident((b.shape[0], cols), (0, at)))
        operands += [a, b]
    return pl.pallas_call(
        functools.partial(outer_sum_kernel, len(pairs)),
        grid=(2 * nx,),
        in_specs=in_specs,
        out_specs=pl.BlockSpec(
            (1, ny, 1, nfar, 2, sub, cols), lambda i: (i // 2, 0, i % 2, 0, 0, 0, 0)
        ),
        out_shape=jax.ShapeDtypeStruct((nx, ny, 2, nfar, 2, sub, cols), bf16),
        compiler_params=pltpu.CompilerParams(vmem_limit_bytes=48 << 20),
        cost_estimate=small_cost(1 << 16),
        name="outer_sum",
    )(*operands)


def rms_scale(hidden):
    return lax.rsqrt(jnp.mean(hidden * hidden, axis=-1, keepdims=True) + EPSILON)


def rms_back(grad_scaled, scaled, inverse):
    return inverse * (grad_scaled - scaled * jnp.mean(grad_scaled * scaled, axis=-1, keepdims=True))


def exchange(pieces):
    return lax.all_to_all(pieces, SEQ, split_axis=0, concat_axis=0, tiled=True)


def local(
    tokens,
    cotangent,
    segments,
    joint_projection_matrix,
    output_weight_rows,
    gate_up_weight,
    down_weight_rows,
    attn_gain,
    ffn_gain,
):
    n = lax.axis_size(SEQ)
    me = lax.axis_index(SEQ)
    seqs, rows, width = tokens.shape
    full_len = segments.shape[1]
    heads = H // n
    qw = heads * HD
    sub = joint_projection_matrix.shape[0]
    part = FF // 4
    nx, nfar, ny = (lax.axis_size(axis) for axis in ("x", "far", "y"))
    flow = Flow()

    column = jnp.arange(full_len, dtype=jnp.int32)
    starts_here = jnp.concatenate(
        [jnp.ones((seqs, 1), dtype=bool), segments[:, 1:] != segments[:, :-1]], axis=1
    )
    doc_start = lax.cummax(jnp.where(starts_here, column, 0), axis=1)
    position = lax.dynamic_slice_in_dim(column - doc_start, me * rows, rows, 1)
    doc_start = doc_start.reshape(seqs, n, rows)
    first_block = doc_start[:, :, 0] // rows
    plain_from = jnp.minimum((doc_start[:, :, -1] + rows - 1) // rows, jnp.arange(n))
    plain_from = jnp.maximum(plain_from, first_block)
    doc_start = doc_start[:, :, None, :]
    frequency = ROTARY_BASE ** (-(jnp.arange(HD // 2, dtype=f32) * 2.0) / HD)
    angles = position.astype(f32).reshape(seqs * rows, 1) * frequency
    cosine = jnp.concatenate([jnp.cos(angles)] * 4, axis=1)
    sine = jnp.concatenate([-jnp.sin(angles), jnp.sin(angles)] * 2, axis=1)

    hidden_all = tokens.reshape(seqs * rows, width).astype(f32)
    grad_out_all = cotangent.reshape(seqs * rows, width)
    gain_one = attn_gain.astype(f32)
    gain_two = ffn_gain.astype(f32)

    def own_rows(weight):
        gathered = lax.all_gather(weight, ("x",) + SEQ, axis=0, tiled=True)
        return gathered.reshape(nx, -1, weight.shape[1])

    def core_features(values):
        w = width // (2 * nx)
        bit = my_bit(CORE)
        return tuple(
            jnp.concatenate(
                [lax.dynamic_slice_in_dim(values, (2 * i + c) * w, w, 1) for i in range(nx)], axis=1
            )
            for c in (bit, 1 - bit)
        )

    def flat(values):
        return values.reshape(-1, values.shape[-1])

    def lane_halves(values, key):
        w = values.shape[-1] // 2
        bit = my_bit(key)
        return (
            lax.dynamic_slice_in_dim(values, bit * w, w, values.ndim - 1),
            lax.dynamic_slice_in_dim(values, (1 - bit) * w, w, values.ndim - 1),
        )

    def lanes_by_bit(mine, other, key):
        low = my_bit(key) == 0
        return [jnp.where(low, mine, other), jnp.where(low, other, mine)]

    class Group:
        def __init__(self, values):
            self.values, self.core = values, swap(values, CORE)
            self.arrived = swap(values, NEAR)

        def done(self):
            near = self.arrived
            return jnp.concatenate([self.values, self.core, near, swap(near, CORE)], axis=0)

    class GroupSum:
        def __init__(self, partial):
            self.mine = partial.reshape(2, 2, rows, -1)
            self.arrived = swap(self.mine[:, 1], CORE)

        def next(self):
            both = self.mine[:, 0].astype(f32) + self.arrived.astype(f32)
            self.mine = both[0]
            self.arrived = swap(both[1].astype(bf16), NEAR)

        def done(self):
            return self.mine + self.arrived.astype(f32)

    qkv = Gather(joint_projection_matrix, "near", 0)
    out = Gather(output_weight_rows, "far", 0)
    flow.close(flow.token, wait=[qkv])

    qkv = Gather(qkv.done(), "far", 0)
    near_parts, near_swaps = [], []
    for weight in (gate_up_weight[:, :FF], gate_up_weight[:, FF:], down_weight_rows):
        mine, other = lane_halves(weight, NEAR)
        near_parts.append(mine)
        near_swaps.append(other)
    near_swap = Swap(flow.open(jnp.stack(near_swaps)), NEAR)
    inverse_one = rms_scale(hidden_all)
    scaled_one = hidden_all * inverse_one
    normed_one = (scaled_one * gain_one).astype(bf16)
    normed_one_own, normed_one_other = core_features(normed_one)
    normed_one_own, normed_one_other, cosine, sine = flow.close(
        normed_one_own, normed_one_other, cosine, sine, wait=[qkv, near_swap, out]
    )

    left, right = jnp.split(qkv.done(), 2, axis=-1)
    left = Gather(left, "y", 2)
    right = Gather(right, "x", 0)
    core_parts, core_swaps = [], []
    for mine, arrived in zip(near_parts, near_swap.arrived):
        mine, other = lane_halves(by_bit(mine, arrived, NEAR, 0), CORE)
        core_parts.append(mine)
        core_swaps.append(other)
    core_swap = Swap(jnp.stack(core_swaps), CORE)
    out = Gather(out.done(), "near", 1)
    flow.close(flow.token, wait=[left, right, core_swap, out])

    def over_xy(values):
        gathered = lax.all_gather(flat(values), ("x", "y"), axis=0, tiled=True)
        return gathered.reshape((nx * ny,) + values.shape)

    left = Gather(left.done(), "x", 0)
    right = Gather(right.done(), "y", 3)
    gate, up, down = (
        by_bit(mine, arrived, CORE, 0) for mine, arrived in zip(core_parts, core_swap.arrived)
    )
    gate = Gather(gate, "far", 1)
    w_out_own = over_xy(out.done())
    grad_group_0 = Group(flow.open(grad_out_all[:rows]))
    up, down = flow.close(up, down, wait=[left, right, gate, grad_group_0])

    w_own = jnp.concatenate([flat(left.done()), flat(right.done())], axis=1)
    w_swap = Swap(w_own, CORE)
    up = Gather(up, "far", 1)
    grad_group_1 = Group(flow.open(grad_out_all[rows:]))
    projected = dot(normed_one_own, w_own)
    w_other = w_swap.arrived
    projected = projected + dot(normed_one_other, w_other)
    packed_0 = pack_heads(projected, cosine, sine, 0, rows, n)
    packed_0 = flow.close(packed_0, wait=[up, grad_group_1])

    def attend_one(b, qkv_b):
        return attend(first_block[b], plain_from[b], doc_start[b], qkv_b, heads)

    packed_0, projected, w_other = flow.open(packed_0, projected, w_other)
    qkv_0 = exchange(packed_0)
    w_gate_up = over_xy(jnp.concatenate([gate.done(), up.done()], axis=-1))
    packed_1 = pack_heads(projected, cosine, sine, 1, rows, n)
    core_arg = lax.axis_index("core").astype(jnp.int32).reshape(1)
    w_shape = (nx, 1, nfar * 2, -1, w_own.shape[1])
    w_qkv = flat(interleave(core_arg, w_own.reshape(w_shape), w_other.reshape(w_shape)))
    qkv_0, packed_1, w_qkv = flow.close(qkv_0, packed_1, w_qkv)

    qkv_0, packed_1 = flow.open(qkv_0, packed_1)
    qkv_1 = exchange(packed_1)
    attended_0, raw_0, lse_0 = attend_one(0, qkv_0)
    attended_0, qkv_1, w_out_own = flow.close(attended_0, qkv_1, w_out_own)

    attended_0, qkv_1 = flow.open(attended_0, qkv_1)
    back_0 = exchange(attended_0)
    out_swap = Swap(w_out_own, CORE)
    attended_1, raw_1, lse_1 = attend_one(1, qkv_1)
    attended_1, back_0 = flow.close(attended_1, back_0, wait=[out_swap])

    def after_attention(b, back):
        attended = jnp.concatenate([back[s] for s in range(n)], axis=1)
        hidden = flow.open(tokens[b]).astype(f32)
        middle = hidden + dot(attended, w_out, ((1,), (1,)))
        inverse = rms_scale(middle)
        scaled = middle * inverse
        return attended, middle, inverse, scaled, (scaled * gain_two).astype(bf16)

    attended_1, back_0 = flow.open(attended_1, back_0)
    back_1 = exchange(attended_1)
    w_shape = (nx, ny, nfar * 2, sub, width)
    w_out = interleave(core_arg, w_out_own.reshape(w_shape), out_swap.arrived.reshape(w_shape))
    w_out = flat(w_out)
    down = Gather(flow.open(down), "far", 1)
    attended_0, middle_0, inverse_0, scaled_0, normed_0 = after_attention(0, back_0)
    back_1, normed_0 = flow.close(back_1, normed_0)

    back_1, normed_0 = flow.open(back_1, normed_0)
    group_0 = Group(normed_0)
    attended_1, middle_1, inverse_1, scaled_1, normed_1 = after_attention(1, back_1)
    normed_1, w_gate_up = flow.close(normed_1, w_gate_up, wait=[group_0, down])
    w_down = over_xy(down.done())
    group_1 = Group(normed_1)
    group_0 = group_0.done()

    gate_0, up_0, active_0 = ffn_forward(group_0, w_gate_up)
    grad_group_0 = grad_group_0.done()
    grad_group_1 = grad_group_1.done()
    active_0 = flow.close(active_0, wait=[group_1])

    group_1 = group_1.done()
    gate_1, up_1, active_1 = ffn_forward(flow.open(group_1), w_gate_up)
    active_1 = flow.close(active_1)

    outer = lambda a, b: dot(a, b, ((0,), (0,)))
    owners = (nx, nfar, ny)

    def sum_to_owners(terms):
        rest = terms.shape[2:]
        terms = terms.reshape(-1, terms.shape[-1])
        total = lax.psum_scatter(terms, ("x", "y"), scatter_dimension=0, tiled=True)
        return total.reshape(rest)

    d_down = outer_sum(
        [(grad_group_0, active_0), (grad_group_1, flow.open(active_1))], part, 0, owners
    )
    d_down = flow.close(d_down)

    d_down = sum_to_owners(flow.open(d_down))
    both_0 = ffn_backward(flow.open(grad_group_0), w_down, gate_0, up_0)
    terms_0 = flow.close(project_rows(both_0, w_gate_up))

    grad_normed_0 = GroupSum(terms_0)
    partial_0 = project_rows(flow.open(active_0), w_down)
    partial_0 = flow.close(partial_0, wait=[grad_normed_0])
    grad_normed_0.next()
    result_0 = GroupSum(partial_0)
    both_1 = ffn_backward(flow.open(grad_group_1), w_down, gate_1, up_1)
    terms_1 = project_rows(both_1, w_gate_up)
    terms_1 = flow.close(terms_1, wait=[grad_normed_0, result_0])

    def before_attention(b, g, scaled, inverse):
        grad_middle = grad_out_all[b * rows : (b + 1) * rows].astype(f32) + rms_back(
            g * gain_two, scaled, inverse
        )
        grad_branch = grad_middle.astype(bf16)
        grad_attended = dot(grad_branch, w_out).astype(bf16)
        grad_heads = [grad_attended[:, d * qw : (d + 1) * qw] for d in range(n)]
        return grad_middle, grad_branch, jnp.stack(grad_heads)

    grad_normed_1 = GroupSum(terms_1)
    grad_normed_0 = grad_normed_0.done()
    grad_middle_0, grad_branch_0, grad_heads_0 = before_attention(
        0, grad_normed_0, scaled_0, inverse_0
    )
    grad_heads_0 = flow.close(grad_heads_0, wait=[grad_normed_1])

    grad_normed_1.next()
    grad_heads_0 = exchange(grad_heads_0)
    d_up = outer_sum([(flow.open(group_0), both_0), (group_1, both_1)], part, 1, owners)
    d_up = flow.close(d_up, wait=[grad_normed_1])

    d_up = sum_to_owners(flow.open(d_up))
    d_gate = outer_sum([(flow.open(group_0), both_0), (group_1, both_1)], part, 0, owners)
    d_gate, grad_heads_0 = flow.close(d_gate, grad_heads_0)

    d_gate = sum_to_owners(flow.open(d_gate))
    grad_normed_1 = grad_normed_1.done()
    grad_middle_1, grad_branch_1, grad_heads_1 = before_attention(
        1, grad_normed_1, scaled_1, inverse_1
    )
    grad_heads_1 = flow.close(grad_heads_1)

    grad_heads_1 = exchange(grad_heads_1)
    grad_branch = jnp.concatenate([grad_branch_0, grad_branch_1], axis=0)
    attended = jnp.concatenate([attended_0, attended_1], axis=0)
    d_out = outer(flow.open(grad_branch), attended).astype(bf16)
    d_out = flow.close(d_out.reshape((nx, 2, -1, attended.shape[1])))

    def core_sum(mine, send):
        total = mine.astype(f32) + swap(send.astype(bf16), CORE).astype(f32)
        total = total.astype(bf16).reshape((nx, nfar, 2, ny, sub, total.shape[-1]))
        return total.transpose((0, 3, 1, 2, 4, 5))

    def attend_back_one(b, qkv_b, grad_b, raw_b, lse_b):
        dq, dkv = attend_back(
            first_block[b], plain_from[b], doc_start[b], qkv_b, grad_b, raw_b, lse_b, heads
        )
        return jnp.concatenate([dq, dkv], axis=2)

    d_out = sum_to_owners(core_sum(*choose(d_out, CORE, 1)))
    back_0 = attend_back_one(0, qkv_0, flow.open(grad_heads_0), raw_0, lse_0)
    d_down = Scatter(flow.open(d_down), "far", 1)
    result_0.next()
    back_0, grad_heads_1 = flow.close(back_0, grad_heads_1, wait=[d_down, result_0])

    back_0 = exchange(back_0)
    back_1 = attend_back_one(1, qkv_1, flow.open(grad_heads_1), raw_1, lse_1)
    back_1, back_0 = flow.close(back_1, back_0)

    back_1 = exchange(back_1)
    partial_1 = project_rows(flow.open(active_1), w_down)
    grad_proj_0 = unpack_heads(flow.open(back_0), cosine[:rows], sine[:rows])
    d_up = Scatter(flow.open(d_up), "far", 1)
    back_1, grad_proj_0, partial_1 = flow.close(back_1, grad_proj_0, partial_1, wait=[d_up])

    d_gate = Scatter(flow.open(d_gate), "far", 1)
    result_1 = GroupSum(partial_1)
    grad_proj_1 = unpack_heads(back_1, cosine[rows:], sine[rows:])
    grad_proj = jnp.concatenate([grad_proj_0, grad_proj_1], axis=0)
    core_back = outer_rows(
        [(normed_one_other[:rows], grad_proj_0), (normed_one_other[rows:], grad_proj_1)]
    )
    core_back = Swap(core_back, CORE)
    grad_normed_one = rows_by(grad_proj, w_qkv)
    grad_proj, grad_normed_one = flow.close(
        grad_proj, grad_normed_one, wait=[core_back, result_1, d_gate]
    )
    d_qkv = outer(normed_one_own, grad_proj) + core_back.arrived.astype(f32)
    d_qkv = d_qkv.astype(bf16).reshape((nx, nfar, 2, ny, sub, -1))
    left, right = flow.close(*jnp.split(d_qkv, 2, axis=-1))

    left = Scatter(left, "x", 0)
    right = Scatter(right, "y", 3)
    result_1.next()
    d_out = Scatter(flow.open(d_out), "far", 0)
    ffn = jnp.stack([t.done(last=True) for t in (d_gate, d_up, d_down)])
    mine, send = choose(ffn, NEAR, 2)
    near_back = Swap(send.astype(bf16), NEAR)
    flow.close(flow.token, wait=[left, right])

    left = Scatter(left.done(), "y", 2)
    right = Scatter(right.done(), "x", 0)
    attn_gain_grad = jnp.sum(grad_normed_one * scaled_one, axis=0)
    late_0, late_1 = flow.open(grad_normed_0, grad_normed_1)
    ffn_gain_grad = jnp.sum(late_0 * scaled_0, axis=0) + jnp.sum(late_1 * scaled_1, axis=0)
    gains = jnp.stack([attn_gain_grad, ffn_gain_grad])
    gains, grad_normed_one = flow.close(gains, grad_normed_one, wait=[left, right, near_back])

    d_qkv = Scatter(jnp.concatenate([left.done(), right.done()], axis=-1), "far", 0)
    gains = sum_axes(gains, "x", "y", "core")
    quarters = []
    for part_of in lanes_by_bit(mine, near_back.arrived.astype(f32), NEAR):
        part_mine, part_send = choose(part_of, CORE, 1)
        quarters += lanes_by_bit(part_mine, swap(part_send.astype(bf16), CORE).astype(f32), CORE)
    d_gate_up = jnp.concatenate([q[k] for k in (0, 1) for q in quarters], axis=1)
    d_down = jnp.concatenate([q[2] for q in quarters], axis=1)
    grad_input = jnp.concatenate([grad_middle_0, grad_middle_1], axis=0) + rms_back(
        grad_normed_one * gain_one, scaled_one, inverse_one
    )
    grad_input, gains, d_gate_up, d_down = flow.close(
        grad_input, gains, d_gate_up, d_down, wait=[d_qkv, d_out, result_1]
    )

    d_qkv = Scatter(d_qkv.done(), "near", 0)
    d_out = Scatter(d_out.done(), "near", 0)
    gains = sum_axes(gains, "near", "far")
    result = jnp.concatenate([middle_0 + result_0.done(), middle_1 + result_1.done()], axis=0)
    return (
        result.astype(bf16).reshape(tokens.shape),
        grad_input.reshape(tokens.shape),
        d_qkv.done(last=True),
        d_out.done(last=True),
        d_gate_up,
        d_down,
        gains[0],
        gains[1],
    )


def solution(mesh):
    dp, seq = mesh.devices.shape
    shape = (dp // 2, 2, seq // 4, 2, 2)
    fine = Mesh(mesh.devices.reshape(shape), ("x", "core") + SEQ)
    by_token = P(("x", "core"), SEQ, None)
    by_row = P(("x", "core") + SEQ, None)
    return jax.shard_map(
        local,
        mesh=fine,
        in_specs=(
            by_token,
            by_token,
            P(("x", "core"), None),
            by_row,
            by_row,
            by_row,
            by_row,
            P(),
            P(),
        ),
        out_specs=(by_token, by_token, by_row, by_row, by_row, by_row, P(), P()),
        check_vma=False,
    )
```

```python
import functools
import math

import jax
import jax.numpy as jnp
from jax import lax
from jax.experimental import pallas as pl
from jax.experimental.pallas import tpu as pltpu
from jax.sharding import Mesh
from jax.sharding import PartitionSpec as P

H = 32
HD = 64
KV = 4
FF = 5632

EPSILON = 1e-05
NEG = -1e30
ROTARY_BASE = 10000.0
LOG2E = math.log2(math.e)
LANES = 128

bf16 = jnp.bfloat16
f32 = jnp.float32


def dot(a, b, dims=((1,), (0,))):
    return lax.dot_general(a, b, (dims, ((), ())), preferred_element_type=f32)


CORE = ("core", 0)
NEAR = ("near", 0)
SEQ = ("far", "near", "y")


def axis_bits(axis):
    return [(axis, b) for b in reversed(range((lax.axis_size(axis) - 1).bit_length()))]


def my_bit(key):
    axis, b = key
    return (lax.axis_index(axis) >> b) & 1


def swap(values, key):
    axis, b = key
    return lax.ppermute(values, axis, [(i, i ^ (1 << b)) for i in range(lax.axis_size(axis))])


class Flow:
    def __init__(self):
        self.token = jnp.zeros((), f32)

    def open(self, *values):
        opened = lax.optimization_barrier(values + (self.token,))[:-1]
        return opened if len(values) > 1 else opened[0]

    def close(self, *values, wait=()):
        arrived = tuple(transfer.arrived for transfer in wait)
        closed = lax.optimization_barrier(values + arrived + (self.token,))
        for transfer, value in zip(wait, closed[len(values) :]):
            transfer.arrived = value
        self.token = closed[-1]
        return closed[: len(values)] if len(values) > 1 else closed[0]


def choose(values, key, axis):
    bit = my_bit(key)
    return (
        lax.dynamic_index_in_dim(values, bit, axis, keepdims=False),
        lax.dynamic_index_in_dim(values, 1 - bit, axis, keepdims=False),
    )


def by_bit(mine, other, key, axis):
    low = my_bit(key) == 0
    return jnp.stack([jnp.where(low, mine, other), jnp.where(low, other, mine)], axis=axis)


class Swap:
    def __init__(self, values, key):
        self.arrived = swap(values, key)


class Gather:
    def __init__(self, values, axis, at):
        self.values, self.axis, self.at = values, axis, at
        self.arrived = swap(values, axis_bits(axis)[0])

    def done(self):
        values, other, shape = self.values, self.arrived, self.values.shape
        for step, key in enumerate(axis_bits(self.axis)):
            if step:
                other = swap(values, key)
            values = by_bit(values, other, key, self.at + step)
        return values.reshape(shape[: self.at] + (lax.axis_size(self.axis),) + shape[self.at :])


class Scatter:
    def __init__(self, values, axis, at):
        self.keys, self.at = axis_bits(axis), at
        shape = values.shape
        values = values.reshape(shape[:at] + (2,) * len(self.keys) + shape[at + 1 :])
        self.start(values)

    def start(self, values):
        self.mine, send = choose(values, self.keys[0], self.at)
        self.arrived = swap(send.astype(bf16), self.keys[0])

    def done(self, last=False):
        while True:
            values = self.mine.astype(f32) + self.arrived.astype(f32)
            if not last:
                values = values.astype(bf16)
            self.keys = self.keys[1:]
            if not self.keys:
                return values
            self.start(values)


def sum_axes(values, *axes):
    for axis in axes:
        for key in axis_bits(axis):
            values = values + swap(values, key)
    return values


def stack_heads(x, heads):
    return jnp.concatenate([x[:, h * HD : (h + 1) * HD] for h in range(heads)], axis=0)


def unstack_heads(x, heads):
    rows = x.shape[0] // heads
    return jnp.concatenate([x[h * rows : (h + 1) * rows] for h in range(heads)], axis=1)


def block_allowed(i, j, rows, start):
    key_pos = j * rows + lax.broadcasted_iota(jnp.int32, (rows, rows), 0)
    query_pos = i * rows + lax.broadcasted_iota(jnp.int32, (rows, rows), 1)
    return (key_pos <= query_pos) & (key_pos >= start)


def attend_kernel(
    heads, lo_ref, hi_ref, start_ref, qkv_ref, out_ref, raw_ref, lse_ref, m_s, l_s, acc_s
):
    rows = qkv_ref.shape[1]
    qw = heads * HD
    scale = LOG2E * HD**-0.5
    i = pl.program_id(0)
    q = stack_heads(qkv_ref[i, :, :qw], heads)
    m_s[...] = jnp.full_like(m_s, NEG)
    l_s[...] = jnp.zeros_like(l_s)
    acc_s[...] = jnp.zeros_like(acc_s)

    def block(j, masked):
        k = qkv_ref[j, :, qw : qw + HD]
        v = qkv_ref[j, :, qw + HD : qw + 2 * HD]
        s = dot(k, q, ((1,), (1,)))
        if masked:
            ok = block_allowed(i, j, rows, start_ref[0])
            s = jnp.where(jnp.concatenate([ok] * heads, axis=1), s, NEG)
        m_old = m_s[...]
        m_new = jnp.maximum(m_old, jnp.max(s, axis=0, keepdims=True) * scale)
        p = jnp.exp2(s * scale - m_new)
        keep = jnp.exp2(m_old - m_new)
        l_s[...] = l_s[...] * keep + jnp.sum(p, axis=0, keepdims=True)
        acc_s[...] = acc_s[...] * keep + dot(v, p.astype(bf16), ((0,), (0,)))
        m_s[...] = m_new

    def masked_step(j, carry):
        block(j, True)
        return carry

    def plain_step(j, carry):
        block(j, False)
        return carry

    block(i, True)
    lax.fori_loop(lo_ref[i], hi_ref[i], masked_step, 0)
    lax.fori_loop(hi_ref[i], i, plain_step, 0)
    total = l_s[...]
    result = unstack_heads(jnp.transpose(acc_s[...] / total), heads)
    raw_ref[0] = result
    out_ref[0] = result.astype(bf16)
    lse_ref[0] = jnp.broadcast_to(m_s[...] + jnp.log2(total), (8, heads * rows))


def attend(lo, hi, start, qkv, heads):
    n, rows, w = qkv.shape
    qw = heads * HD
    smem = pl.BlockSpec(memory_space=pltpu.SMEM)
    pairs = heads * (n * rows) ** 2 // 2
    per_block = lambda shape: pl.BlockSpec((1,) + shape, lambda i: (i, 0, 0))
    return pl.pallas_call(
        functools.partial(attend_kernel, heads),
        grid=(n,),
        out_shape=(
            jax.ShapeDtypeStruct((n, rows, qw), bf16),
            jax.ShapeDtypeStruct((n, rows, qw), f32),
            jax.ShapeDtypeStruct((n, 8, heads * rows), f32),
        ),
        in_specs=[
            smem,
            smem,
            per_block((1, rows)),
            pl.BlockSpec((n, rows, w), lambda i: (0, 0, 0)),
        ],
        out_specs=(per_block((rows, qw)), per_block((rows, qw)), per_block((8, heads * rows))),
        scratch_shapes=[
            pltpu.VMEM((1, heads * rows), f32),
            pltpu.VMEM((1, heads * rows), f32),
            pltpu.VMEM((HD, heads * rows), f32),
        ],
        compiler_params=pltpu.CompilerParams(vmem_limit_bytes=48 << 20),
        cost_estimate=pl.CostEstimate(flops=0, bytes_accessed=1 << 20, transcendentals=0),
        name="attend",
    )(lo, hi, start, qkv)


def attend_back_kernel(
    heads,
    lo_ref,
    hi_ref,
    start_ref,
    qkv_ref,
    g_ref,
    raw_ref,
    lse_ref,
    dq_ref,
    dkv_ref,
    dkv_s,
    dq_s,
):
    n, rows, _ = qkv_ref.shape
    qw = heads * HD
    scale = LOG2E * HD**-0.5
    i = pl.program_id(0)

    @pl.when(i == 0)
    def _():
        dkv_s[...] = jnp.zeros_like(dkv_s)

    dq_s[...] = jnp.zeros_like(dq_s)
    q = stack_heads(qkv_ref[i, :, :qw], heads)
    g_flat = g_ref[i]
    g = stack_heads(g_flat, heads)
    product = g_flat.astype(f32) * raw_ref[0]
    inner = jnp.concatenate(
        [
            jnp.sum(product[:, h * HD : (h + 1) * HD], axis=1, keepdims=True)
            for h in range(heads)
        ],
        axis=0,
    )
    inner = jnp.transpose(jnp.broadcast_to(inner, (heads * rows, LANES)))[:1]
    lse = lse_ref[0, :1]

    def block(j, masked):
        k = qkv_ref[j, :, qw : qw + HD]
        v = qkv_ref[j, :, qw + HD : qw + 2 * HD]
        s = dot(k, q, ((1,), (1,)))
        grad_probs = dot(v, g, ((1,), (1,)))
        p = jnp.exp2(s * scale - lse)
        if masked:
            ok = block_allowed(i, j, rows, start_ref[0])
            p = jnp.where(jnp.concatenate([ok] * heads, axis=1), p, 0.0)
        grad_scores = (p * (grad_probs - inner)).astype(bf16)
        dkv_s[j, :, :HD] += dot(grad_scores, q)
        dkv_s[j, :, HD:] += dot(p.astype(bf16), g)
        dq_s[...] += dot(k, grad_scores, ((0,), (0,)))

    def masked_step(j, carry):
        block(j, True)
        return carry

    def plain_step(j, carry):
        block(j, False)
        return carry

    lax.fori_loop(lo_ref[i], hi_ref[i], masked_step, 0)
    lax.fori_loop(hi_ref[i], i, plain_step, 0)
    block(i, True)
    dq = unstack_heads(jnp.transpose(dq_s[...] * HD**-0.5), heads)
    dq_ref[0] = dq.astype(bf16)

    @pl.when(i == n - 1)
    def _():
        for r in range(n):
            done = dkv_s[r]
            dkv_ref[r] = jnp.concatenate([done[:, :HD] * HD**-0.5, done[:, HD:]], axis=1).astype(
                bf16
            )


def attend_back(lo, hi, start, qkv, grad, raw, lse, heads):
    n, rows, w = qkv.shape
    qw = heads * HD
    smem = pl.BlockSpec(memory_space=pltpu.SMEM)
    pairs = heads * (n * rows) ** 2 // 2
    per_block = lambda shape: pl.BlockSpec((1,) + shape, lambda i: (i, 0, 0))
    whole = lambda shape: pl.BlockSpec(shape, lambda i: (0, 0, 0))
    return pl.pallas_call(
        functools.partial(attend_back_kernel, heads),
        grid=(n,),
        out_shape=(
            jax.ShapeDtypeStruct((n, rows, qw), bf16),
            jax.ShapeDtypeStruct((n, rows, 2 * HD), bf16),
        ),
        in_specs=[
            smem,
            smem,
            per_block((1, rows)),
            whole((n, rows, w)),
            whole((n, rows, qw)),
            per_block((rows, qw)),
            per_block((8, heads * rows)),
        ],
        out_specs=(per_block((rows, qw)), whole((n, rows, 2 * HD))),
        scratch_shapes=[
            pltpu.VMEM((n, rows, 2 * HD), f32),
            pltpu.VMEM((HD, heads * rows), f32),
        ],
        compiler_params=pltpu.CompilerParams(vmem_limit_bytes=48 << 20),
        cost_estimate=pl.CostEstimate(flops=0, bytes_accessed=1 << 20, transcendentals=0),
        name="attend_back",
    )(lo, hi, start, qkv, grad, raw, lse)


def rotate_lanes(v, cosine, signed_sine):
    parts = []
    for c in range(v.shape[1] // LANES):
        part = v[:, c * LANES : (c + 1) * LANES]
        lane = lax.broadcasted_iota(jnp.int32, part.shape, 1)
        other = jnp.where(
            lane % HD < HD // 2,
            pltpu.roll(part, LANES - HD // 2, 1),
            pltpu.roll(part, HD // 2, 1),
        )
        parts.append(part * cosine + other * signed_sine)
    return jnp.concatenate(parts, axis=1) if len(parts) > 1 else parts[0]


def pack_kernel(copies, q_ref, k_ref, v_ref, cos_ref, sin_ref, out_ref):
    qw = q_ref.shape[1]
    cosine = cos_ref[...]
    sine = sin_ref[...]
    out_ref[0, :, :qw] = rotate_lanes(q_ref[...], cosine, sine).astype(bf16)
    k = rotate_lanes(k_ref[...], cosine, sine)
    v = v_ref[...]
    first = (pl.program_id(0) // copies) % 2 == 0
    lane = lax.broadcasted_iota(jnp.int32, k.shape, 1)
    k = jnp.where(first, k, pltpu.roll(k, HD, 1))
    v = jnp.where(first, pltpu.roll(v, HD, 1), v)
    out_ref[0, :, qw:] = jnp.where(lane < HD, k, v).astype(bf16)


def pack_heads(projected, cosine, sine, seq, rows, n):
    qw = H * HD // n
    copies = n // KV
    k_at = H * HD // LANES
    v_at = k_at + KV * HD // LANES
    table = pl.BlockSpec((rows, LANES), lambda d: (seq, 0))
    return pl.pallas_call(
        functools.partial(pack_kernel, copies),
        grid=(n,),
        in_specs=[
            pl.BlockSpec((rows, qw), lambda d: (seq, d)),
            pl.BlockSpec((rows, LANES), lambda d: (seq, k_at + d // copies // 2)),
            pl.BlockSpec((rows, LANES), lambda d: (seq, v_at + d // copies // 2)),
            table,
            table,
        ],
        out_specs=pl.BlockSpec((1, rows, qw + 2 * HD), lambda d: (d, 0, 0)),
        out_shape=jax.ShapeDtypeStruct((n, rows, qw + 2 * HD), bf16),
        cost_estimate=pl.CostEstimate(flops=0, bytes_accessed=6 << 20, transcendentals=0),
        name="pack_heads",
    )(projected, projected, projected, cosine, sine)


def unpack_kernel(n, in_ref, cos_ref, sin_ref, out_ref):
    qw = in_ref.shape[2] - 2 * HD
    copies = n // KV
    cosine = cos_ref[...]
    sine = -sin_ref[...]
    lane = lax.broadcasted_iota(jnp.int32, cosine.shape, 1)
    for d in range(n):
        part = in_ref[d, :, :qw].astype(f32)
        out_ref[:, d * qw : (d + 1) * qw] = rotate_lanes(part, cosine, sine).astype(bf16)
    for pair in range(KV // 2):
        sums = []
        for head in (2 * pair, 2 * pair + 1):
            slots = [in_ref[head * copies + c, :, qw:].astype(f32) for c in range(copies)]
            sums.append(sum(slots[1:], slots[0]))
        k = jnp.where(lane < HD, sums[0], pltpu.roll(sums[1], HD, 1))
        v = jnp.where(lane < HD, pltpu.roll(sums[0], HD, 1), sums[1])
        k_at = H * HD + pair * LANES
        v_at = k_at + KV * HD
        out_ref[:, k_at : k_at + LANES] = rotate_lanes(k, cosine, sine).astype(bf16)
        out_ref[:, v_at : v_at + LANES] = v.astype(bf16)


def unpack_heads(pieces, cosine, sine):
    n, rows, w = pieces.shape
    cols = H * HD + 2 * KV * HD
    return pl.pallas_call(
        functools.partial(unpack_kernel, n),
        out_shape=jax.ShapeDtypeStruct((rows, cols), bf16),
        in_specs=[pl.BlockSpec(memory_space=pltpu.VMEM)] * 3,
        out_specs=pl.BlockSpec(memory_space=pltpu.VMEM),
        compiler_params=pltpu.CompilerParams(vmem_limit_bytes=32 << 20),
        cost_estimate=pl.CostEstimate(flops=0, bytes_accessed=4 << 20, transcendentals=0),
        name="unpack_heads",
    )(pieces, cosine, sine)


def interleave_kernel(core_ref, own_ref, other_ref, out_ref):
    del core_ref
    for i, ref in enumerate((own_ref, other_ref)):

        @pl.when(pl.program_id(2) == i)
        def _():
            out_ref[0, 0, 0] = ref[0, :, 0]


def interleave(core, own, other):
    nx, ny, inner, sub, cols = own.shape
    spec = pl.BlockSpec((1, ny, 1, sub, cols), lambda x, k, i, core_ref: (x, 0, k, 0, 0))
    return pl.pallas_call(
        interleave_kernel,
        grid_spec=pltpu.PrefetchScalarGridSpec(
            num_scalar_prefetch=1,
            grid=(nx, inner, 2),
            in_specs=[spec, spec],
            out_specs=pl.BlockSpec(
                (1, 1, 1, ny, sub, cols), lambda x, k, i, core_ref: (x, core_ref[0] ^ i, k, 0, 0, 0)
            ),
        ),
        out_shape=jax.ShapeDtypeStruct((nx, 2, inner, ny, sub, cols), own.dtype),
        compiler_params=pltpu.CompilerParams(vmem_limit_bytes=48 << 20),
        cost_estimate=pl.CostEstimate(flops=0, bytes_accessed=1 << 16, transcendentals=0),
        name="interleave",
    )(core, own, other)


ROW_TILE = 256


def small_cost(size):
    return pl.CostEstimate(flops=0, bytes_accessed=size, transcendentals=0)


def resident(shape, index):
    return pl.BlockSpec(shape, lambda i: index, pipeline_mode=pl.Buffered(1))


def by_rows(tile, cols, at=0):
    return pl.BlockSpec((tile, cols), lambda i: (i, at))


def load_rows(w_ref, w_s, sems):
    xy, _, nfar, _, sub, _ = w_ref.shape
    ny = 2
    copies = []
    for g in range(xy):
        for core in range(2):
            for far in range(nfar):
                for near in range(2):
                    block = (((g // ny * 2 + core) * nfar + far) * 2 + near) * ny + g % ny
                    copies.append(
                        pltpu.make_async_copy(
                            w_ref.at[g, core, far, near],
                            w_s.at[pl.ds(block * sub, sub)],
                            sems.at[block],
                        )
                    )
    for copy in copies:
        copy.start()
    for copy in copies:
        copy.wait()


def with_weights(kernel):
    def run(x_ref, w_ref, *refs):
        *refs, w_s, sems = refs

        @pl.when(pl.program_id(0) == 0)
        def _():
            load_rows(w_ref, w_s, sems)

        kernel(x_ref, w_s, *refs)

    return run


def over_rows(kernel, x, w, others, outs, name):
    m = x.shape[0]
    blocks = w.shape[0] * w.shape[1] * w.shape[2] * w.shape[3]
    tile = min(ROW_TILE, m)
    return pl.pallas_call(
        with_weights(kernel),
        grid=(m // tile,),
        in_specs=[by_rows(tile, x.shape[1]), pl.BlockSpec(memory_space=pl.ANY)]
        + [by_rows(tile, other.shape[1]) for other in others],
        out_specs=[by_rows(tile, cols) for cols, _ in outs],
        out_shape=[jax.ShapeDtypeStruct((m, cols), t) for cols, t in outs],
        scratch_shapes=[
            pltpu.VMEM((blocks * w.shape[4], w.shape[5]), bf16),
            pltpu.SemaphoreType.DMA((blocks,)),
        ],
        compiler_params=pltpu.CompilerParams(vmem_limit_bytes=48 << 20),
        cost_estimate=small_cost(1 << 16),
        name=name,
    )(x, w, *others)


def ffn_forward_kernel(x_ref, w_ref, gate_ref, up_ref, active_ref):
    units = gate_ref.shape[1]
    x = x_ref[...]
    gate = dot(x, w_ref[:, :units])
    gate_ref[...] = gate
    up = dot(x, w_ref[:, units:])
    up_ref[...] = up
    active_ref[...] = (gate * jax.nn.sigmoid(gate) * up).astype(bf16)


def ffn_forward(x, w_gate_up):
    units = w_gate_up.shape[-1] // 2
    outs = [(units, f32), (units, f32), (units, bf16)]
    return over_rows(ffn_forward_kernel, x, w_gate_up, [], outs, "ffn_forward")


def ffn_backward_kernel(g_ref, w_ref, gate_ref, up_ref, both_ref):
    units = gate_ref.shape[1]
    grad_active = dot(g_ref[...], w_ref[...])
    gate = gate_ref[...]
    s = jax.nn.sigmoid(gate)
    grad_gate = grad_active * up_ref[...] * s * (1.0 + gate * (1.0 - s))
    both_ref[:, :units] = grad_gate.astype(bf16)
    both_ref[:, units:] = (grad_active * gate * s).astype(bf16)


def ffn_backward(grad, w_down, gate, up):
    outs = [(2 * gate.shape[1], bf16)]
    return over_rows(ffn_backward_kernel, grad, w_down, [gate, up], outs, "ffn_backward")[0]


def project_rows_kernel(x_ref, w_ref, out_ref):
    out_ref[...] = dot(x_ref[...], w_ref[...], ((1,), (1,))).astype(bf16)


def project_rows(x, w):
    rows = w.shape[0] * w.shape[1] * w.shape[2] * w.shape[3] * w.shape[4]
    return over_rows(project_rows_kernel, x, w, [], [(rows, bf16)], "project_rows")[0]


def rows_by_kernel(x_ref, w_ref, out_ref):
    out_ref[...] = dot(x_ref[...], w_ref[...], ((1,), (1,)))


def rows_by(x, w):
    m = x.shape[0]
    tile = min(ROW_TILE, m)
    return pl.pallas_call(
        rows_by_kernel,
        grid=(m // tile,),
        in_specs=[by_rows(tile, x.shape[1]), resident(w.shape, (0, 0))],
        out_specs=by_rows(tile, w.shape[0]),
        out_shape=jax.ShapeDtypeStruct((m, w.shape[0]), f32),
        compiler_params=pltpu.CompilerParams(vmem_limit_bytes=48 << 20),
        cost_estimate=small_cost(1 << 16),
        name="rows_by",
    )(x, w)


def outer_rows_kernel(*refs):
    total = None
    for p in range(len(refs) // 2):
        term = dot(refs[2 * p][...], refs[2 * p + 1][...], ((0,), (0,)))
        total = term if total is None else total + term
    refs[-1][...] = total.astype(bf16)


def outer_rows(pairs):
    width = pairs[0][0].shape[1]
    cols = pairs[0][1].shape[1]
    tile = min(ROW_TILE, width)
    in_specs, operands = [], []
    for a, b in pairs:
        in_specs.append(pl.BlockSpec((a.shape[0], tile), lambda i: (0, i)))
        in_specs.append(resident(b.shape, (0, 0)))
        operands += [a, b]
    return pl.pallas_call(
        outer_rows_kernel,
        grid=(width // tile,),
        in_specs=in_specs,
        out_specs=by_rows(tile, cols),
        out_shape=jax.ShapeDtypeStruct((width, cols), bf16),
        compiler_params=pltpu.CompilerParams(vmem_limit_bytes=48 << 20),
        cost_estimate=small_cost(1 << 16),
        name="outer_rows",
    )(*operands)


def outer_sum_kernel(pairs, *refs):
    out_ref = refs[-1]
    _, ny, _, nfar, _, sub, _ = out_ref.shape
    total = None
    for p in range(pairs):
        term = dot(refs[2 * p][...], refs[2 * p + 1][...], ((0,), (0,)))
        total = term if total is None else total + term
    for far in range(nfar):
        for near in range(2):
            for y in range(ny):
                at = ((far * 2 + near) * ny + y) * sub
                out_ref[0, y, 0, far, near] = total[at : at + sub].astype(bf16)


def outer_sum(pairs, cols, at, owners):
    nx, nfar, ny = owners
    width = pairs[0][0].shape[1]
    tile = width // (2 * nx)
    sub = tile // (2 * nfar * ny)
    in_specs, operands = [], []
    for a, b in pairs:
        in_specs.append(pl.BlockSpec((a.shape[0], tile), lambda i: (0, i)))
        in_specs.append(resident((b.shape[0], cols), (0, at)))
        operands += [a, b]
    return pl.pallas_call(
        functools.partial(outer_sum_kernel, len(pairs)),
        grid=(2 * nx,),
        in_specs=in_specs,
        out_specs=pl.BlockSpec(
            (1, ny, 1, nfar, 2, sub, cols), lambda i: (i // 2, 0, i % 2, 0, 0, 0, 0)
        ),
        out_shape=jax.ShapeDtypeStruct((nx, ny, 2, nfar, 2, sub, cols), bf16),
        compiler_params=pltpu.CompilerParams(vmem_limit_bytes=48 << 20),
        cost_estimate=small_cost(1 << 16),
        name="outer_sum",
    )(*operands)


def rms_scale(hidden):
    return lax.rsqrt(jnp.mean(hidden * hidden, axis=-1, keepdims=True) + EPSILON)


def rms_back(grad_scaled, scaled, inverse):
    return inverse * (grad_scaled - scaled * jnp.mean(grad_scaled * scaled, axis=-1, keepdims=True))


def exchange(pieces):
    return lax.all_to_all(pieces, SEQ, split_axis=0, concat_axis=0, tiled=True)


def local(
    tokens,
    cotangent,
    segments,
    joint_projection_matrix,
    output_weight_rows,
    gate_up_weight,
    down_weight_rows,
    attn_gain,
    ffn_gain,
):
    n = lax.axis_size(SEQ)
    me = lax.axis_index(SEQ)
    seqs, rows, width = tokens.shape
    full_len = segments.shape[1]
    heads = H // n
    qw = heads * HD
    sub = joint_projection_matrix.shape[0]
    part = FF // 4
    nx, nfar, ny = (lax.axis_size(axis) for axis in ("x", "far", "y"))
    flow = Flow()

    column = jnp.arange(full_len, dtype=jnp.int32)
    starts_here = jnp.concatenate(
        [jnp.ones((seqs, 1), dtype=bool), segments[:, 1:] != segments[:, :-1]], axis=1
    )
    doc_start = lax.cummax(jnp.where(starts_here, column, 0), axis=1)
    position = lax.dynamic_slice_in_dim(column - doc_start, me * rows, rows, 1)
    doc_start = doc_start.reshape(seqs, n, rows)
    first_block = doc_start[:, :, 0] // rows
    plain_from = jnp.minimum((doc_start[:, :, -1] + rows - 1) // rows, jnp.arange(n))
    plain_from = jnp.maximum(plain_from, first_block)
    doc_start = doc_start[:, :, None, :]
    frequency = ROTARY_BASE ** (-(jnp.arange(HD // 2, dtype=f32) * 2.0) / HD)
    angles = position.astype(f32).reshape(seqs * rows, 1) * frequency
    cosine = jnp.concatenate([jnp.cos(angles)] * 4, axis=1)
    sine = jnp.concatenate([-jnp.sin(angles), jnp.sin(angles)] * 2, axis=1)

    hidden_all = tokens.reshape(seqs * rows, width).astype(f32)
    grad_out_all = cotangent.reshape(seqs * rows, width)
    gain_one = attn_gain.astype(f32)
    gain_two = ffn_gain.astype(f32)

    def own_rows(weight):
        gathered = lax.all_gather(weight, ("x",) + SEQ, axis=0, tiled=True)
        return gathered.reshape(nx, -1, weight.shape[1])

    def core_features(values):
        w = width // (2 * nx)
        bit = my_bit(CORE)
        return tuple(
            jnp.concatenate(
                [lax.dynamic_slice_in_dim(values, (2 * i + c) * w, w, 1) for i in range(nx)], axis=1
            )
            for c in (bit, 1 - bit)
        )

    def flat(values):
        return values.reshape(-1, values.shape[-1])

    def lane_halves(values, key):
        w = values.shape[-1] // 2
        bit = my_bit(key)
        return (
            lax.dynamic_slice_in_dim(values, bit * w, w, values.ndim - 1),
            lax.dynamic_slice_in_dim(values, (1 - bit) * w, w, values.ndim - 1),
        )

    def lanes_by_bit(mine, other, key):
        low = my_bit(key) == 0
        return [jnp.where(low, mine, other), jnp.where(low, other, mine)]

    class Group:
        def __init__(self, values):
            self.values, self.core = values, swap(values, CORE)
            self.arrived = swap(values, NEAR)

        def done(self):
            near = self.arrived
            return jnp.concatenate([self.values, self.core, near, swap(near, CORE)], axis=0)

    class GroupSum:
        def __init__(self, partial):
            self.mine = partial.reshape(2, 2, rows, -1)
            self.arrived = swap(self.mine[:, 1], CORE)

        def next(self):
            both = self.mine[:, 0].astype(f32) + self.arrived.astype(f32)
            self.mine = both[0]
            self.arrived = swap(both[1].astype(bf16), NEAR)

        def done(self):
            return self.mine + self.arrived.astype(f32)

    qkv = Gather(joint_projection_matrix, "near", 0)
    out = Gather(output_weight_rows, "far", 0)
    flow.close(flow.token, wait=[qkv])

    qkv = Gather(qkv.done(), "far", 0)
    near_parts, near_swaps = [], []
    for weight in (gate_up_weight[:, :FF], gate_up_weight[:, FF:], down_weight_rows):
        mine, other = lane_halves(weight, NEAR)
        near_parts.append(mine)
        near_swaps.append(other)
    near_swap = Swap(flow.open(jnp.stack(near_swaps)), NEAR)
    inverse_one = rms_scale(hidden_all)
    scaled_one = hidden_all * inverse_one
    normed_one = (scaled_one * gain_one).astype(bf16)
    normed_one_own, normed_one_other = core_features(normed_one)
    normed_one_own, normed_one_other, cosine, sine = flow.close(
        normed_one_own, normed_one_other, cosine, sine, wait=[qkv, near_swap, out]
    )

    left, right = jnp.split(qkv.done(), 2, axis=-1)
    left = Gather(left, "y", 2)
    right = Gather(right, "x", 0)
    core_parts, core_swaps = [], []
    for mine, arrived in zip(near_parts, near_swap.arrived):
        mine, other = lane_halves(by_bit(mine, arrived, NEAR, 0), CORE)
        core_parts.append(mine)
        core_swaps.append(other)
    core_swap = Swap(jnp.stack(core_swaps), CORE)
    out = Gather(out.done(), "near", 1)
    flow.close(flow.token, wait=[left, right, core_swap, out])

    def over_xy(values):
        gathered = lax.all_gather(flat(values), ("x", "y"), axis=0, tiled=True)
        return gathered.reshape((nx * ny,) + values.shape)

    left = Gather(left.done(), "x", 0)
    right = Gather(right.done(), "y", 3)
    gate, up, down = (
        by_bit(mine, arrived, CORE, 0) for mine, arrived in zip(core_parts, core_swap.arrived)
    )
    gate = Gather(gate, "far", 1)
    w_out_own = over_xy(out.done())
    grad_group_0 = Group(flow.open(grad_out_all[:rows]))
    up, down = flow.close(up, down, wait=[left, right, gate, grad_group_0])

    w_own = jnp.concatenate([flat(left.done()), flat(right.done())], axis=1)
    w_swap = Swap(w_own, CORE)
    up = Gather(up, "far", 1)
    grad_group_1 = Group(flow.open(grad_out_all[rows:]))
    projected = dot(normed_one_own, w_own)
    w_other = w_swap.arrived
    projected = projected + dot(normed_one_other, w_other)
    packed_0 = pack_heads(projected, cosine, sine, 0, rows, n)
    packed_0 = flow.close(packed_0, wait=[up, grad_group_1])

    def attend_one(b, qkv_b):
        return attend(first_block[b], plain_from[b], doc_start[b], qkv_b, heads)

    packed_0, projected, w_other = flow.open(packed_0, projected, w_other)
    qkv_0 = exchange(packed_0)
    w_gate_up = over_xy(jnp.concatenate([gate.done(), up.done()], axis=-1))
    packed_1 = pack_heads(projected, cosine, sine, 1, rows, n)
    core_arg = lax.axis_index("core").astype(jnp.int32).reshape(1)
    w_shape = (nx, 1, nfar * 2, -1, w_own.shape[1])
    w_qkv = flat(interleave(core_arg, w_own.reshape(w_shape), w_other.reshape(w_shape)))
    qkv_0, packed_1, w_qkv, w_out_own = flow.close(qkv_0, packed_1, w_qkv, w_out_own)

    qkv_0, packed_1 = flow.open(qkv_0, packed_1)
    qkv_1 = exchange(packed_1)
    out_swap = Swap(flow.open(w_out_own), CORE)
    attended_0, raw_0, lse_0 = attend_one(0, qkv_0)
    attended_0, qkv_1 = flow.close(attended_0, qkv_1, wait=[out_swap])

    attended_0, qkv_1 = flow.open(attended_0, qkv_1)
    back_0 = exchange(attended_0)
    w_shape = (nx, ny, nfar * 2, sub, width)
    w_out = interleave(core_arg, w_out_own.reshape(w_shape), out_swap.arrived.reshape(w_shape))
    down = Gather(flow.open(down), "far", 1)
    attended_1, raw_1, lse_1 = attend_one(1, qkv_1)
    attended_1, back_0, w_out = flow.close(attended_1, back_0, flat(w_out), wait=[down])

    def after_attention(b, back):
        attended = jnp.concatenate([back[s] for s in range(n)], axis=1)
        hidden = flow.open(tokens[b]).astype(f32)
        middle = hidden + rows_by(attended, w_out)
        inverse = rms_scale(middle)
        scaled = middle * inverse
        return attended, middle, inverse, scaled, (scaled * gain_two).astype(bf16)

    attended_1, back_0, w_out = flow.open(attended_1, back_0, w_out)
    back_1 = exchange(attended_1)
    attended_0, middle_0, inverse_0, scaled_0, normed_0 = after_attention(0, back_0)
    normed_0 = flow.close(normed_0)

    group_0 = Group(normed_0)
    back_1 = flow.close(back_1)
    attended_1, middle_1, inverse_1, scaled_1, normed_1 = after_attention(1, back_1)
    normed_1, w_gate_up = flow.close(normed_1, w_gate_up, wait=[group_0])
    down.arrived = flow.open(down.arrived)
    w_down = over_xy(down.done())
    group_1 = Group(normed_1)
    group_0 = group_0.done()

    gate_0, up_0, active_0 = ffn_forward(group_0, w_gate_up)
    active_0 = flow.close(active_0, wait=[group_1])
    grad_group_0.arrived, grad_group_1.arrived = flow.open(
        grad_group_0.arrived, grad_group_1.arrived
    )
    grad_group_0 = grad_group_0.done()
    grad_group_1 = grad_group_1.done()

    group_1 = group_1.done()
    gate_1, up_1, active_1 = ffn_forward(flow.open(group_1), w_gate_up)
    active_1 = flow.close(active_1)

    outer = lambda a, b: dot(a, b, ((0,), (0,)))
    owners = (nx, nfar, ny)

    def sum_to_owners(terms):
        rest = terms.shape[2:]
        terms = terms.reshape(-1, terms.shape[-1])
        total = lax.psum_scatter(terms, ("x", "y"), scatter_dimension=0, tiled=True)
        return total.reshape(rest)

    d_down = outer_sum(
        [(grad_group_0, active_0), (grad_group_1, flow.open(active_1))], part, 0, owners
    )
    d_down = flow.close(d_down)

    d_down = sum_to_owners(flow.open(d_down))
    both_0 = ffn_backward(flow.open(grad_group_0), w_down, gate_0, up_0)
    terms_0 = flow.close(project_rows(both_0, w_gate_up))

    grad_normed_0 = GroupSum(terms_0)
    partial_0 = project_rows(flow.open(active_0), w_down)
    partial_0 = flow.close(partial_0, wait=[grad_normed_0])
    grad_normed_0.next()
    result_0 = GroupSum(partial_0)
    both_1 = ffn_backward(flow.open(grad_group_1), w_down, gate_1, up_1)
    terms_1 = project_rows(both_1, w_gate_up)
    terms_1 = flow.close(terms_1, wait=[grad_normed_0, result_0])

    def before_attention(b, g, scaled, inverse):
        grad_middle = grad_out_all[b * rows : (b + 1) * rows].astype(f32) + rms_back(
            g * gain_two, scaled, inverse
        )
        grad_branch = grad_middle.astype(bf16)
        grad_attended = dot(grad_branch, w_out).astype(bf16)
        grad_heads = [grad_attended[:, d * qw : (d + 1) * qw] for d in range(n)]
        return grad_middle, grad_branch, jnp.stack(grad_heads)

    grad_normed_1 = GroupSum(terms_1)
    grad_normed_0 = grad_normed_0.done()
    grad_middle_0, grad_branch_0, grad_heads_0 = before_attention(
        0, grad_normed_0, scaled_0, inverse_0
    )
    grad_heads_0 = flow.close(grad_heads_0, wait=[grad_normed_1])

    grad_normed_1.next()
    grad_heads_0 = exchange(grad_heads_0)
    d_up = outer_sum([(flow.open(group_0), both_0), (group_1, both_1)], part, 1, owners)
    d_up = flow.close(d_up, wait=[grad_normed_1])

    d_up = sum_to_owners(flow.open(d_up))
    d_gate = outer_sum([(flow.open(group_0), both_0), (group_1, both_1)], part, 0, owners)
    d_gate, grad_heads_0 = flow.close(d_gate, grad_heads_0)

    d_gate = sum_to_owners(flow.open(d_gate))
    grad_normed_1 = grad_normed_1.done()
    grad_middle_1, grad_branch_1, grad_heads_1 = before_attention(
        1, grad_normed_1, scaled_1, inverse_1
    )
    grad_heads_1 = flow.close(grad_heads_1)

    grad_heads_1 = exchange(grad_heads_1)
    grad_branch = jnp.concatenate([grad_branch_0, grad_branch_1], axis=0)
    attended = jnp.concatenate([attended_0, attended_1], axis=0)
    d_out = outer(flow.open(grad_branch), attended).astype(bf16)
    d_out = flow.close(d_out.reshape((nx, 2, -1, attended.shape[1])))

    def core_sum(mine, send):
        total = mine.astype(f32) + swap(send.astype(bf16), CORE).astype(f32)
        total = total.astype(bf16).reshape((nx, nfar, 2, ny, sub, total.shape[-1]))
        return total.transpose((0, 3, 1, 2, 4, 5))

    def attend_back_one(b, qkv_b, grad_b, raw_b, lse_b):
        dq, dkv = attend_back(
            first_block[b], plain_from[b], doc_start[b], qkv_b, grad_b, raw_b, lse_b, heads
        )
        return jnp.concatenate([dq, dkv], axis=2)

    d_out = sum_to_owners(core_sum(*choose(d_out, CORE, 1)))
    back_0 = attend_back_one(0, qkv_0, flow.open(grad_heads_0), raw_0, lse_0)
    d_down = Scatter(flow.open(d_down), "far", 1)
    result_0.next()
    back_0, grad_heads_1 = flow.close(back_0, grad_heads_1, wait=[d_down, result_0])

    back_0 = exchange(back_0)
    back_1 = attend_back_one(1, qkv_1, flow.open(grad_heads_1), raw_1, lse_1)
    back_1, back_0 = flow.close(back_1, back_0)

    back_1 = exchange(back_1)
    partial_1 = project_rows(flow.open(active_1), w_down)
    grad_proj_0 = unpack_heads(flow.open(back_0), cosine[:rows], sine[:rows])
    d_up = Scatter(flow.open(d_up), "far", 1)
    back_1, grad_proj_0, partial_1 = flow.close(back_1, grad_proj_0, partial_1, wait=[d_up])

    d_gate = Scatter(flow.open(d_gate), "far", 1)
    result_1 = GroupSum(partial_1)
    grad_proj_1 = unpack_heads(back_1, cosine[rows:], sine[rows:])
    grad_proj = jnp.concatenate([grad_proj_0, grad_proj_1], axis=0)
    core_back = outer_rows(
        [(normed_one_other[:rows], grad_proj_0), (normed_one_other[rows:], grad_proj_1)]
    )
    core_back = Swap(core_back, CORE)
    grad_normed_one = rows_by(grad_proj, w_qkv)
    grad_proj, grad_normed_one = flow.close(
        grad_proj, grad_normed_one, wait=[core_back, result_1, d_gate]
    )
    d_qkv = outer(normed_one_own, grad_proj) + core_back.arrived.astype(f32)
    d_qkv = d_qkv.astype(bf16).reshape((nx, nfar, 2, ny, sub, -1))
    left, right = flow.close(*jnp.split(d_qkv, 2, axis=-1))

    left = Scatter(left, "x", 0)
    right = Scatter(right, "y", 3)
    result_1.next()
    d_out = Scatter(flow.open(d_out), "far", 0)
    ffn = jnp.stack([t.done(last=True) for t in (d_gate, d_up, d_down)])
    mine, send = choose(ffn, NEAR, 2)
    near_back = Swap(send.astype(bf16), NEAR)
    flow.close(flow.token, wait=[left, right])

    left = Scatter(left.done(), "y", 2)
    right = Scatter(right.done(), "x", 0)
    attn_gain_grad = jnp.sum(grad_normed_one * scaled_one, axis=0)
    late_0, late_1 = flow.open(grad_normed_0, grad_normed_1)
    ffn_gain_grad = jnp.sum(late_0 * scaled_0, axis=0) + jnp.sum(late_1 * scaled_1, axis=0)
    gains = jnp.stack([attn_gain_grad, ffn_gain_grad])
    gains, grad_normed_one = flow.close(gains, grad_normed_one, wait=[left, right, near_back])

    d_qkv = Scatter(jnp.concatenate([left.done(), right.done()], axis=-1), "far", 0)
    gains = sum_axes(gains, "x", "y", "core")
    quarters = []
    for part_of in lanes_by_bit(mine, near_back.arrived.astype(f32), NEAR):
        part_mine, part_send = choose(part_of, CORE, 1)
        quarters += lanes_by_bit(part_mine, swap(part_send.astype(bf16), CORE).astype(f32), CORE)
    d_gate_up = jnp.concatenate([q[k] for k in (0, 1) for q in quarters], axis=1)
    d_down = jnp.concatenate([q[2] for q in quarters], axis=1)
    grad_input = jnp.concatenate([grad_middle_0, grad_middle_1], axis=0) + rms_back(
        grad_normed_one * gain_one, scaled_one, inverse_one
    )
    grad_input, gains, d_gate_up, d_down = flow.close(
        grad_input, gains, d_gate_up, d_down, wait=[d_qkv, d_out, result_1]
    )

    d_qkv = Scatter(d_qkv.done(), "near", 0)
    d_out = Scatter(d_out.done(), "near", 0)
    gains = sum_axes(gains, "near", "far")
    result = jnp.concatenate([middle_0 + result_0.done(), middle_1 + result_1.done()], axis=0)
    return (
        result.astype(bf16).reshape(tokens.shape),
        grad_input.reshape(tokens.shape),
        d_qkv.done(last=True),
        d_out.done(last=True),
        d_gate_up,
        d_down,
        gains[0],
        gains[1],
    )


def solution(mesh):
    dp, seq = mesh.devices.shape
    shape = (dp // 2, 2, seq // 4, 2, 2)
    fine = Mesh(mesh.devices.reshape(shape), ("x", "core") + SEQ)
    by_token = P(("x", "core"), SEQ, None)
    by_row = P(("x", "core") + SEQ, None)
    return jax.shard_map(
        local,
        mesh=fine,
        in_specs=(
            by_token,
            by_token,
            P(("x", "core"), None),
            by_row,
            by_row,
            by_row,
            by_row,
            P(),
            P(),
        ),
        out_specs=(by_token, by_token, by_row, by_row, by_row, by_row, P(), P()),
        check_vma=False,
    )
```

```python
import functools
import math

import jax
import jax.numpy as jnp
from jax import lax
from jax.experimental import pallas as pl
from jax.experimental.pallas import tpu as pltpu
from jax.sharding import Mesh
from jax.sharding import PartitionSpec as P

H = 32
HD = 64
KV = 4
FF = 5632

EPSILON = 1e-05
NEG = -1e30
ROTARY_BASE = 10000.0
LOG2E = math.log2(math.e)
LANES = 128

bf16 = jnp.bfloat16
f32 = jnp.float32


def dot(a, b, dims=((1,), (0,))):
    return lax.dot_general(a, b, (dims, ((), ())), preferred_element_type=f32)


CORE = ("core", 0)
NEAR = ("near", 0)
SEQ = ("far", "near", "y")


def axis_bits(axis):
    return [(axis, b) for b in reversed(range((lax.axis_size(axis) - 1).bit_length()))]


def my_bit(key):
    axis, b = key
    return (lax.axis_index(axis) >> b) & 1


def swap(values, key):
    axis, b = key
    return lax.ppermute(values, axis, [(i, i ^ (1 << b)) for i in range(lax.axis_size(axis))])


class Flow:
    def __init__(self):
        self.token = jnp.zeros((), f32)

    def open(self, *values):
        opened = lax.optimization_barrier(values + (self.token,))[:-1]
        return opened if len(values) > 1 else opened[0]

    def close(self, *values, wait=()):
        arrived = tuple(transfer.arrived for transfer in wait)
        closed = lax.optimization_barrier(values + arrived + (self.token,))
        for transfer, value in zip(wait, closed[len(values) :]):
            transfer.arrived = value
        self.token = closed[-1]
        return closed[: len(values)] if len(values) > 1 else closed[0]


def choose(values, key, axis):
    bit = my_bit(key)
    return (
        lax.dynamic_index_in_dim(values, bit, axis, keepdims=False),
        lax.dynamic_index_in_dim(values, 1 - bit, axis, keepdims=False),
    )


def by_bit(mine, other, key, axis):
    low = my_bit(key) == 0
    return jnp.stack([jnp.where(low, mine, other), jnp.where(low, other, mine)], axis=axis)


class Swap:
    def __init__(self, values, key):
        self.arrived = swap(values, key)


class Gather:
    def __init__(self, values, axis, at):
        self.values, self.axis, self.at = values, axis, at
        self.arrived = swap(values, axis_bits(axis)[0])

    def done(self):
        values, other, shape = self.values, self.arrived, self.values.shape
        for step, key in enumerate(axis_bits(self.axis)):
            if step:
                other = swap(values, key)
            values = by_bit(values, other, key, self.at + step)
        return values.reshape(shape[: self.at] + (lax.axis_size(self.axis),) + shape[self.at :])


class Scatter:
    def __init__(self, values, axis, at):
        self.keys, self.at = axis_bits(axis), at
        shape = values.shape
        values = values.reshape(shape[:at] + (2,) * len(self.keys) + shape[at + 1 :])
        self.start(values)

    def start(self, values):
        self.mine, send = choose(values, self.keys[0], self.at)
        self.arrived = swap(send.astype(bf16), self.keys[0])

    def done(self, last=False):
        while True:
            values = self.mine.astype(f32) + self.arrived.astype(f32)
            if not last:
                values = values.astype(bf16)
            self.keys = self.keys[1:]
            if not self.keys:
                return values
            self.start(values)


def sum_axes(values, *axes):
    for axis in axes:
        for key in axis_bits(axis):
            values = values + swap(values, key)
    return values


def stack_heads(x, heads):
    return jnp.concatenate([x[:, h * HD : (h + 1) * HD] for h in range(heads)], axis=0)


def unstack_heads(x, heads):
    rows = x.shape[0] // heads
    return jnp.concatenate([x[h * rows : (h + 1) * rows] for h in range(heads)], axis=1)


def block_allowed(i, j, rows, start):
    key_pos = j * rows + lax.broadcasted_iota(jnp.int32, (rows, rows), 0)
    query_pos = i * rows + lax.broadcasted_iota(jnp.int32, (rows, rows), 1)
    return (key_pos <= query_pos) & (key_pos >= start)


def attend_kernel(
    heads, lo_ref, hi_ref, start_ref, qkv_ref, out_ref, raw_ref, lse_ref, m_s, l_s, acc_s
):
    rows = qkv_ref.shape[1]
    qw = heads * HD
    scale = LOG2E * HD**-0.5
    i = pl.program_id(0)
    q = stack_heads(qkv_ref[i, :, :qw], heads)
    m_s[...] = jnp.full_like(m_s, NEG)
    l_s[...] = jnp.zeros_like(l_s)
    acc_s[...] = jnp.zeros_like(acc_s)

    def block(j, masked):
        k = qkv_ref[j, :, qw : qw + HD]
        v = qkv_ref[j, :, qw + HD : qw + 2 * HD]
        s = dot(k, q, ((1,), (1,)))
        if masked:
            ok = block_allowed(i, j, rows, start_ref[0])
            s = jnp.where(jnp.concatenate([ok] * heads, axis=1), s, NEG)
        m_old = m_s[...]
        m_new = jnp.maximum(m_old, jnp.max(s, axis=0, keepdims=True) * scale)
        p = jnp.exp2(s * scale - m_new)
        keep = jnp.exp2(m_old - m_new)
        l_s[...] = l_s[...] * keep + jnp.sum(p, axis=0, keepdims=True)
        acc_s[...] = acc_s[...] * keep + dot(v, p.astype(bf16), ((0,), (0,)))
        m_s[...] = m_new

    def masked_step(j, carry):
        block(j, True)
        return carry

    def plain_step(j, carry):
        block(j, False)
        return carry

    block(i, True)
    lax.fori_loop(lo_ref[i], hi_ref[i], masked_step, 0)
    lax.fori_loop(hi_ref[i], i, plain_step, 0)
    total = l_s[...]
    result = unstack_heads(jnp.transpose(acc_s[...] / total), heads)
    raw_ref[0] = result
    out_ref[0] = result.astype(bf16)
    lse_ref[0] = jnp.broadcast_to(m_s[...] + jnp.log2(total), (8, heads * rows))


def attend(lo, hi, start, qkv, heads):
    n, rows, w = qkv.shape
    qw = heads * HD
    smem = pl.BlockSpec(memory_space=pltpu.SMEM)
    pairs = heads * (n * rows) ** 2 // 2
    per_block = lambda shape: pl.BlockSpec((1,) + shape, lambda i: (i, 0, 0))
    return pl.pallas_call(
        functools.partial(attend_kernel, heads),
        grid=(n,),
        out_shape=(
            jax.ShapeDtypeStruct((n, rows, qw), bf16),
            jax.ShapeDtypeStruct((n, rows, qw), f32),
            jax.ShapeDtypeStruct((n, 8, heads * rows), f32),
        ),
        in_specs=[
            smem,
            smem,
            per_block((1, rows)),
            pl.BlockSpec((n, rows, w), lambda i: (0, 0, 0)),
        ],
        out_specs=(per_block((rows, qw)), per_block((rows, qw)), per_block((8, heads * rows))),
        scratch_shapes=[
            pltpu.VMEM((1, heads * rows), f32),
            pltpu.VMEM((1, heads * rows), f32),
            pltpu.VMEM((HD, heads * rows), f32),
        ],
        compiler_params=pltpu.CompilerParams(vmem_limit_bytes=48 << 20),
        cost_estimate=pl.CostEstimate(flops=0, bytes_accessed=1 << 20, transcendentals=0),
        name="attend",
    )(lo, hi, start, qkv)


def attend_back_kernel(
    heads,
    lo_ref,
    hi_ref,
    start_ref,
    qkv_ref,
    g_ref,
    raw_ref,
    lse_ref,
    dq_ref,
    dkv_ref,
    dkv_s,
    dq_s,
):
    n, rows, _ = qkv_ref.shape
    qw = heads * HD
    scale = LOG2E * HD**-0.5
    i = pl.program_id(0)

    @pl.when(i == 0)
    def _():
        dkv_s[...] = jnp.zeros_like(dkv_s)

    dq_s[...] = jnp.zeros_like(dq_s)
    q = stack_heads(qkv_ref[i, :, :qw], heads)
    g_flat = g_ref[i]
    g = stack_heads(g_flat, heads)
    product = g_flat.astype(f32) * raw_ref[0]
    inner = jnp.concatenate(
        [
            jnp.sum(product[:, h * HD : (h + 1) * HD], axis=1, keepdims=True)
            for h in range(heads)
        ],
        axis=0,
    )
    inner = jnp.transpose(jnp.broadcast_to(inner, (heads * rows, LANES)))[:1]
    lse = lse_ref[0, :1]

    def block(j, masked):
        k = qkv_ref[j, :, qw : qw + HD]
        v = qkv_ref[j, :, qw + HD : qw + 2 * HD]
        s = dot(k, q, ((1,), (1,)))
        grad_probs = dot(v, g, ((1,), (1,)))
        p = jnp.exp2(s * scale - lse)
        if masked:
            ok = block_allowed(i, j, rows, start_ref[0])
            p = jnp.where(jnp.concatenate([ok] * heads, axis=1), p, 0.0)
        grad_scores = (p * (grad_probs - inner)).astype(bf16)
        dkv_s[j, :, :HD] += dot(grad_scores, q)
        dkv_s[j, :, HD:] += dot(p.astype(bf16), g)
        dq_s[...] += dot(k, grad_scores, ((0,), (0,)))

    def masked_step(j, carry):
        block(j, True)
        return carry

    def plain_step(j, carry):
        block(j, False)
        return carry

    lax.fori_loop(lo_ref[i], hi_ref[i], masked_step, 0)
    lax.fori_loop(hi_ref[i], i, plain_step, 0)
    block(i, True)
    dq = unstack_heads(jnp.transpose(dq_s[...] * HD**-0.5), heads)
    dq_ref[0] = dq.astype(bf16)

    @pl.when(i == n - 1)
    def _():
        for r in range(n):
            done = dkv_s[r]
            dkv_ref[r] = jnp.concatenate([done[:, :HD] * HD**-0.5, done[:, HD:]], axis=1).astype(
                bf16
            )


def attend_back(lo, hi, start, qkv, grad, raw, lse, heads):
    n, rows, w = qkv.shape
    qw = heads * HD
    smem = pl.BlockSpec(memory_space=pltpu.SMEM)
    pairs = heads * (n * rows) ** 2 // 2
    per_block = lambda shape: pl.BlockSpec((1,) + shape, lambda i: (i, 0, 0))
    whole = lambda shape: pl.BlockSpec(shape, lambda i: (0, 0, 0))
    return pl.pallas_call(
        functools.partial(attend_back_kernel, heads),
        grid=(n,),
        out_shape=(
            jax.ShapeDtypeStruct((n, rows, qw), bf16),
            jax.ShapeDtypeStruct((n, rows, 2 * HD), bf16),
        ),
        in_specs=[
            smem,
            smem,
            per_block((1, rows)),
            whole((n, rows, w)),
            whole((n, rows, qw)),
            per_block((rows, qw)),
            per_block((8, heads * rows)),
        ],
        out_specs=(per_block((rows, qw)), whole((n, rows, 2 * HD))),
        scratch_shapes=[
            pltpu.VMEM((n, rows, 2 * HD), f32),
            pltpu.VMEM((HD, heads * rows), f32),
        ],
        compiler_params=pltpu.CompilerParams(vmem_limit_bytes=48 << 20),
        cost_estimate=pl.CostEstimate(flops=0, bytes_accessed=1 << 20, transcendentals=0),
        name="attend_back",
    )(lo, hi, start, qkv, grad, raw, lse)


def rotate_lanes(v, cosine, signed_sine):
    parts = []
    for c in range(v.shape[1] // LANES):
        part = v[:, c * LANES : (c + 1) * LANES]
        lane = lax.broadcasted_iota(jnp.int32, part.shape, 1)
        other = jnp.where(
            lane % HD < HD // 2,
            pltpu.roll(part, LANES - HD // 2, 1),
            pltpu.roll(part, HD // 2, 1),
        )
        parts.append(part * cosine + other * signed_sine)
    return jnp.concatenate(parts, axis=1) if len(parts) > 1 else parts[0]


def pack_kernel(copies, q_ref, k_ref, v_ref, cos_ref, sin_ref, out_ref):
    qw = q_ref.shape[1]
    cosine = cos_ref[...]
    sine = sin_ref[...]
    out_ref[0, :, :qw] = rotate_lanes(q_ref[...], cosine, sine).astype(bf16)
    k = rotate_lanes(k_ref[...], cosine, sine)
    v = v_ref[...]
    first = (pl.program_id(0) // copies) % 2 == 0
    lane = lax.broadcasted_iota(jnp.int32, k.shape, 1)
    k = jnp.where(first, k, pltpu.roll(k, HD, 1))
    v = jnp.where(first, pltpu.roll(v, HD, 1), v)
    out_ref[0, :, qw:] = jnp.where(lane < HD, k, v).astype(bf16)


def pack_heads(projected, cosine, sine, seq, rows, n):
    qw = H * HD // n
    copies = n // KV
    k_at = H * HD // LANES
    v_at = k_at + KV * HD // LANES
    table = pl.BlockSpec((rows, LANES), lambda d: (seq, 0))
    return pl.pallas_call(
        functools.partial(pack_kernel, copies),
        grid=(n,),
        in_specs=[
            pl.BlockSpec((rows, qw), lambda d: (seq, d)),
            pl.BlockSpec((rows, LANES), lambda d: (seq, k_at + d // copies // 2)),
            pl.BlockSpec((rows, LANES), lambda d: (seq, v_at + d // copies // 2)),
            table,
            table,
        ],
        out_specs=pl.BlockSpec((1, rows, qw + 2 * HD), lambda d: (d, 0, 0)),
        out_shape=jax.ShapeDtypeStruct((n, rows, qw + 2 * HD), bf16),
        cost_estimate=pl.CostEstimate(flops=0, bytes_accessed=6 << 20, transcendentals=0),
        name="pack_heads",
    )(projected, projected, projected, cosine, sine)


def unpack_kernel(n, in_ref, cos_ref, sin_ref, out_ref):
    qw = in_ref.shape[2] - 2 * HD
    copies = n // KV
    cosine = cos_ref[...]
    sine = -sin_ref[...]
    lane = lax.broadcasted_iota(jnp.int32, cosine.shape, 1)
    for d in range(n):
        part = in_ref[d, :, :qw].astype(f32)
        out_ref[:, d * qw : (d + 1) * qw] = rotate_lanes(part, cosine, sine).astype(bf16)
    for pair in range(KV // 2):
        sums = []
        for head in (2 * pair, 2 * pair + 1):
            slots = [in_ref[head * copies + c, :, qw:].astype(f32) for c in range(copies)]
            sums.append(sum(slots[1:], slots[0]))
        k = jnp.where(lane < HD, sums[0], pltpu.roll(sums[1], HD, 1))
        v = jnp.where(lane < HD, pltpu.roll(sums[0], HD, 1), sums[1])
        k_at = H * HD + pair * LANES
        v_at = k_at + KV * HD
        out_ref[:, k_at : k_at + LANES] = rotate_lanes(k, cosine, sine).astype(bf16)
        out_ref[:, v_at : v_at + LANES] = v.astype(bf16)


def unpack_heads(pieces, cosine, sine):
    n, rows, w = pieces.shape
    cols = H * HD + 2 * KV * HD
    return pl.pallas_call(
        functools.partial(unpack_kernel, n),
        out_shape=jax.ShapeDtypeStruct((rows, cols), bf16),
        in_specs=[pl.BlockSpec(memory_space=pltpu.VMEM)] * 3,
        out_specs=pl.BlockSpec(memory_space=pltpu.VMEM),
        compiler_params=pltpu.CompilerParams(vmem_limit_bytes=32 << 20),
        cost_estimate=pl.CostEstimate(flops=0, bytes_accessed=4 << 20, transcendentals=0),
        name="unpack_heads",
    )(pieces, cosine, sine)


def interleave_kernel(core_ref, own_ref, other_ref, out_ref):
    del core_ref
    for i, ref in enumerate((own_ref, other_ref)):

        @pl.when(pl.program_id(2) == i)
        def _():
            out_ref[0, 0, 0] = ref[0, :, 0]


def interleave(core, own, other):
    nx, ny, inner, sub, cols = own.shape
    spec = pl.BlockSpec((1, ny, 1, sub, cols), lambda x, k, i, core_ref: (x, 0, k, 0, 0))
    return pl.pallas_call(
        interleave_kernel,
        grid_spec=pltpu.PrefetchScalarGridSpec(
            num_scalar_prefetch=1,
            grid=(nx, inner, 2),
            in_specs=[spec, spec],
            out_specs=pl.BlockSpec(
                (1, 1, 1, ny, sub, cols), lambda x, k, i, core_ref: (x, core_ref[0] ^ i, k, 0, 0, 0)
            ),
        ),
        out_shape=jax.ShapeDtypeStruct((nx, 2, inner, ny, sub, cols), own.dtype),
        compiler_params=pltpu.CompilerParams(vmem_limit_bytes=48 << 20),
        cost_estimate=pl.CostEstimate(flops=0, bytes_accessed=1 << 16, transcendentals=0),
        name="interleave",
    )(core, own, other)


ROW_TILE = 256


def small_cost(size):
    return pl.CostEstimate(flops=0, bytes_accessed=size, transcendentals=0)


def resident(shape, index):
    return pl.BlockSpec(shape, lambda i: index, pipeline_mode=pl.Buffered(1))


def by_rows(tile, cols, at=0):
    return pl.BlockSpec((tile, cols), lambda i: (i, at))


def row_copies(w_ref, w_s, sems):
    xy, _, nfar, _, sub, _ = w_ref.shape
    ny = 2
    copies = []
    for x in range(xy // ny):
        for core in range(2):
            for far in range(nfar):
                for near in range(2):
                    for y in range(ny):
                        block = len(copies)
                        copies.append(
                            pltpu.make_async_copy(
                                w_ref.at[x * ny + y, core, far, near],
                                w_s.at[pl.ds(block * sub, sub)],
                                sems.at[block],
                            )
                        )
    return copies


def load_rows(w_ref, w_s, sems):
    copies = row_copies(w_ref, w_s, sems)
    for copy in copies:
        copy.start()
    for copy in copies:
        copy.wait()


def with_weights(kernel):
    def run(x_ref, w_ref, *refs):
        *refs, w_s, sems = refs

        @pl.when(pl.program_id(0) == 0)
        def _():
            load_rows(w_ref, w_s, sems)

        kernel(x_ref, w_s, *refs)

    return run


def over_rows(kernel, x, w, others, outs, name):
    m = x.shape[0]
    blocks = w.shape[0] * w.shape[1] * w.shape[2] * w.shape[3]
    tile = min(ROW_TILE, m)
    return pl.pallas_call(
        with_weights(kernel),
        grid=(m // tile,),
        in_specs=[by_rows(tile, x.shape[1]), pl.BlockSpec(memory_space=pl.ANY)]
        + [by_rows(tile, other.shape[1]) for other in others],
        out_specs=[by_rows(tile, cols) for cols, _ in outs],
        out_shape=[jax.ShapeDtypeStruct((m, cols), t) for cols, t in outs],
        scratch_shapes=[
            pltpu.VMEM((blocks * w.shape[4], w.shape[5]), bf16),
            pltpu.SemaphoreType.DMA((blocks,)),
        ],
        compiler_params=pltpu.CompilerParams(vmem_limit_bytes=48 << 20),
        cost_estimate=small_cost(1 << 16),
        name=name,
    )(x, w, *others)


def ffn_forward_kernel(x_ref, w_ref, gate_ref, up_ref, active_ref):
    units = gate_ref.shape[1]
    x = x_ref[...]
    gate = dot(x, w_ref[:, :units])
    gate_ref[...] = gate
    up = dot(x, w_ref[:, units:])
    up_ref[...] = up
    active_ref[...] = (gate * jax.nn.sigmoid(gate) * up).astype(bf16)


def ffn_forward(x, w_gate_up):
    units = w_gate_up.shape[-1] // 2
    outs = [(units, f32), (units, f32), (units, bf16)]
    return over_rows(ffn_forward_kernel, x, w_gate_up, [], outs, "ffn_forward")


def ffn_backward_kernel(g_ref, w_ref, gate_ref, up_ref, both_ref):
    units = gate_ref.shape[1]
    grad_active = dot(g_ref[...], w_ref[...])
    gate = gate_ref[...]
    s = jax.nn.sigmoid(gate)
    grad_gate = grad_active * up_ref[...] * s * (1.0 + gate * (1.0 - s))
    both_ref[:, :units] = grad_gate.astype(bf16)
    both_ref[:, units:] = (grad_active * gate * s).astype(bf16)


def ffn_backward(grad, w_down, gate, up):
    outs = [(2 * gate.shape[1], bf16)]
    return over_rows(ffn_backward_kernel, grad, w_down, [gate, up], outs, "ffn_backward")[0]


def project_rows_kernel(x_ref, w_ref, out_ref, w_s, sems):
    first = pl.program_id(0) == 0
    x = x_ref[...]

    @pl.when(first)
    def _():
        copies = row_copies(w_ref, w_s, sems)
        for copy in copies:
            copy.start()
        rows = w_s.shape[0] // 8
        count = len(copies) // 8
        for group in range(8):
            for copy in copies[group * count : (group + 1) * count]:
                copy.wait()
            part = slice(group * rows, (group + 1) * rows)
            out_ref[:, part] = dot(x, w_s[part, :], ((1,), (1,))).astype(bf16)

    @pl.when(jnp.logical_not(first))
    def _():
        out_ref[...] = dot(x, w_s[...], ((1,), (1,))).astype(bf16)


def project_rows(x, w):
    m = x.shape[0]
    blocks = w.shape[0] * w.shape[1] * w.shape[2] * w.shape[3]
    rows = blocks * w.shape[4]
    tile = min(ROW_TILE, m)
    return pl.pallas_call(
        project_rows_kernel,
        grid=(m // tile,),
        in_specs=[by_rows(tile, x.shape[1]), pl.BlockSpec(memory_space=pl.ANY)],
        out_specs=by_rows(tile, rows),
        out_shape=jax.ShapeDtypeStruct((m, rows), bf16),
        scratch_shapes=[pltpu.VMEM((rows, w.shape[5]), bf16), pltpu.SemaphoreType.DMA((blocks,))],
        compiler_params=pltpu.CompilerParams(vmem_limit_bytes=48 << 20),
        cost_estimate=small_cost(1 << 16),
        name="project_rows",
    )(x, w)


def rows_by_kernel(x_ref, w_ref, out_ref):
    out_ref[...] = dot(x_ref[...], w_ref[...], ((1,), (1,)))


def rows_by(x, w):
    m = x.shape[0]
    tile = min(ROW_TILE, m)
    return pl.pallas_call(
        rows_by_kernel,
        grid=(m // tile,),
        in_specs=[by_rows(tile, x.shape[1]), resident(w.shape, (0, 0))],
        out_specs=by_rows(tile, w.shape[0]),
        out_shape=jax.ShapeDtypeStruct((m, w.shape[0]), f32),
        compiler_params=pltpu.CompilerParams(vmem_limit_bytes=48 << 20),
        cost_estimate=small_cost(1 << 16),
        name="rows_by",
    )(x, w)


def outer_rows_kernel(*refs):
    total = None
    for p in range(len(refs) // 2):
        term = dot(refs[2 * p][...], refs[2 * p + 1][...], ((0,), (0,)))
        total = term if total is None else total + term
    refs[-1][...] = total.astype(bf16)


def outer_rows(pairs):
    width = pairs[0][0].shape[1]
    cols = pairs[0][1].shape[1]
    tile = min(ROW_TILE, width)
    in_specs, operands = [], []
    for a, b in pairs:
        in_specs.append(pl.BlockSpec((a.shape[0], tile), lambda i: (0, i)))
        in_specs.append(resident(b.shape, (0, 0)))
        operands += [a, b]
    return pl.pallas_call(
        outer_rows_kernel,
        grid=(width // tile,),
        in_specs=in_specs,
        out_specs=by_rows(tile, cols),
        out_shape=jax.ShapeDtypeStruct((width, cols), bf16),
        compiler_params=pltpu.CompilerParams(vmem_limit_bytes=48 << 20),
        cost_estimate=small_cost(1 << 16),
        name="outer_rows",
    )(*operands)


def outer_sum_kernel(pairs, *refs):
    out_ref = refs[-1]
    _, ny, _, nfar, _, sub, _ = out_ref.shape
    total = None
    for p in range(pairs):
        term = dot(refs[2 * p][...], refs[2 * p + 1][...], ((0,), (0,)))
        total = term if total is None else total + term
    for far in range(nfar):
        for near in range(2):
            for y in range(ny):
                at = ((far * 2 + near) * ny + y) * sub
                out_ref[0, y, 0, far, near] = total[at : at + sub].astype(bf16)


def outer_sum(pairs, cols, at, owners):
    nx, nfar, ny = owners
    width = pairs[0][0].shape[1]
    tile = width // (2 * nx)
    sub = tile // (2 * nfar * ny)
    in_specs, operands = [], []
    for a, b in pairs:
        in_specs.append(pl.BlockSpec((a.shape[0], tile), lambda i: (0, i)))
        in_specs.append(resident((b.shape[0], cols), (0, at)))
        operands += [a, b]
    return pl.pallas_call(
        functools.partial(outer_sum_kernel, len(pairs)),
        grid=(2 * nx,),
        in_specs=in_specs,
        out_specs=pl.BlockSpec(
            (1, ny, 1, nfar, 2, sub, cols), lambda i: (i // 2, 0, i % 2, 0, 0, 0, 0)
        ),
        out_shape=jax.ShapeDtypeStruct((nx, ny, 2, nfar, 2, sub, cols), bf16),
        compiler_params=pltpu.CompilerParams(vmem_limit_bytes=48 << 20),
        cost_estimate=small_cost(1 << 16),
        name="outer_sum",
    )(*operands)


def rms_scale(hidden):
    return lax.rsqrt(jnp.mean(hidden * hidden, axis=-1, keepdims=True) + EPSILON)


def rms_back(grad_scaled, scaled, inverse):
    return inverse * (grad_scaled - scaled * jnp.mean(grad_scaled * scaled, axis=-1, keepdims=True))


def exchange(pieces):
    return lax.all_to_all(pieces, SEQ, split_axis=0, concat_axis=0, tiled=True)


def local(
    tokens,
    cotangent,
    segments,
    joint_projection_matrix,
    output_weight_rows,
    gate_up_weight,
    down_weight_rows,
    attn_gain,
    ffn_gain,
):
    n = lax.axis_size(SEQ)
    me = lax.axis_index(SEQ)
    seqs, rows, width = tokens.shape
    full_len = segments.shape[1]
    heads = H // n
    qw = heads * HD
    sub = joint_projection_matrix.shape[0]
    part = FF // 4
    nx, nfar, ny = (lax.axis_size(axis) for axis in ("x", "far", "y"))
    flow = Flow()

    column = jnp.arange(full_len, dtype=jnp.int32)
    starts_here = jnp.concatenate(
        [jnp.ones((seqs, 1), dtype=bool), segments[:, 1:] != segments[:, :-1]], axis=1
    )
    doc_start = lax.cummax(jnp.where(starts_here, column, 0), axis=1)
    position = lax.dynamic_slice_in_dim(column - doc_start, me * rows, rows, 1)
    doc_start = doc_start.reshape(seqs, n, rows)
    first_block = doc_start[:, :, 0] // rows
    plain_from = jnp.minimum((doc_start[:, :, -1] + rows - 1) // rows, jnp.arange(n))
    plain_from = jnp.maximum(plain_from, first_block)
    doc_start = doc_start[:, :, None, :]
    frequency = ROTARY_BASE ** (-(jnp.arange(HD // 2, dtype=f32) * 2.0) / HD)
    angles = position.astype(f32).reshape(seqs * rows, 1) * frequency
    cosine = jnp.concatenate([jnp.cos(angles)] * 4, axis=1)
    sine = jnp.concatenate([-jnp.sin(angles), jnp.sin(angles)] * 2, axis=1)

    hidden_all = tokens.reshape(seqs * rows, width).astype(f32)
    grad_out_all = cotangent.reshape(seqs * rows, width)
    gain_one = attn_gain.astype(f32)
    gain_two = ffn_gain.astype(f32)

    def own_rows(weight):
        gathered = lax.all_gather(weight, ("x",) + SEQ, axis=0, tiled=True)
        return gathered.reshape(nx, -1, weight.shape[1])

    def core_features(values):
        w = width // (2 * nx)
        bit = my_bit(CORE)
        return tuple(
            jnp.concatenate(
                [lax.dynamic_slice_in_dim(values, (2 * i + c) * w, w, 1) for i in range(nx)], axis=1
            )
            for c in (bit, 1 - bit)
        )

    def flat(values):
        return values.reshape(-1, values.shape[-1])

    def lane_halves(values, key):
        w = values.shape[-1] // 2
        bit = my_bit(key)
        return (
            lax.dynamic_slice_in_dim(values, bit * w, w, values.ndim - 1),
            lax.dynamic_slice_in_dim(values, (1 - bit) * w, w, values.ndim - 1),
        )

    def lanes_by_bit(mine, other, key):
        low = my_bit(key) == 0
        return [jnp.where(low, mine, other), jnp.where(low, other, mine)]

    class Group:
        def __init__(self, values):
            self.values, self.core = values, swap(values, CORE)
            self.arrived = swap(values, NEAR)

        def done(self):
            near = self.arrived
            return jnp.concatenate([self.values, self.core, near, swap(near, CORE)], axis=0)

    class GroupSum:
        def __init__(self, partial):
            self.mine = partial.reshape(2, 2, rows, -1)
            self.arrived = swap(self.mine[:, 1], CORE)

        def next(self):
            both = self.mine[:, 0].astype(f32) + self.arrived.astype(f32)
            self.mine = both[0]
            self.arrived = swap(both[1].astype(bf16), NEAR)

        def done(self):
            return self.mine + self.arrived.astype(f32)

    qkv = Gather(joint_projection_matrix, "near", 0)
    out = Gather(output_weight_rows, "far", 0)
    flow.close(flow.token, wait=[qkv])

    qkv = Gather(qkv.done(), "far", 0)
    near_parts, near_swaps = [], []
    for weight in (gate_up_weight[:, :FF], gate_up_weight[:, FF:], down_weight_rows):
        mine, other = lane_halves(weight, NEAR)
        near_parts.append(mine)
        near_swaps.append(other)
    near_swap = Swap(flow.open(jnp.stack(near_swaps)), NEAR)
    inverse_one = rms_scale(hidden_all)
    scaled_one = hidden_all * inverse_one
    normed_one = (scaled_one * gain_one).astype(bf16)
    normed_one_own, normed_one_other = core_features(normed_one)
    normed_one_own, normed_one_other, cosine, sine = flow.close(
        normed_one_own, normed_one_other, cosine, sine, wait=[qkv, near_swap, out]
    )

    left, right = jnp.split(qkv.done(), 2, axis=-1)
    left = Gather(left, "y", 2)
    right = Gather(right, "x", 0)
    core_parts, core_swaps = [], []
    for mine, arrived in zip(near_parts, near_swap.arrived):
        mine, other = lane_halves(by_bit(mine, arrived, NEAR, 0), CORE)
        core_parts.append(mine)
        core_swaps.append(other)
    core_swap = Swap(jnp.stack(core_swaps), CORE)
    out = Gather(out.done(), "near", 1)
    flow.close(flow.token, wait=[left, right, core_swap, out])

    def over_xy(values):
        gathered = lax.all_gather(flat(values), ("x", "y"), axis=0, tiled=True)
        return gathered.reshape((nx * ny,) + values.shape)

    left = Gather(left.done(), "x", 0)
    right = Gather(right.done(), "y", 3)
    gate, up, down = (
        by_bit(mine, arrived, CORE, 0) for mine, arrived in zip(core_parts, core_swap.arrived)
    )
    gate = Gather(gate, "far", 1)
    w_out_own = over_xy(out.done())
    grad_group_0 = Group(flow.open(grad_out_all[:rows]))
    up, down = flow.close(up, down, wait=[left, right, gate, grad_group_0])

    w_own = jnp.concatenate([flat(left.done()), flat(right.done())], axis=1)
    w_swap = Swap(w_own, CORE)
    up = Gather(up, "far", 1)
    projected = dot(normed_one_own, w_own)
    w_other = w_swap.arrived
    projected = projected + dot(normed_one_other, w_other)
    packed_0 = pack_heads(projected, cosine, sine, 0, rows, n)
    packed_0 = flow.close(packed_0, wait=[up])

    def attend_one(b, qkv_b):
        return attend(first_block[b], plain_from[b], doc_start[b], qkv_b, heads)

    packed_0, projected, w_other = flow.open(packed_0, projected, w_other)
    qkv_0 = exchange(packed_0)
    w_gate_up = over_xy(jnp.concatenate([gate.done(), up.done()], axis=-1))
    packed_1 = pack_heads(projected, cosine, sine, 1, rows, n)
    core_arg = lax.axis_index("core").astype(jnp.int32).reshape(1)
    w_shape = (nx, 1, nfar * 2, -1, w_own.shape[1])
    w_qkv = flat(interleave(core_arg, w_own.reshape(w_shape), w_other.reshape(w_shape)))
    qkv_0, packed_1, w_qkv, w_out_own = flow.close(qkv_0, packed_1, w_qkv, w_out_own)

    qkv_0, packed_1 = flow.open(qkv_0, packed_1)
    qkv_1 = exchange(packed_1)
    out_swap = Swap(flow.open(w_out_own), CORE)
    attended_0, raw_0, lse_0 = attend_one(0, qkv_0)
    attended_0, qkv_1 = flow.close(attended_0, qkv_1, wait=[out_swap])

    attended_0, qkv_1 = flow.open(attended_0, qkv_1)
    back_0 = exchange(attended_0)
    w_shape = (nx, ny, nfar * 2, sub, width)
    w_out = interleave(core_arg, w_out_own.reshape(w_shape), out_swap.arrived.reshape(w_shape))
    down = Gather(flow.open(down), "far", 1)
    attended_1, raw_1, lse_1 = attend_one(1, qkv_1)
    attended_1, back_0, w_out = flow.close(attended_1, back_0, flat(w_out), wait=[down])

    def after_attention(b, back):
        attended = jnp.concatenate([back[s] for s in range(n)], axis=1)
        hidden = flow.open(tokens[b]).astype(f32)
        middle = hidden + rows_by(attended, w_out)
        inverse = rms_scale(middle)
        scaled = middle * inverse
        return attended, middle, inverse, scaled, (scaled * gain_two).astype(bf16)

    attended_1, back_0, w_out = flow.open(attended_1, back_0, w_out)
    back_1 = exchange(attended_1)
    attended_0, middle_0, inverse_0, scaled_0, normed_0 = after_attention(0, back_0)
    normed_0 = flow.close(normed_0)

    group_0 = Group(normed_0)
    back_1 = flow.close(back_1)
    attended_1, middle_1, inverse_1, scaled_1, normed_1 = after_attention(1, back_1)
    normed_1, w_gate_up = flow.close(normed_1, w_gate_up, wait=[group_0])
    down.arrived = flow.open(down.arrived)
    w_down = over_xy(down.done())
    group_1 = Group(normed_1)
    group_0 = group_0.done()

    gate_0, up_0, active_0 = ffn_forward(group_0, w_gate_up)
    active_0 = flow.close(active_0, wait=[group_1])
    grad_group_0.arrived = flow.open(grad_group_0.arrived)
    grad_group_0 = grad_group_0.done()
    grad_group_1 = Group(flow.open(grad_out_all[rows:]))

    group_1 = group_1.done()
    gate_1, up_1, active_1 = ffn_forward(flow.open(group_1), w_gate_up)
    active_1 = flow.close(active_1, wait=[grad_group_1])
    grad_group_1 = grad_group_1.done()

    outer = lambda a, b: dot(a, b, ((0,), (0,)))
    owners = (nx, nfar, ny)

    def sum_to_owners(terms):
        rest = terms.shape[2:]
        terms = terms.reshape(-1, terms.shape[-1])
        total = lax.psum_scatter(terms, ("x", "y"), scatter_dimension=0, tiled=True)
        return total.reshape(rest)

    d_down = outer_sum(
        [(grad_group_0, active_0), (grad_group_1, flow.open(active_1))], part, 0, owners
    )
    d_down = flow.close(d_down)

    d_down = sum_to_owners(flow.open(d_down))
    both_0 = ffn_backward(flow.open(grad_group_0), w_down, gate_0, up_0)
    terms_0 = flow.close(project_rows(both_0, w_gate_up))

    grad_normed_0 = GroupSum(terms_0)
    partial_0 = project_rows(flow.open(active_0), w_down)
    partial_0 = flow.close(partial_0, wait=[grad_normed_0])
    grad_normed_0.next()
    result_0 = GroupSum(partial_0)
    both_1 = ffn_backward(flow.open(grad_group_1), w_down, gate_1, up_1)
    terms_1 = project_rows(both_1, w_gate_up)
    terms_1 = flow.close(terms_1, wait=[grad_normed_0, result_0])

    def before_attention(b, g, scaled, inverse):
        grad_middle = grad_out_all[b * rows : (b + 1) * rows].astype(f32) + rms_back(
            g * gain_two, scaled, inverse
        )
        grad_branch = grad_middle.astype(bf16)
        grad_attended = dot(grad_branch, w_out).astype(bf16)
        grad_heads = [grad_attended[:, d * qw : (d + 1) * qw] for d in range(n)]
        return grad_middle, grad_branch, jnp.stack(grad_heads)

    grad_normed_1 = GroupSum(terms_1)
    grad_normed_0 = grad_normed_0.done()
    grad_middle_0, grad_branch_0, grad_heads_0 = before_attention(
        0, grad_normed_0, scaled_0, inverse_0
    )
    grad_heads_0 = flow.close(grad_heads_0, wait=[grad_normed_1])

    grad_normed_1.next()
    grad_heads_0 = exchange(grad_heads_0)
    d_up = outer_sum([(flow.open(group_0), both_0), (group_1, both_1)], part, 1, owners)
    d_up = flow.close(d_up, wait=[grad_normed_1])

    d_up = sum_to_owners(flow.open(d_up))
    d_gate = outer_sum([(flow.open(group_0), both_0), (group_1, both_1)], part, 0, owners)
    d_gate, grad_heads_0 = flow.close(d_gate, grad_heads_0)

    d_gate = sum_to_owners(flow.open(d_gate))
    grad_normed_1 = grad_normed_1.done()
    grad_middle_1, grad_branch_1, grad_heads_1 = before_attention(
        1, grad_normed_1, scaled_1, inverse_1
    )
    grad_heads_1 = flow.close(grad_heads_1)

    grad_heads_1 = exchange(grad_heads_1)
    grad_branch = jnp.concatenate([grad_branch_0, grad_branch_1], axis=0)
    attended = jnp.concatenate([attended_0, attended_1], axis=0)
    d_out = outer(flow.open(grad_branch), attended).astype(bf16)
    d_out = flow.close(d_out.reshape((nx, 2, -1, attended.shape[1])))

    def core_sum(mine, send):
        total = mine.astype(f32) + swap(send.astype(bf16), CORE).astype(f32)
        total = total.astype(bf16).reshape((nx, nfar, 2, ny, sub, total.shape[-1]))
        return total.transpose((0, 3, 1, 2, 4, 5))

    def attend_back_one(b, qkv_b, grad_b, raw_b, lse_b):
        dq, dkv = attend_back(
            first_block[b], plain_from[b], doc_start[b], qkv_b, grad_b, raw_b, lse_b, heads
        )
        return jnp.concatenate([dq, dkv], axis=2)

    d_out = sum_to_owners(core_sum(*choose(d_out, CORE, 1)))
    back_0 = attend_back_one(0, qkv_0, flow.open(grad_heads_0), raw_0, lse_0)
    d_down = Scatter(flow.open(d_down), "far", 1)
    result_0.next()
    back_0, grad_heads_1 = flow.close(back_0, grad_heads_1, wait=[d_down, result_0])

    back_0 = exchange(back_0)
    back_1 = attend_back_one(1, qkv_1, flow.open(grad_heads_1), raw_1, lse_1)
    back_1, back_0 = flow.close(back_1, back_0)

    back_1 = exchange(back_1)
    partial_1 = project_rows(flow.open(active_1), w_down)
    grad_proj_0 = unpack_heads(flow.open(back_0), cosine[:rows], sine[:rows])
    d_up = Scatter(flow.open(d_up), "far", 1)
    back_1, grad_proj_0, partial_1 = flow.close(back_1, grad_proj_0, partial_1, wait=[d_up])

    d_gate = Scatter(flow.open(d_gate), "far", 1)
    result_1 = GroupSum(partial_1)
    grad_proj_1 = unpack_heads(back_1, cosine[rows:], sine[rows:])
    grad_proj = jnp.concatenate([grad_proj_0, grad_proj_1], axis=0)
    core_back = outer_rows(
        [(normed_one_other[:rows], grad_proj_0), (normed_one_other[rows:], grad_proj_1)]
    )
    core_back = Swap(core_back, CORE)
    grad_normed_one = rows_by(grad_proj, w_qkv)
    grad_proj, grad_normed_one = flow.close(
        grad_proj, grad_normed_one, wait=[core_back, result_1, d_gate]
    )
    d_qkv = outer(normed_one_own, grad_proj) + core_back.arrived.astype(f32)
    d_qkv = d_qkv.astype(bf16).reshape((nx, nfar, 2, ny, sub, -1))
    left, right = flow.close(*jnp.split(d_qkv, 2, axis=-1))

    left = Scatter(left, "x", 0)
    right = Scatter(right, "y", 3)
    result_1.next()
    d_out = Scatter(flow.open(d_out), "far", 0)
    ffn = jnp.stack([t.done(last=True) for t in (d_gate, d_up, d_down)])
    mine, send = choose(ffn, NEAR, 2)
    near_back = Swap(send.astype(bf16), NEAR)
    flow.close(flow.token, wait=[left, right])

    left = Scatter(left.done(), "y", 2)
    right = Scatter(right.done(), "x", 0)
    attn_gain_grad = jnp.sum(grad_normed_one * scaled_one, axis=0)
    late_0, late_1 = flow.open(grad_normed_0, grad_normed_1)
    ffn_gain_grad = jnp.sum(late_0 * scaled_0, axis=0) + jnp.sum(late_1 * scaled_1, axis=0)
    gains = jnp.stack([attn_gain_grad, ffn_gain_grad])
    gains, grad_normed_one = flow.close(gains, grad_normed_one, wait=[left, right, near_back])

    d_qkv = Scatter(jnp.concatenate([left.done(), right.done()], axis=-1), "far", 0)
    gains = sum_axes(gains, "x", "y", "core")
    quarters = []
    for part_of in lanes_by_bit(mine, near_back.arrived.astype(f32), NEAR):
        part_mine, part_send = choose(part_of, CORE, 1)
        quarters += lanes_by_bit(part_mine, swap(part_send.astype(bf16), CORE).astype(f32), CORE)
    d_gate_up = jnp.concatenate([q[k] for k in (0, 1) for q in quarters], axis=1)
    d_down = jnp.concatenate([q[2] for q in quarters], axis=1)
    grad_input = jnp.concatenate([grad_middle_0, grad_middle_1], axis=0) + rms_back(
        grad_normed_one * gain_one, scaled_one, inverse_one
    )
    grad_input, gains, d_gate_up, d_down = flow.close(
        grad_input, gains, d_gate_up, d_down, wait=[d_qkv, d_out, result_1]
    )

    d_qkv = Scatter(d_qkv.done(), "near", 0)
    d_out = Scatter(d_out.done(), "near", 0)
    gains = sum_axes(gains, "near", "far")
    result = jnp.concatenate([middle_0 + result_0.done(), middle_1 + result_1.done()], axis=0)
    return (
        result.astype(bf16).reshape(tokens.shape),
        grad_input.reshape(tokens.shape),
        d_qkv.done(last=True),
        d_out.done(last=True),
        d_gate_up,
        d_down,
        gains[0],
        gains[1],
    )


def solution(mesh):
    dp, seq = mesh.devices.shape
    shape = (dp // 2, 2, seq // 4, 2, 2)
    fine = Mesh(mesh.devices.reshape(shape), ("x", "core") + SEQ)
    by_token = P(("x", "core"), SEQ, None)
    by_row = P(("x", "core") + SEQ, None)
    return jax.shard_map(
        local,
        mesh=fine,
        in_specs=(
            by_token,
            by_token,
            P(("x", "core"), None),
            by_row,
            by_row,
            by_row,
            by_row,
            P(),
            P(),
        ),
        out_specs=(by_token, by_token, by_row, by_row, by_row, by_row, P(), P()),
        check_vma=False,
    )
```

```python
import functools
import math

import jax
import jax.numpy as jnp
from jax import lax
from jax.experimental import pallas as pl
from jax.experimental.pallas import tpu as pltpu
from jax.sharding import Mesh
from jax.sharding import PartitionSpec as P

H = 32
HD = 64
KV = 4
FF = 5632

EPSILON = 1e-05
NEG = -1e30
ROTARY_BASE = 10000.0
LOG2E = math.log2(math.e)
LANES = 128

bf16 = jnp.bfloat16
f32 = jnp.float32


def dot(a, b, dims=((1,), (0,))):
    return lax.dot_general(a, b, (dims, ((), ())), preferred_element_type=f32)


CORE = ("core", 0)
NEAR = ("near", 0)
SEQ = ("far", "near", "y")


def axis_bits(axis):
    return [(axis, b) for b in reversed(range((lax.axis_size(axis) - 1).bit_length()))]


def my_bit(key):
    axis, b = key
    return (lax.axis_index(axis) >> b) & 1


def swap(values, key):
    axis, b = key
    return lax.ppermute(values, axis, [(i, i ^ (1 << b)) for i in range(lax.axis_size(axis))])


class Flow:
    def __init__(self):
        self.token = jnp.zeros((), f32)

    def open(self, *values):
        opened = lax.optimization_barrier(values + (self.token,))[:-1]
        return opened if len(values) > 1 else opened[0]

    def close(self, *values, wait=()):
        arrived = tuple(transfer.arrived for transfer in wait)
        closed = lax.optimization_barrier(values + arrived + (self.token,))
        for transfer, value in zip(wait, closed[len(values) :]):
            transfer.arrived = value
        self.token = closed[-1]
        return closed[: len(values)] if len(values) > 1 else closed[0]


def choose(values, key, axis):
    bit = my_bit(key)
    return (
        lax.dynamic_index_in_dim(values, bit, axis, keepdims=False),
        lax.dynamic_index_in_dim(values, 1 - bit, axis, keepdims=False),
    )


def by_bit(mine, other, key, axis):
    low = my_bit(key) == 0
    return jnp.stack([jnp.where(low, mine, other), jnp.where(low, other, mine)], axis=axis)


class Swap:
    def __init__(self, values, key):
        self.arrived = swap(values, key)


class Gather:
    def __init__(self, values, axis, at):
        self.values, self.axis, self.at = values, axis, at
        self.arrived = swap(values, axis_bits(axis)[0])

    def done(self):
        values, other, shape = self.values, self.arrived, self.values.shape
        for step, key in enumerate(axis_bits(self.axis)):
            if step:
                other = swap(values, key)
            values = by_bit(values, other, key, self.at + step)
        return values.reshape(shape[: self.at] + (lax.axis_size(self.axis),) + shape[self.at :])


class Scatter:
    def __init__(self, values, axis, at):
        self.keys, self.at = axis_bits(axis), at
        shape = values.shape
        values = values.reshape(shape[:at] + (2,) * len(self.keys) + shape[at + 1 :])
        self.start(values)

    def start(self, values):
        self.mine, send = choose(values, self.keys[0], self.at)
        self.arrived = swap(send.astype(bf16), self.keys[0])

    def done(self, last=False):
        while True:
            values = self.mine.astype(f32) + self.arrived.astype(f32)
            if not last:
                values = values.astype(bf16)
            self.keys = self.keys[1:]
            if not self.keys:
                return values
            self.start(values)


def sum_axes(values, *axes):
    for axis in axes:
        for key in axis_bits(axis):
            values = values + swap(values, key)
    return values


def stack_heads(x, heads):
    return jnp.concatenate([x[:, h * HD : (h + 1) * HD] for h in range(heads)], axis=0)


def unstack_heads(x, heads):
    rows = x.shape[0] // heads
    return jnp.concatenate([x[h * rows : (h + 1) * rows] for h in range(heads)], axis=1)


def block_allowed(i, j, rows, start):
    key_pos = j * rows + lax.broadcasted_iota(jnp.int32, (rows, rows), 0)
    query_pos = i * rows + lax.broadcasted_iota(jnp.int32, (rows, rows), 1)
    return (key_pos <= query_pos) & (key_pos >= start)


def attend_kernel(
    heads, lo_ref, hi_ref, start_ref, qkv_ref, out_ref, raw_ref, lse_ref, m_s, l_s, acc_s
):
    rows = qkv_ref.shape[1]
    qw = heads * HD
    scale = LOG2E * HD**-0.5
    i = pl.program_id(0)
    q = stack_heads(qkv_ref[i, :, :qw], heads)
    m_s[...] = jnp.full_like(m_s, NEG)
    l_s[...] = jnp.zeros_like(l_s)
    acc_s[...] = jnp.zeros_like(acc_s)

    def block(j, masked):
        k = qkv_ref[j, :, qw : qw + HD]
        v = qkv_ref[j, :, qw + HD : qw + 2 * HD]
        s = dot(k, q, ((1,), (1,)))
        if masked:
            ok = block_allowed(i, j, rows, start_ref[0])
            s = jnp.where(jnp.concatenate([ok] * heads, axis=1), s, NEG)
        m_old = m_s[...]
        m_new = jnp.maximum(m_old, jnp.max(s, axis=0, keepdims=True) * scale)
        p = jnp.exp2(s * scale - m_new)
        keep = jnp.exp2(m_old - m_new)
        l_s[...] = l_s[...] * keep + jnp.sum(p, axis=0, keepdims=True)
        acc_s[...] = acc_s[...] * keep + dot(v, p.astype(bf16), ((0,), (0,)))
        m_s[...] = m_new

    def masked_step(j, carry):
        block(j, True)
        return carry

    def plain_step(j, carry):
        block(j, False)
        return carry

    block(i, True)
    lax.fori_loop(lo_ref[i], hi_ref[i], masked_step, 0)
    lax.fori_loop(hi_ref[i], i, plain_step, 0)
    total = l_s[...]
    result = unstack_heads(jnp.transpose(acc_s[...] / total), heads)
    raw_ref[0] = result
    out_ref[0] = result.astype(bf16)
    lse_ref[0] = jnp.broadcast_to(m_s[...] + jnp.log2(total), (8, heads * rows))


def attend(lo, hi, start, qkv, heads):
    n, rows, w = qkv.shape
    qw = heads * HD
    smem = pl.BlockSpec(memory_space=pltpu.SMEM)
    pairs = heads * (n * rows) ** 2 // 2
    per_block = lambda shape: pl.BlockSpec((1,) + shape, lambda i: (i, 0, 0))
    return pl.pallas_call(
        functools.partial(attend_kernel, heads),
        grid=(n,),
        out_shape=(
            jax.ShapeDtypeStruct((n, rows, qw), bf16),
            jax.ShapeDtypeStruct((n, rows, qw), f32),
            jax.ShapeDtypeStruct((n, 8, heads * rows), f32),
        ),
        in_specs=[
            smem,
            smem,
            per_block((1, rows)),
            pl.BlockSpec((n, rows, w), lambda i: (0, 0, 0)),
        ],
        out_specs=(per_block((rows, qw)), per_block((rows, qw)), per_block((8, heads * rows))),
        scratch_shapes=[
            pltpu.VMEM((1, heads * rows), f32),
            pltpu.VMEM((1, heads * rows), f32),
            pltpu.VMEM((HD, heads * rows), f32),
        ],
        compiler_params=pltpu.CompilerParams(vmem_limit_bytes=48 << 20),
        cost_estimate=pl.CostEstimate(flops=0, bytes_accessed=1 << 20, transcendentals=0),
        name="attend",
    )(lo, hi, start, qkv)


def attend_back_kernel(
    heads,
    lo_ref,
    hi_ref,
    start_ref,
    qkv_ref,
    g_ref,
    raw_ref,
    lse_ref,
    dq_ref,
    dkv_ref,
    dkv_s,
    dq_s,
):
    n, rows, _ = qkv_ref.shape
    qw = heads * HD
    scale = LOG2E * HD**-0.5
    i = pl.program_id(0)

    @pl.when(i == 0)
    def _():
        dkv_s[...] = jnp.zeros_like(dkv_s)

    dq_s[...] = jnp.zeros_like(dq_s)
    q = stack_heads(qkv_ref[i, :, :qw], heads)
    g_flat = g_ref[i]
    g = stack_heads(g_flat, heads)
    product = g_flat.astype(f32) * raw_ref[0]
    inner = jnp.concatenate(
        [
            jnp.sum(product[:, h * HD : (h + 1) * HD], axis=1, keepdims=True)
            for h in range(heads)
        ],
        axis=0,
    )
    inner = jnp.transpose(jnp.broadcast_to(inner, (heads * rows, LANES)))[:1]
    lse = lse_ref[0, :1]

    def block(j, masked):
        k = qkv_ref[j, :, qw : qw + HD]
        v = qkv_ref[j, :, qw + HD : qw + 2 * HD]
        s = dot(k, q, ((1,), (1,)))
        grad_probs = dot(v, g, ((1,), (1,)))
        p = jnp.exp2(s * scale - lse)
        if masked:
            ok = block_allowed(i, j, rows, start_ref[0])
            p = jnp.where(jnp.concatenate([ok] * heads, axis=1), p, 0.0)
        grad_scores = (p * (grad_probs - inner)).astype(bf16)
        dkv_s[j, :, :HD] += dot(grad_scores, q)
        dkv_s[j, :, HD:] += dot(p.astype(bf16), g)
        dq_s[...] += dot(k, grad_scores, ((0,), (0,)))

    def masked_step(j, carry):
        block(j, True)
        return carry

    def plain_step(j, carry):
        block(j, False)
        return carry

    lax.fori_loop(lo_ref[i], hi_ref[i], masked_step, 0)
    lax.fori_loop(hi_ref[i], i, plain_step, 0)
    block(i, True)
    dq = unstack_heads(jnp.transpose(dq_s[...] * HD**-0.5), heads)
    dq_ref[0] = dq.astype(bf16)

    @pl.when(i == n - 1)
    def _():
        for r in range(n):
            done = dkv_s[r]
            dkv_ref[r] = jnp.concatenate([done[:, :HD] * HD**-0.5, done[:, HD:]], axis=1).astype(
                bf16
            )


def attend_back(lo, hi, start, qkv, grad, raw, lse, heads):
    n, rows, w = qkv.shape
    qw = heads * HD
    smem = pl.BlockSpec(memory_space=pltpu.SMEM)
    pairs = heads * (n * rows) ** 2 // 2
    per_block = lambda shape: pl.BlockSpec((1,) + shape, lambda i: (i, 0, 0))
    whole = lambda shape: pl.BlockSpec(shape, lambda i: (0, 0, 0))
    return pl.pallas_call(
        functools.partial(attend_back_kernel, heads),
        grid=(n,),
        out_shape=(
            jax.ShapeDtypeStruct((n, rows, qw), bf16),
            jax.ShapeDtypeStruct((n, rows, 2 * HD), bf16),
        ),
        in_specs=[
            smem,
            smem,
            per_block((1, rows)),
            whole((n, rows, w)),
            whole((n, rows, qw)),
            per_block((rows, qw)),
            per_block((8, heads * rows)),
        ],
        out_specs=(per_block((rows, qw)), whole((n, rows, 2 * HD))),
        scratch_shapes=[
            pltpu.VMEM((n, rows, 2 * HD), f32),
            pltpu.VMEM((HD, heads * rows), f32),
        ],
        compiler_params=pltpu.CompilerParams(vmem_limit_bytes=48 << 20),
        cost_estimate=pl.CostEstimate(flops=0, bytes_accessed=1 << 20, transcendentals=0),
        name="attend_back",
    )(lo, hi, start, qkv, grad, raw, lse)


def rotate_lanes(v, cosine, signed_sine):
    parts = []
    for c in range(v.shape[1] // LANES):
        part = v[:, c * LANES : (c + 1) * LANES]
        lane = lax.broadcasted_iota(jnp.int32, part.shape, 1)
        other = jnp.where(
            lane % HD < HD // 2,
            pltpu.roll(part, LANES - HD // 2, 1),
            pltpu.roll(part, HD // 2, 1),
        )
        parts.append(part * cosine + other * signed_sine)
    return jnp.concatenate(parts, axis=1) if len(parts) > 1 else parts[0]


def pack_kernel(copies, q_ref, k_ref, v_ref, cos_ref, sin_ref, out_ref):
    qw = q_ref.shape[1]
    cosine = cos_ref[...]
    sine = sin_ref[...]
    out_ref[0, :, :qw] = rotate_lanes(q_ref[...], cosine, sine).astype(bf16)
    k = rotate_lanes(k_ref[...], cosine, sine)
    v = v_ref[...]
    first = (pl.program_id(0) // copies) % 2 == 0
    lane = lax.broadcasted_iota(jnp.int32, k.shape, 1)
    k = jnp.where(first, k, pltpu.roll(k, HD, 1))
    v = jnp.where(first, pltpu.roll(v, HD, 1), v)
    out_ref[0, :, qw:] = jnp.where(lane < HD, k, v).astype(bf16)


def pack_heads(projected, cosine, sine, seq, rows, n):
    qw = H * HD // n
    copies = n // KV
    k_at = H * HD // LANES
    v_at = k_at + KV * HD // LANES
    table = pl.BlockSpec((rows, LANES), lambda d: (seq, 0))
    return pl.pallas_call(
        functools.partial(pack_kernel, copies),
        grid=(n,),
        in_specs=[
            pl.BlockSpec((rows, qw), lambda d: (seq, d)),
            pl.BlockSpec((rows, LANES), lambda d: (seq, k_at + d // copies // 2)),
            pl.BlockSpec((rows, LANES), lambda d: (seq, v_at + d // copies // 2)),
            table,
            table,
        ],
        out_specs=pl.BlockSpec((1, rows, qw + 2 * HD), lambda d: (d, 0, 0)),
        out_shape=jax.ShapeDtypeStruct((n, rows, qw + 2 * HD), bf16),
        cost_estimate=pl.CostEstimate(flops=0, bytes_accessed=6 << 20, transcendentals=0),
        name="pack_heads",
    )(projected, projected, projected, cosine, sine)


def unpack_kernel(n, in_ref, cos_ref, sin_ref, out_ref):
    qw = in_ref.shape[2] - 2 * HD
    copies = n // KV
    cosine = cos_ref[...]
    sine = -sin_ref[...]
    lane = lax.broadcasted_iota(jnp.int32, cosine.shape, 1)
    for d in range(n):
        part = in_ref[d, :, :qw].astype(f32)
        out_ref[:, d * qw : (d + 1) * qw] = rotate_lanes(part, cosine, sine).astype(bf16)
    for pair in range(KV // 2):
        sums = []
        for head in (2 * pair, 2 * pair + 1):
            slots = [in_ref[head * copies + c, :, qw:].astype(f32) for c in range(copies)]
            sums.append(sum(slots[1:], slots[0]))
        k = jnp.where(lane < HD, sums[0], pltpu.roll(sums[1], HD, 1))
        v = jnp.where(lane < HD, pltpu.roll(sums[0], HD, 1), sums[1])
        k_at = H * HD + pair * LANES
        v_at = k_at + KV * HD
        out_ref[:, k_at : k_at + LANES] = rotate_lanes(k, cosine, sine).astype(bf16)
        out_ref[:, v_at : v_at + LANES] = v.astype(bf16)


def unpack_heads(pieces, cosine, sine):
    n, rows, w = pieces.shape
    cols = H * HD + 2 * KV * HD
    return pl.pallas_call(
        functools.partial(unpack_kernel, n),
        out_shape=jax.ShapeDtypeStruct((rows, cols), bf16),
        in_specs=[pl.BlockSpec(memory_space=pltpu.VMEM)] * 3,
        out_specs=pl.BlockSpec(memory_space=pltpu.VMEM),
        compiler_params=pltpu.CompilerParams(vmem_limit_bytes=32 << 20),
        cost_estimate=pl.CostEstimate(flops=0, bytes_accessed=4 << 20, transcendentals=0),
        name="unpack_heads",
    )(pieces, cosine, sine)


def interleave_kernel(core_ref, own_ref, other_ref, out_ref):
    del core_ref
    for i, ref in enumerate((own_ref, other_ref)):

        @pl.when(pl.program_id(2) == i)
        def _():
            out_ref[0, 0, 0] = ref[0, :, 0]


def interleave(core, own, other):
    nx, ny, inner, sub, cols = own.shape
    spec = pl.BlockSpec((1, ny, 1, sub, cols), lambda x, k, i, core_ref: (x, 0, k, 0, 0))
    return pl.pallas_call(
        interleave_kernel,
        grid_spec=pltpu.PrefetchScalarGridSpec(
            num_scalar_prefetch=1,
            grid=(nx, inner, 2),
            in_specs=[spec, spec],
            out_specs=pl.BlockSpec(
                (1, 1, 1, ny, sub, cols), lambda x, k, i, core_ref: (x, core_ref[0] ^ i, k, 0, 0, 0)
            ),
        ),
        out_shape=jax.ShapeDtypeStruct((nx, 2, inner, ny, sub, cols), own.dtype),
        compiler_params=pltpu.CompilerParams(vmem_limit_bytes=48 << 20),
        cost_estimate=pl.CostEstimate(flops=0, bytes_accessed=1 << 16, transcendentals=0),
        name="interleave",
    )(core, own, other)


ROW_TILE = 256


def small_cost(size):
    return pl.CostEstimate(flops=0, bytes_accessed=size, transcendentals=0)


def resident(shape, index):
    return pl.BlockSpec(shape, lambda i: index, pipeline_mode=pl.Buffered(1))


def by_rows(tile, cols, at=0):
    return pl.BlockSpec((tile, cols), lambda i: (i, at))


def load_rows(w_ref, w_s, sems):
    xy, _, nfar, _, sub, _ = w_ref.shape
    ny = 2
    copies = []
    for g in range(xy):
        for core in range(2):
            for far in range(nfar):
                for near in range(2):
                    block = (((g // ny * 2 + core) * nfar + far) * 2 + near) * ny + g % ny
                    copies.append(
                        pltpu.make_async_copy(
                            w_ref.at[g, core, far, near],
                            w_s.at[pl.ds(block * sub, sub)],
                            sems.at[block],
                        )
                    )
    for copy in copies:
        copy.start()
    for copy in copies:
        copy.wait()


def with_weights(kernel):
    def run(x_ref, w_ref, *refs):
        *refs, w_s, sems = refs

        @pl.when(pl.program_id(0) == 0)
        def _():
            load_rows(w_ref, w_s, sems)

        kernel(x_ref, w_s, *refs)

    return run


def over_rows(kernel, x, w, others, outs, name):
    m = x.shape[0]
    blocks = w.shape[0] * w.shape[1] * w.shape[2] * w.shape[3]
    tile = min(ROW_TILE, m)
    return pl.pallas_call(
        with_weights(kernel),
        grid=(m // tile,),
        in_specs=[by_rows(tile, x.shape[1]), pl.BlockSpec(memory_space=pl.ANY)]
        + [by_rows(tile, other.shape[1]) for other in others],
        out_specs=[by_rows(tile, cols) for cols, _ in outs],
        out_shape=[jax.ShapeDtypeStruct((m, cols), t) for cols, t in outs],
        scratch_shapes=[
            pltpu.VMEM((blocks * w.shape[4], w.shape[5]), bf16),
            pltpu.SemaphoreType.DMA((blocks,)),
        ],
        compiler_params=pltpu.CompilerParams(vmem_limit_bytes=48 << 20),
        cost_estimate=small_cost(1 << 16),
        name=name,
    )(x, w, *others)


def ffn_forward_kernel(x_ref, w_ref, gate_ref, up_ref, active_ref):
    units = gate_ref.shape[1]
    x = x_ref[...]
    gate = dot(x, w_ref[:, :units])
    gate_ref[...] = gate
    up = dot(x, w_ref[:, units:])
    up_ref[...] = up
    active_ref[...] = (gate * jax.nn.sigmoid(gate) * up).astype(bf16)


def ffn_forward(x, w_gate_up):
    units = w_gate_up.shape[-1] // 2
    outs = [(units, f32), (units, f32), (units, bf16)]
    return over_rows(ffn_forward_kernel, x, w_gate_up, [], outs, "ffn_forward")


def ffn_backward_kernel(g_ref, w_ref, gate_ref, up_ref, both_ref):
    units = gate_ref.shape[1]
    grad_active = dot(g_ref[...], w_ref[...])
    gate = gate_ref[...]
    s = jax.nn.sigmoid(gate)
    grad_gate = grad_active * up_ref[...] * s * (1.0 + gate * (1.0 - s))
    both_ref[:, :units] = grad_gate.astype(bf16)
    both_ref[:, units:] = (grad_active * gate * s).astype(bf16)


def ffn_backward(grad, w_down, gate, up):
    outs = [(2 * gate.shape[1], bf16)]
    return over_rows(ffn_backward_kernel, grad, w_down, [gate, up], outs, "ffn_backward")[0]


def project_rows_kernel(x_ref, w_ref, out_ref):
    out_ref[...] = dot(x_ref[...], w_ref[...], ((1,), (1,))).astype(bf16)


def project_rows(x, w):
    rows = w.shape[0] * w.shape[1] * w.shape[2] * w.shape[3] * w.shape[4]
    return over_rows(project_rows_kernel, x, w, [], [(rows, bf16)], "project_rows")[0]


def rows_by_kernel(x_ref, w_ref, out_ref):
    out_ref[...] = dot(x_ref[...], w_ref[...], ((1,), (1,)))


def rows_by(x, w):
    m = x.shape[0]
    tile = min(ROW_TILE, m)
    return pl.pallas_call(
        rows_by_kernel,
        grid=(m // tile,),
        in_specs=[by_rows(tile, x.shape[1]), resident(w.shape, (0, 0))],
        out_specs=by_rows(tile, w.shape[0]),
        out_shape=jax.ShapeDtypeStruct((m, w.shape[0]), f32),
        compiler_params=pltpu.CompilerParams(vmem_limit_bytes=48 << 20),
        cost_estimate=small_cost(1 << 16),
        name="rows_by",
    )(x, w)


def outer_rows_kernel(*refs):
    total = None
    for p in range(len(refs) // 2):
        term = dot(refs[2 * p][...], refs[2 * p + 1][...], ((0,), (0,)))
        total = term if total is None else total + term
    refs[-1][...] = total.astype(bf16)


def outer_rows(pairs):
    width = pairs[0][0].shape[1]
    cols = pairs[0][1].shape[1]
    tile = min(ROW_TILE, width)
    in_specs, operands = [], []
    for a, b in pairs:
        in_specs.append(pl.BlockSpec((a.shape[0], tile), lambda i: (0, i)))
        in_specs.append(resident(b.shape, (0, 0)))
        operands += [a, b]
    return pl.pallas_call(
        outer_rows_kernel,
        grid=(width // tile,),
        in_specs=in_specs,
        out_specs=by_rows(tile, cols),
        out_shape=jax.ShapeDtypeStruct((width, cols), bf16),
        compiler_params=pltpu.CompilerParams(vmem_limit_bytes=48 << 20),
        cost_estimate=small_cost(1 << 16),
        name="outer_rows",
    )(*operands)


def outer_sum_kernel(pairs, *refs):
    out_ref = refs[-1]
    _, ny, _, nfar, _, sub, _ = out_ref.shape
    total = None
    for p in range(pairs):
        term = dot(refs[2 * p][...], refs[2 * p + 1][...], ((0,), (0,)))
        total = term if total is None else total + term
    for far in range(nfar):
        for near in range(2):
            for y in range(ny):
                at = ((far * 2 + near) * ny + y) * sub
                out_ref[0, y, 0, far, near] = total[at : at + sub].astype(bf16)


def outer_sum(pairs, cols, at, owners):
    nx, nfar, ny = owners
    width = pairs[0][0].shape[1]
    tile = width // (2 * nx)
    sub = tile // (2 * nfar * ny)
    in_specs, operands = [], []
    for a, b in pairs:
        in_specs.append(pl.BlockSpec((a.shape[0], tile), lambda i: (0, i)))
        in_specs.append(resident((b.shape[0], cols), (0, at)))
        operands += [a, b]
    return pl.pallas_call(
        functools.partial(outer_sum_kernel, len(pairs)),
        grid=(2 * nx,),
        in_specs=in_specs,
        out_specs=pl.BlockSpec(
            (1, ny, 1, nfar, 2, sub, cols), lambda i: (i // 2, 0, i % 2, 0, 0, 0, 0)
        ),
        out_shape=jax.ShapeDtypeStruct((nx, ny, 2, nfar, 2, sub, cols), bf16),
        compiler_params=pltpu.CompilerParams(vmem_limit_bytes=48 << 20),
        cost_estimate=small_cost(1 << 16),
        name="outer_sum",
    )(*operands)


def rms_scale(hidden):
    return lax.rsqrt(jnp.mean(hidden * hidden, axis=-1, keepdims=True) + EPSILON)


def rms_back(grad_scaled, scaled, inverse):
    return inverse * (grad_scaled - scaled * jnp.mean(grad_scaled * scaled, axis=-1, keepdims=True))


def exchange(pieces):
    return lax.all_to_all(pieces, SEQ, split_axis=0, concat_axis=0, tiled=True)


def local(
    tokens,
    cotangent,
    segments,
    joint_projection_matrix,
    output_weight_rows,
    gate_up_weight,
    down_weight_rows,
    attn_gain,
    ffn_gain,
):
    n = lax.axis_size(SEQ)
    me = lax.axis_index(SEQ)
    seqs, rows, width = tokens.shape
    full_len = segments.shape[1]
    heads = H // n
    qw = heads * HD
    sub = joint_projection_matrix.shape[0]
    part = FF // 4
    nx, nfar, ny = (lax.axis_size(axis) for axis in ("x", "far", "y"))
    flow = Flow()

    column = jnp.arange(full_len, dtype=jnp.int32)
    starts_here = jnp.concatenate(
        [jnp.ones((seqs, 1), dtype=bool), segments[:, 1:] != segments[:, :-1]], axis=1
    )
    doc_start = lax.cummax(jnp.where(starts_here, column, 0), axis=1)
    position = lax.dynamic_slice_in_dim(column - doc_start, me * rows, rows, 1)
    doc_start = doc_start.reshape(seqs, n, rows)
    first_block = doc_start[:, :, 0] // rows
    plain_from = jnp.minimum((doc_start[:, :, -1] + rows - 1) // rows, jnp.arange(n))
    plain_from = jnp.maximum(plain_from, first_block)
    doc_start = doc_start[:, :, None, :]
    frequency = ROTARY_BASE ** (-(jnp.arange(HD // 2, dtype=f32) * 2.0) / HD)
    angles = position.astype(f32).reshape(seqs * rows, 1) * frequency
    cosine = jnp.concatenate([jnp.cos(angles)] * 4, axis=1)
    sine = jnp.concatenate([-jnp.sin(angles), jnp.sin(angles)] * 2, axis=1)

    hidden_all = tokens.reshape(seqs * rows, width).astype(f32)
    grad_out_all = cotangent.reshape(seqs * rows, width)
    gain_one = attn_gain.astype(f32)
    gain_two = ffn_gain.astype(f32)

    def own_rows(weight):
        gathered = lax.all_gather(weight, ("x",) + SEQ, axis=0, tiled=True)
        return gathered.reshape(nx, -1, weight.shape[1])

    def core_features(values):
        w = width // (2 * nx)
        bit = my_bit(CORE)
        return tuple(
            jnp.concatenate(
                [lax.dynamic_slice_in_dim(values, (2 * i + c) * w, w, 1) for i in range(nx)], axis=1
            )
            for c in (bit, 1 - bit)
        )

    def flat(values):
        return values.reshape(-1, values.shape[-1])

    def lane_halves(values, key):
        w = values.shape[-1] // 2
        bit = my_bit(key)
        return (
            lax.dynamic_slice_in_dim(values, bit * w, w, values.ndim - 1),
            lax.dynamic_slice_in_dim(values, (1 - bit) * w, w, values.ndim - 1),
        )

    def lanes_by_bit(mine, other, key):
        low = my_bit(key) == 0
        return [jnp.where(low, mine, other), jnp.where(low, other, mine)]

    class Group:
        def __init__(self, values):
            self.values, self.core = values, swap(values, CORE)
            self.arrived = swap(values, NEAR)

        def done(self):
            near = self.arrived
            return jnp.concatenate([self.values, self.core, near, swap(near, CORE)], axis=0)

    class GroupSum:
        def __init__(self, partial):
            self.mine = partial.reshape(2, 2, rows, -1)
            self.arrived = swap(self.mine[:, 1], CORE)

        def next(self):
            both = self.mine[:, 0].astype(f32) + self.arrived.astype(f32)
            self.mine = both[0]
            self.arrived = swap(both[1].astype(bf16), NEAR)

        def done(self):
            return self.mine + self.arrived.astype(f32)

    qkv = Gather(joint_projection_matrix, "near", 0)
    out = Gather(output_weight_rows, "far", 0)
    flow.close(flow.token, wait=[qkv])

    qkv = Gather(qkv.done(), "far", 0)
    near_parts, near_swaps = [], []
    for weight in (gate_up_weight[:, :FF], gate_up_weight[:, FF:], down_weight_rows):
        mine, other = lane_halves(weight, NEAR)
        near_parts.append(mine)
        near_swaps.append(other)
    near_swap = Swap(flow.open(jnp.stack(near_swaps)), NEAR)
    inverse_one = rms_scale(hidden_all)
    scaled_one = hidden_all * inverse_one
    normed_one = (scaled_one * gain_one).astype(bf16)
    normed_one_own, normed_one_other = core_features(normed_one)
    normed_one_own, normed_one_other, cosine, sine = flow.close(
        normed_one_own, normed_one_other, cosine, sine, wait=[qkv, near_swap, out]
    )

    left, right = jnp.split(qkv.done(), 2, axis=-1)
    left = Gather(left, "y", 2)
    right = Gather(right, "x", 0)
    core_parts, core_swaps = [], []
    for mine, arrived in zip(near_parts, near_swap.arrived):
        mine, other = lane_halves(by_bit(mine, arrived, NEAR, 0), CORE)
        core_parts.append(mine)
        core_swaps.append(other)
    core_swap = Swap(jnp.stack(core_swaps), CORE)
    out = Gather(out.done(), "near", 1)
    flow.close(flow.token, wait=[left, right, core_swap, out])

    def over_xy(values):
        gathered = lax.all_gather(flat(values), ("x", "y"), axis=0, tiled=True)
        return gathered.reshape((nx * ny,) + values.shape)

    left = Gather(left.done(), "x", 0)
    right = Gather(right.done(), "y", 3)
    gate, up, down = (
        by_bit(mine, arrived, CORE, 0) for mine, arrived in zip(core_parts, core_swap.arrived)
    )
    gate = Gather(gate, "far", 1)
    w_out_own = over_xy(out.done())
    grad_group_0 = Group(flow.open(grad_out_all[:rows]))
    up, down = flow.close(up, down, wait=[left, right, gate, grad_group_0])

    w_own = jnp.concatenate([flat(left.done()), flat(right.done())], axis=1)
    w_swap = Swap(w_own, CORE)
    up = Gather(up, "far", 1)
    projected = dot(normed_one_own, w_own)
    w_other = w_swap.arrived
    projected = projected + dot(normed_one_other, w_other)
    packed_0 = pack_heads(projected, cosine, sine, 0, rows, n)
    packed_0 = flow.close(packed_0, wait=[up])

    def attend_one(b, qkv_b):
        return attend(first_block[b], plain_from[b], doc_start[b], qkv_b, heads)

    packed_0, projected, w_other = flow.open(packed_0, projected, w_other)
    qkv_0 = exchange(packed_0)
    w_gate_up = over_xy(jnp.concatenate([gate.done(), up.done()], axis=-1))
    packed_1 = pack_heads(projected, cosine, sine, 1, rows, n)
    core_arg = lax.axis_index("core").astype(jnp.int32).reshape(1)
    w_shape = (nx, 1, nfar * 2, -1, w_own.shape[1])
    w_qkv = flat(interleave(core_arg, w_own.reshape(w_shape), w_other.reshape(w_shape)))
    qkv_0, packed_1, w_qkv, w_out_own = flow.close(qkv_0, packed_1, w_qkv, w_out_own)

    qkv_0, packed_1 = flow.open(qkv_0, packed_1)
    qkv_1 = exchange(packed_1)
    out_swap = Swap(flow.open(w_out_own), CORE)
    attended_0, raw_0, lse_0 = attend_one(0, qkv_0)
    attended_0, qkv_1 = flow.close(attended_0, qkv_1, wait=[out_swap])

    attended_0, qkv_1 = flow.open(attended_0, qkv_1)
    back_0 = exchange(attended_0)
    w_shape = (nx, ny, nfar * 2, sub, width)
    w_out = interleave(core_arg, w_out_own.reshape(w_shape), out_swap.arrived.reshape(w_shape))
    down = Gather(flow.open(down), "far", 1)
    attended_1, raw_1, lse_1 = attend_one(1, qkv_1)
    attended_1, back_0, w_out = flow.close(attended_1, back_0, flat(w_out), wait=[down])

    def after_attention(b, back):
        attended = jnp.concatenate([back[s] for s in range(n)], axis=1)
        hidden = flow.open(tokens[b]).astype(f32)
        middle = hidden + rows_by(attended, w_out)
        inverse = rms_scale(middle)
        scaled = middle * inverse
        return attended, middle, inverse, scaled, (scaled * gain_two).astype(bf16)

    attended_1, back_0, w_out = flow.open(attended_1, back_0, w_out)
    back_1 = exchange(attended_1)
    attended_0, middle_0, inverse_0, scaled_0, normed_0 = after_attention(0, back_0)
    normed_0 = flow.close(normed_0)

    group_0 = Group(normed_0)
    back_1 = flow.close(back_1)
    attended_1, middle_1, inverse_1, scaled_1, normed_1 = after_attention(1, back_1)
    normed_1, w_gate_up = flow.close(normed_1, w_gate_up, wait=[group_0])
    down.arrived = flow.open(down.arrived)
    w_down = over_xy(down.done())
    group_1 = Group(normed_1)
    group_0 = group_0.done()

    gate_0, up_0, active_0 = ffn_forward(group_0, w_gate_up)
    active_0 = flow.close(active_0, wait=[group_1])
    grad_group_0.arrived = flow.open(grad_group_0.arrived)
    grad_group_0 = grad_group_0.done()
    grad_group_1 = Group(flow.open(grad_out_all[rows:]))

    group_1 = group_1.done()
    gate_1, up_1, active_1 = ffn_forward(flow.open(group_1), w_gate_up)
    active_1 = flow.close(active_1, wait=[grad_group_1])
    grad_group_1 = grad_group_1.done()

    outer = lambda a, b: dot(a, b, ((0,), (0,)))
    owners = (nx, nfar, ny)

    def sum_to_owners(terms):
        rest = terms.shape[2:]
        terms = terms.reshape(-1, terms.shape[-1])
        total = lax.psum_scatter(terms, ("x", "y"), scatter_dimension=0, tiled=True)
        return total.reshape(rest)

    d_down = outer_sum(
        [(grad_group_0, active_0), (grad_group_1, flow.open(active_1))], part, 0, owners
    )
    d_down = flow.close(d_down)

    d_down = sum_to_owners(flow.open(d_down))
    both_0 = ffn_backward(flow.open(grad_group_0), w_down, gate_0, up_0)
    terms_0 = flow.close(project_rows(both_0, w_gate_up))

    grad_normed_0 = GroupSum(terms_0)
    partial_0 = project_rows(flow.open(active_0), w_down)
    partial_0 = flow.close(partial_0, wait=[grad_normed_0])
    grad_normed_0.next()
    result_0 = GroupSum(partial_0)
    both_1 = ffn_backward(flow.open(grad_group_1), w_down, gate_1, up_1)
    terms_1 = project_rows(both_1, w_gate_up)
    terms_1 = flow.close(terms_1, wait=[grad_normed_0, result_0])

    def before_attention(b, g, scaled, inverse):
        grad_middle = grad_out_all[b * rows : (b + 1) * rows].astype(f32) + rms_back(
            g * gain_two, scaled, inverse
        )
        grad_branch = grad_middle.astype(bf16)
        grad_attended = dot(grad_branch, w_out).astype(bf16)
        grad_heads = [grad_attended[:, d * qw : (d + 1) * qw] for d in range(n)]
        return grad_middle, grad_branch, jnp.stack(grad_heads)

    grad_normed_1 = GroupSum(terms_1)
    grad_normed_0 = grad_normed_0.done()
    grad_middle_0, grad_branch_0, grad_heads_0 = before_attention(
        0, grad_normed_0, scaled_0, inverse_0
    )
    grad_heads_0 = flow.close(grad_heads_0, wait=[grad_normed_1])

    grad_normed_1.next()
    grad_heads_0 = exchange(grad_heads_0)
    d_up = outer_sum([(flow.open(group_0), both_0), (group_1, both_1)], part, 1, owners)
    d_up = flow.close(d_up, wait=[grad_normed_1])

    d_up = sum_to_owners(flow.open(d_up))
    d_gate = outer_sum([(flow.open(group_0), both_0), (group_1, both_1)], part, 0, owners)
    d_gate, grad_heads_0 = flow.close(d_gate, grad_heads_0)

    d_gate = sum_to_owners(flow.open(d_gate))
    grad_normed_1 = grad_normed_1.done()
    grad_middle_1, grad_branch_1, grad_heads_1 = before_attention(
        1, grad_normed_1, scaled_1, inverse_1
    )
    grad_heads_1 = flow.close(grad_heads_1)

    grad_heads_1 = exchange(grad_heads_1)
    grad_branch = jnp.concatenate([grad_branch_0, grad_branch_1], axis=0)
    attended = jnp.concatenate([attended_0, attended_1], axis=0)
    d_out = outer(flow.open(grad_branch), attended).astype(bf16)
    d_out = flow.close(d_out.reshape((nx, 2, -1, attended.shape[1])))

    def core_sum(mine, send):
        total = mine.astype(f32) + swap(send.astype(bf16), CORE).astype(f32)
        total = total.astype(bf16).reshape((nx, nfar, 2, ny, sub, total.shape[-1]))
        return total.transpose((0, 3, 1, 2, 4, 5))

    def attend_back_one(b, qkv_b, grad_b, raw_b, lse_b):
        dq, dkv = attend_back(
            first_block[b], plain_from[b], doc_start[b], qkv_b, grad_b, raw_b, lse_b, heads
        )
        return jnp.concatenate([dq, dkv], axis=2)

    d_out = sum_to_owners(core_sum(*choose(d_out, CORE, 1)))
    back_0 = attend_back_one(0, qkv_0, flow.open(grad_heads_0), raw_0, lse_0)
    d_down = Scatter(flow.open(d_down), "far", 1)
    result_0.next()
    back_0, grad_heads_1 = flow.close(back_0, grad_heads_1, wait=[d_down, result_0])

    back_0 = exchange(back_0)
    back_1 = attend_back_one(1, qkv_1, flow.open(grad_heads_1), raw_1, lse_1)
    back_1, back_0 = flow.close(back_1, back_0)

    back_1 = exchange(back_1)
    partial_1 = project_rows(flow.open(active_1), w_down)
    grad_proj_0 = unpack_heads(flow.open(back_0), cosine[:rows], sine[:rows])
    d_up = Scatter(flow.open(d_up), "far", 1)
    back_1, grad_proj_0, partial_1 = flow.close(back_1, grad_proj_0, partial_1, wait=[d_up])

    d_gate = Scatter(flow.open(d_gate), "far", 1)
    result_1 = GroupSum(partial_1)
    grad_proj_1 = unpack_heads(back_1, cosine[rows:], sine[rows:])
    grad_proj = jnp.concatenate([grad_proj_0, grad_proj_1], axis=0)
    core_back = outer_rows(
        [(normed_one_other[:rows], grad_proj_0), (normed_one_other[rows:], grad_proj_1)]
    )
    core_back = Swap(core_back, CORE)
    grad_normed_one = rows_by(grad_proj, w_qkv)
    grad_proj, grad_normed_one = flow.close(
        grad_proj, grad_normed_one, wait=[core_back, result_1, d_gate]
    )
    d_qkv = outer(normed_one_own, grad_proj) + core_back.arrived.astype(f32)
    d_qkv = d_qkv.astype(bf16).reshape((nx, nfar, 2, ny, sub, -1))
    left, right = flow.close(*jnp.split(d_qkv, 2, axis=-1))

    left = Scatter(left, "x", 0)
    right = Scatter(right, "y", 3)
    result_1.next()
    d_out = Scatter(flow.open(d_out), "far", 0)
    ffn = jnp.stack([t.done(last=True) for t in (d_gate, d_up, d_down)])
    mine, send = choose(ffn, NEAR, 2)
    near_back = Swap(send.astype(bf16), NEAR)
    flow.close(flow.token, wait=[left, right])

    left = Scatter(left.done(), "y", 2)
    right = Scatter(right.done(), "x", 0)
    attn_gain_grad = jnp.sum(grad_normed_one * scaled_one, axis=0)
    late_0, late_1 = flow.open(grad_normed_0, grad_normed_1)
    ffn_gain_grad = jnp.sum(late_0 * scaled_0, axis=0) + jnp.sum(late_1 * scaled_1, axis=0)
    gains = jnp.stack([attn_gain_grad, ffn_gain_grad])
    gains, grad_normed_one = flow.close(gains, grad_normed_one, wait=[left, right, near_back])

    d_qkv = Scatter(jnp.concatenate([left.done(), right.done()], axis=-1), "far", 0)
    gains = sum_axes(gains, "x", "y", "core")
    quarters = []
    for part_of in lanes_by_bit(mine, near_back.arrived.astype(f32), NEAR):
        part_mine, part_send = choose(part_of, CORE, 1)
        quarters += lanes_by_bit(part_mine, swap(part_send.astype(bf16), CORE).astype(f32), CORE)
    d_gate_up = jnp.concatenate([q[k] for k in (0, 1) for q in quarters], axis=1)
    d_down = jnp.concatenate([q[2] for q in quarters], axis=1)
    grad_input = jnp.concatenate([grad_middle_0, grad_middle_1], axis=0) + rms_back(
        grad_normed_one * gain_one, scaled_one, inverse_one
    )
    grad_input, gains, d_gate_up, d_down = flow.close(
        grad_input, gains, d_gate_up, d_down, wait=[d_qkv, d_out, result_1]
    )

    d_qkv = Scatter(d_qkv.done(), "near", 0)
    d_out = Scatter(d_out.done(), "near", 0)
    gains = sum_axes(gains, "near", "far")
    result = jnp.concatenate([middle_0 + result_0.done(), middle_1 + result_1.done()], axis=0)
    return (
        result.astype(bf16).reshape(tokens.shape),
        grad_input.reshape(tokens.shape),
        d_qkv.done(last=True),
        d_out.done(last=True),
        d_gate_up,
        d_down,
        gains[0],
        gains[1],
    )


def solution(mesh):
    dp, seq = mesh.devices.shape
    shape = (dp // 2, 2, seq // 4, 2, 2)
    fine = Mesh(mesh.devices.reshape(shape), ("x", "core") + SEQ)
    by_token = P(("x", "core"), SEQ, None)
    by_row = P(("x", "core") + SEQ, None)
    return jax.shard_map(
        local,
        mesh=fine,
        in_specs=(
            by_token,
            by_token,
            P(("x", "core"), None),
            by_row,
            by_row,
            by_row,
            by_row,
            P(),
            P(),
        ),
        out_specs=(by_token, by_token, by_row, by_row, by_row, by_row, P(), P()),
        check_vma=False,
    )
```
